128 devices in a mesh: pipe: 4 (over z_lo, core), dp: 32 (over x, z_hi, y).
Axes of the slice: x: 4, y: 4, z: 4 (z_hi: 2, z_lo: 2; z = z_hi * 2 + z_lo), core: 2. Of those that a mesh axis runs over, the one named last changes fastest.
Arguments:
- segment_data: bfloat16 [4, 32, 2, 512, 384], P('pipe', 'dp'), may hold values from -6 to 6
- clip_frames: int32 [32, 2, 2, 8], P('dp'), may hold values from 0 to 32, as said below
- encoder_gains: bfloat16 [2, 384], replicated, may hold values from 0.25 to 1.75
- encoder_biases: bfloat16 [6, 384], replicated, may hold values from -3 to 3
- encoder_project: bfloat16 [384, 1152], replicated, may hold values from -0.3125 to 0.3125
- encoder_merge: bfloat16 [384, 384], replicated, may hold values from -1.25 to 1.25
- encoder_expand: bfloat16 [384, 1536], replicated, may hold values from -0.3125 to 0.3125
- encoder_expand_bias: bfloat16 [1536], replicated, may hold values from -3 to 3
- encoder_reduce: bfloat16 [1536, 384], replicated, may hold values from -0.15625 to 0.15625
- predictor_embed: bfloat16 [384, 384], replicated, may hold values from -0.3125 to 0.3125
- predictor_embed_bias: bfloat16 [384], replicated, may hold values from -3 to 3
- predictor_gains: bfloat16 [2, 384], replicated, may hold values from 0.25 to 1.75
- predictor_biases: bfloat16 [6, 384], replicated, may hold values from -3 to 3
- predictor_project: bfloat16 [384, 1152], replicated, may hold values from -0.3125 to 0.3125
- predictor_merge: bfloat16 [384, 384], replicated, may hold values from -1.25 to 1.25
- predictor_expand: bfloat16 [384, 1536], replicated, may hold values from -0.3125 to 0.3125
- predictor_expand_bias: bfloat16 [1536], replicated, may hold values from -3 to 3
- predictor_reduce: bfloat16 [1536, 384], replicated, may hold values from -0.15625 to 0.15625
Outputs:
- segment_result: float32 [4, 32, 2, 512, 384], P('pipe', 'dp')
- grad_encoder_gains: float32 [2, 384], replicated
- grad_encoder_biases: float32 [6, 384], replicated
- grad_encoder_project: float32 [384, 1152], replicated
- grad_encoder_merge: float32 [384, 384], replicated
- grad_encoder_expand: float32 [384, 1536], replicated
- grad_encoder_expand_bias: float32 [1536], replicated
- grad_encoder_reduce: float32 [1536, 384], replicated
- grad_predictor_embed: float32 [384, 384], replicated
- grad_predictor_embed_bias: float32 [384], replicated
- grad_predictor_gains: float32 [2, 384], replicated
- grad_predictor_biases: float32 [6, 384], replicated
- grad_predictor_project: float32 [384, 1152], replicated
- grad_predictor_merge: float32 [384, 384], replicated
- grad_predictor_expand: float32 [384, 1536], replicated
- grad_predictor_expand_bias: float32 [1536], replicated
- grad_predictor_reduce: float32 [1536, 384], replicated
The draws below stay inside these ranges and needn't reach their ends.
Inputs may be any that keep to these rules, and one draw needn't show every extreme that they name: `clip_frames`: in each slot the nonzero counts (8, 16 or 32) come first and zeros after; every slot holds at least one clip; a slot's counts sum to at most 64, and some slot reaches that sum in every draw.
All inputs are finite; a program needn't handle non-finite values.
Results may differ from the reference program's by a relative error of at most 0.025.
Values may be sent and summed in bfloat16 or wider, within the bound.
A program may use at most 256 MiB of HBM per device.

```python
import math
import jax
import jax.numpy as jnp
from jax import lax

HEADS = 6
D = 384
FF = 1536
PHEADS = 12
PD = 384
PFF = 1536
PATCH = 16
SLOT_T = 32
MICRO = 2
CLIPS = 8
CAP = 512
N_PIPE = 4
N_DP = 32


def draw_clip_frames(key, part):
    key = jax.random.fold_in(key, 7)
    length_key, kept_key, full_key = jax.random.split(key, 3)
    slot_count = N_DP * MICRO * 2
    unit_count = SLOT_T // 4
    length_code = jax.random.randint(length_key, (slot_count, CLIPS), 0, 3)
    lengths = jnp.where(length_code == 0, 1, jnp.where(length_code == 1, 2, 4)).astype(jnp.int32)
    kept_count = jax.random.randint(kept_key, (slot_count, 1), 1, CLIPS + 1)
    clip_ends = jnp.cumsum(lengths, axis=1)
    clip_order = jnp.arange(CLIPS, dtype=jnp.int32)[None, :]
    fitting = (clip_ends <= unit_count) & (clip_order < kept_count)
    frames = jnp.where(fitting, lengths * 8, 0)
    full_slot = jax.random.randint(full_key, (), 0, slot_count)
    pattern = jnp.where(clip_order < 2, 32, 0)
    slot_order = jnp.arange(slot_count, dtype=jnp.int32)[:, None]
    frames = jnp.where(slot_order == full_slot, pattern, frames)
    return frames.reshape(N_DP, MICRO, 2, CLIPS).astype(jnp.int32)


def steps_of(rng, extent, pieces, smallest, high):
    loudness = 1.0
    for dim, blocks in pieces:
        draws = jax.random.uniform(jax.random.fold_in(jax.random.fold_in(rng, 6), dim), (blocks,), jnp.float32, smallest / len(pieces), high / len(pieces))
        loudness = loudness * jnp.repeat(jnp.exp(draws), extent[dim] // blocks).reshape((-1,) + (1,) * (len(extent) - 1 - dim))
    return loudness


def gaussian(stream_key, extent, width, bound, pieces=(), held_as=jnp.bfloat16):
    values = jax.random.normal(stream_key, extent, jnp.float32) * width
    if len(pieces) > 0:
        values = steps_of(stream_key, extent, pieces, -0.22, 0.18) * values
    return jnp.clip(values, min=-bound, max=bound).astype(held_as)


def setup_inputs(seed: int = 0) -> dict:
    seeds = jax.random.split(jax.random.key(seed), 19)
    return {
        "segment_data": gaussian(seeds[0], (N_PIPE, N_DP, MICRO, CAP, D), 1.0, 6.0, ((0, 4), (1, 32))),
        "clip_frames": draw_clip_frames(jax.random.fold_in(seeds[18], 71), 0),
        "encoder_gains": jnp.clip(1.0 + 0.15 * jax.random.normal(seeds[2], (2, D), jnp.float32), 0.25, 1.75).astype(jnp.bfloat16),
        "encoder_biases": gaussian(seeds[3], (6, D), 0.3, 3.0),
        "encoder_project": gaussian(seeds[4], (D, 3 * D), D ** -0.5, 0.3125),
        "encoder_merge": gaussian(seeds[5], (D, D), (D // 16) ** -0.5, 1.25),
        "encoder_expand": gaussian(seeds[6], (D, FF), D ** -0.5, 0.3125),
        "encoder_expand_bias": gaussian(seeds[7], (FF,), 0.3, 3.0),
        "encoder_reduce": gaussian(seeds[8], (FF, D), FF ** -0.5, 0.15625),
        "predictor_embed": gaussian(seeds[9], (D, PD), D ** -0.5, 0.3125),
        "predictor_embed_bias": gaussian(seeds[10], (PD,), 0.3, 3.0),
        "predictor_gains": jnp.clip(1.0 + 0.15 * jax.random.normal(seeds[11], (2, PD), jnp.float32), 0.25, 1.75).astype(jnp.bfloat16),
        "predictor_biases": gaussian(seeds[12], (6, PD), 0.3, 3.0),
        "predictor_project": gaussian(seeds[13], (PD, 3 * PD), PD ** -0.5, 0.3125),
        "predictor_merge": gaussian(seeds[14], (PD, PD), (PD // 16) ** -0.5, 1.25),
        "predictor_expand": gaussian(seeds[15], (PD, PFF), PD ** -0.5, 0.3125),
        "predictor_expand_bias": gaussian(seeds[16], (PFF,), 0.3, 3.0),
        "predictor_reduce": gaussian(seeds[17], (PFF, PD), PFF ** -0.5, 0.15625),
    }


epsilon = 1e-06
masked_score = -1e+30

@jax.custom_vjp
def low(v):
    return lax.optimization_barrier(v.astype(jnp.bfloat16)).astype(jnp.float32)

@jax.custom_vjp
def low_back(v):
    return v

def low_keep(v):
    return (low(v), None)

def low_pass(kept, grad):
    return (grad,)

def back_keep(v):
    return (v, None)

def back_low(kept, grad):
    return (low(grad),)
low.defvjp(low_keep, low_pass)
low_back.defvjp(back_keep, back_low)

def layout(frames):
    clip_ends = jnp.cumsum(frames // 2).astype(jnp.int32)
    tubelet = jnp.arange(CAP, dtype=jnp.int32) // PATCH
    clip_number = lax.optimization_barrier(jnp.sum((tubelet[:, None] >= clip_ends[None, :]).astype(jnp.int32), axis=1)).astype(jnp.int32)
    live_rows = tubelet < clip_ends[CLIPS - 1]
    clip_labels = jnp.where(live_rows, clip_number, CLIPS + tubelet).astype(jnp.int32)
    return (clip_labels, live_rows.astype(jnp.float32))

def product(first_operand, second_operand):
    return jnp.dot(first_operand, second_operand, precision=lax.Precision.HIGHEST)

def layer_norm(stream, gain_row, shift_row):
    average = lax.optimization_barrier(jnp.mean(stream, axis=-1, keepdims=True))
    centred = stream - average
    inverse = lax.rsqrt(lax.optimization_barrier(jnp.mean(centred * centred, axis=-1, keepdims=True)) + epsilon)
    return centred * inverse * gain_row + shift_row

def residual_block(stream, gains, biases, project_weight, merge_weight, expand_weight, expand_bias, reduce_weight, clip_labels, head_count):
    features = stream.shape[-1]
    head_size = features // head_count
    normed = low(layer_norm(stream, gains[0], biases[0]))
    packed_bias = jnp.concatenate([biases[1], jnp.zeros_like(biases[1]), biases[2]])
    packed = low(low_back(product(normed, project_weight) + packed_bias))
    queries = packed[:, :features].reshape(-1, head_count, head_size)
    key_rows = packed[:, features:2 * features].reshape(-1, head_count, head_size)
    values = packed[:, 2 * features:].reshape(-1, head_count, head_size)
    scores = jnp.einsum('qhd,khd->hqk', queries, key_rows, precision=lax.Precision.HIGHEST) * (1.0 / math.sqrt(head_size))
    scores = low_back(scores)
    same_clip = clip_labels[:, None] == clip_labels[None, :]
    scores = jnp.where(same_clip[None], scores, masked_score)
    largest = lax.optimization_barrier(jnp.max(scores, axis=-1, keepdims=True))
    exponent = jnp.exp(scores - largest)
    probability = low(exponent / lax.optimization_barrier(jnp.sum(exponent, axis=-1, keepdims=True)))
    attended = jnp.einsum('hqk,khd->qhd', probability, values, precision=lax.Precision.HIGHEST).reshape(-1, features)
    attended = low(low_back(attended))
    middle = stream + low_back(product(attended, merge_weight) + biases[3])
    second = low(layer_norm(middle, gains[1], biases[4]))
    pre_act = low_back(product(second, expand_weight) + expand_bias)
    activated = low(jax.nn.gelu(pre_act, approximate=False))
    return middle + low_back(product(activated, reduce_weight) + biases[5])

def slot_output(params, stream_in, frames):
    encoder, predictor = params
    clip_labels, live_rows = layout(frames)
    hidden = residual_block(stream_in, *encoder, clip_labels, HEADS)
    outgoing = low(low_back(hidden))
    embedded = low_back(product(outgoing, predictor[0]) + predictor[1])
    predicted = residual_block(embedded, *predictor[2:], clip_labels, PHEADS)
    return predicted * live_rows[:, None]

def to_slots(block_data):
    return jnp.transpose(block_data, (1, 2, 0, 3, 4)).reshape(-1, CAP, D).astype(jnp.float32)

def from_slots(slot_rows):
    return jnp.transpose(slot_rows.reshape(N_DP, MICRO, 2, CAP, D), (2, 0, 1, 3, 4))

def reference(segment_data, clip_frames, encoder_gains, encoder_biases, encoder_project, encoder_merge, encoder_expand, encoder_expand_bias, encoder_reduce, predictor_embed, predictor_embed_bias, predictor_gains, predictor_biases, predictor_project, predictor_merge, predictor_expand, predictor_expand_bias, predictor_reduce):
    encoder = tuple((weight.astype(jnp.float32) for weight in (encoder_gains, encoder_biases, encoder_project, encoder_merge, encoder_expand, encoder_expand_bias, encoder_reduce)))
    predictor = tuple((weight.astype(jnp.float32) for weight in (predictor_embed, predictor_embed_bias, predictor_gains, predictor_biases, predictor_project, predictor_merge, predictor_expand, predictor_expand_bias, predictor_reduce)))
    inputs = to_slots(segment_data[:2])
    cotangent = to_slots(segment_data[2:])
    frame_rows = clip_frames.reshape(-1, CLIPS)
    checked = jax.checkpoint(slot_output)

    def forward(params, streams):

        def advance(carried, slot_item):
            return (carried, checked(params, slot_item[0], slot_item[1]))
        carry_out, outputs = lax.scan(advance, jnp.zeros((), jnp.float32), (streams, frame_rows))
        return outputs
    outputs, pullback = jax.vjp(forward, (encoder, predictor), inputs)
    gradients, input_grad = pullback(cotangent)
    encoder_grads, predictor_grads = gradients
    segment_result = jnp.concatenate([from_slots(input_grad), from_slots(outputs)], axis=0)
    return (segment_result, encoder_grads[0], encoder_grads[1], encoder_grads[2], encoder_grads[3], encoder_grads[4], encoder_grads[5], encoder_grads[6], predictor_grads[0], predictor_grads[1], predictor_grads[2], predictor_grads[3], predictor_grads[4], predictor_grads[5], predictor_grads[6], predictor_grads[7], predictor_grads[8])
```

```python
import functools
import math

import jax
import jax.numpy as jnp
from jax import lax
from jax.experimental import pallas as pl
from jax.experimental.pallas import tpu as pltpu
from jax.sharding import PartitionSpec as P

HEADS = 6
PHEADS = 12
CLIPS = 8
F = 384
FF = 1536
ROWS = 512
UNIT = 64
UNITS = ROWS // UNIT
BLOCK = 256
BLOCKS = ROWS // BLOCK
PART = 5120
EPS = 1e-06
MASKED = -1e30

f32 = jnp.float32
bf16 = jnp.bfloat16


def dot(a, b, ca, cb):
    return lax.dot_general(a, b, (((ca,), (cb,)), ((), ())), preferred_element_type=f32)


def unit_order(frames):
    units = [frames[c] // 8 for c in range(CLIPS)]
    start, place = [], []
    total = jnp.int32(0)
    for c in range(CLIPS):
        start.append(total)
        total = total + units[c]
    for c in range(CLIPS):
        before = jnp.int32(0)
        for d in range(CLIPS):
            if d < c:
                ahead = units[d] >= units[c]
            elif d > c:
                ahead = units[d] > units[c]
            else:
                continue
            before = before + jnp.where(ahead, units[d], 0)
        place.append(before)
    source, target, label = [], [], []
    for j in range(UNITS):
        src, dst, lab = jnp.int32(j), jnp.int32(j), jnp.int32(CLIPS + j)
        for c in range(CLIPS):
            held = (j >= place[c]) & (j < place[c] + units[c])
            src = jnp.where(held, start[c] + j - place[c], src)
            lab = jnp.where(held, c, lab)
            owns = (j >= start[c]) & (j < start[c] + units[c])
            dst = jnp.where(owns, place[c] + j - start[c], dst)
        source.append(src)
        target.append(dst)
        label.append(lab)
    return source, target, label, total


def spread(values, shape, axis):
    at = lax.broadcasted_iota(jnp.int32, shape, axis) // UNIT
    out = jnp.full(shape, values[0], jnp.int32)
    for i in range(1, len(values)):
        out = jnp.where(at == i, values[i], out)
    return out


def fill_mask(mask_ref, label):
    for b in range(BLOCKS):
        own = label[b * 4 : b * 4 + 4]
        down = spread(own, (BLOCK, BLOCK), 0)
        across = spread(own, (BLOCK, BLOCK), 1)
        mask_ref[b] = jnp.where(down == across, 0.0, MASKED).astype(f32)


def norm(v, gain, shift):
    mean = jnp.mean(v, axis=0, keepdims=True)
    centred = v - mean
    inverse = lax.rsqrt(jnp.mean(centred * centred, axis=0, keepdims=True) + EPS)
    normed = centred * inverse
    return normed * gain + shift, normed, inverse


def norm_back(k, normed, inverse):
    return inverse * (
        k
        - jnp.mean(k, axis=0, keepdims=True)
        - normed * jnp.mean(k * normed, axis=0, keepdims=True)
    )


def block_forward(stream_ref, out_ref, w, s, heads, mask_ref):
    size = F // heads
    scale = math.log2(math.e) / math.sqrt(size)
    vec = w.vec
    for t in range(ROWS // 128):
        cols = slice(t * 128, t * 128 + 128)
        full, normed, inverse = norm(stream_ref[:, cols], vec[:, 0:1], vec[:, 2:3])
        s.n1[:, cols] = normed
        s.i1[:, cols] = inverse
        s.a1[:, cols] = full.astype(bf16)
    for part in range(3):
        rows = slice(part * F, part * F + F)
        z = dot(w.project[:, rows], s.a1[...], 0, 0)
        if part == 0:
            z = z + vec[:, 3:4]
        if part == 2:
            z = z + vec[:, 4:5]
        s.z[rows, :] = z.astype(bf16)
    for b in range(BLOCKS):
        cols = slice(b * BLOCK, b * BLOCK + BLOCK)
        for h in range(heads):
            own = slice(h * size, h * size + size)
            q = s.z[h * size : h * size + size, cols]
            k = s.z[F + h * size : F + h * size + size, cols]
            v = s.z[2 * F + h * size : 2 * F + h * size + size, cols]
            score = dot(k, q, 0, 0) * scale + mask_ref[b]
            e = jnp.exp2(score - jnp.max(score, axis=0, keepdims=True))
            over = 1.0 / jnp.sum(e, axis=0, keepdims=True)
            e = e.astype(bf16)
            s.e[h, b] = e
            s.over[h : h + 1, cols] = over
            s.o[own, cols] = (dot(v, e, 1, 0) * over).astype(bf16)
    middle = stream_ref[...] + (dot(w.merge[...], s.o[...], 0, 0) + vec[:, 5:6])
    s.m1[...] = middle
    for t in range(ROWS // 128):
        cols = slice(t * 128, t * 128 + 128)
        full, normed, inverse = norm(s.m1[:, cols], vec[:, 1:2], vec[:, 6:7])
        s.n2[:, cols] = normed
        s.i2[:, cols] = inverse
        s.a2[:, cols] = full.astype(bf16)
    for part in range(4):
        rows = slice(part * F, part * F + F)
        u = dot(w.expand[:, rows], s.a2[...], 0, 0) + vec[:, 8 + part : 9 + part]
        below = 0.5 * lax.erf(u * math.sqrt(0.5)) + 0.5
        density = jnp.exp2(u * u * (-0.5 * math.log2(math.e))) * (1.0 / math.sqrt(2.0 * math.pi))
        s.act[rows, :] = (u * below).astype(bf16)
        s.slope[rows, :] = (below + u * density).astype(bf16)
    out_ref[...] = s.m1[...] + (dot(w.reduce[...], s.act[...], 0, 0) + vec[:, 7:8])


def place(grad_ref, at, value):
    for c in range(3):
        grad_ref[c, at : at + value.shape[0], :] = value[:, c * 128 : c * 128 + 128].astype(bf16)


def total(x):
    return jnp.sum(x.astype(f32), axis=1, keepdims=True)


def block_backward(grad_ref, w, s, heads, g_ref, base):
    size = F // heads
    vec = w.vec
    sums = [None] * 12
    s.q[...] = grad_ref[...].astype(bf16)
    q2 = s.q[...]
    sums[7] = total(q2)
    for part in range(4):
        rows = slice(part * F, part * F + F)
        place(g_ref, base + 3072 + part * F, dot(s.act[rows, :], q2, 1, 1))
        du = (dot(w.reduce[rows, :], q2, 1, 0) * s.slope[rows, :].astype(f32)).astype(bf16)
        s.du[rows, :] = du
        sums[8 + part] = total(du)
        place(g_ref, base + 1536 + part * F, dot(s.a2[...], du, 1, 1))
    da = dot(w.expand[...], s.du[...], 1, 0)
    s.t[...] = da
    sums[1] = total(da * s.n2[...])
    sums[6] = total(da)
    for t in range(ROWS // 128):
        cols = slice(t * 128, t * 128 + 128)
        grad_ref[:, cols] += norm_back(s.t[:, cols] * vec[:, 1:2], s.n2[:, cols], s.i2[:, cols])
    s.q[...] = grad_ref[...].astype(bf16)
    q1 = s.q[...]
    sums[5] = total(q1)
    place(g_ref, base + 1152, dot(s.o[...], q1, 1, 1))
    s.t[...] = dot(w.merge[...], q1, 1, 0)
    for b in range(BLOCKS):
        cols = slice(b * BLOCK, b * BLOCK + BLOCK)
        for h in range(heads):
            lo = h * size
            own = slice(lo, lo + size)
            q = s.z[lo : lo + size, cols]
            k = s.z[F + lo : F + lo + size, cols]
            v = s.z[2 * F + lo : 2 * F + lo + size, cols]
            do = (s.t[own, cols] * s.over[h : h + 1, cols]).astype(bf16)
            delta = jnp.sum(do.astype(f32) * s.o[own, cols].astype(f32), axis=0, keepdims=True)
            e = s.e[h, b]
            dp = dot(v, do, 0, 0) - delta
            ds = dp.astype(bf16) * e
            s.dz[2 * F + lo : 2 * F + lo + size, cols] = dot(do, e, 1, 1).astype(bf16)
            s.dz[lo : lo + size, cols] = (dot(k, ds, 1, 0) * (1.0 / math.sqrt(size))).astype(bf16)
            s.dz[F + lo : F + lo + size, cols] = (dot(q, ds, 1, 1) * (1.0 / math.sqrt(size))).astype(bf16)
    sums[3] = total(s.dz[0:F, :])
    sums[4] = total(s.dz[2 * F : 3 * F, :])
    for part in range(3):
        rows = slice(part * F, part * F + F)
        place(g_ref, base + part * F, dot(s.a1[...], s.dz[rows, :], 1, 1))
    da = dot(w.project[...], s.dz[...], 1, 0)
    s.t[...] = da
    sums[0] = total(da * s.n1[...])
    sums[2] = total(da)
    for t in range(ROWS // 128):
        cols = slice(t * 128, t * 128 + 128)
        grad_ref[:, cols] += norm_back(s.t[:, cols] * vec[:, 0:1], s.n1[:, cols], s.i1[:, cols])
    return sums


def columns(gains, biases, hidden):
    rows = [gains.astype(f32), biases.astype(f32)]
    for part in range(4):
        rows.append(hidden[:, part * F : part * F + F].astype(f32))
    rows.append(jnp.zeros((4, F), f32))
    return jnp.concatenate(rows, axis=0).T


def place_sums(g_ref, at, sums):
    lane = lax.broadcasted_iota(jnp.int32, (F, 128), 1)
    table = jnp.zeros((F, 128), f32)
    for i, column in enumerate(sums):
        table = jnp.where(lane == i, column, table)
    place(g_ref, at, table.T[0:16, :])


class Refs:
    pass


KEPT = (
    ("n1", (F, ROWS), f32), ("i1", (1, ROWS), f32), ("a1", (F, ROWS), bf16), ("z", (3 * F, ROWS), bf16),
    ("o", (F, ROWS), bf16), ("m1", (F, ROWS), f32), ("n2", (F, ROWS), f32), ("i2", (1, ROWS), f32),
    ("a2", (F, ROWS), bf16), ("act", (FF, ROWS), bf16), ("slope", (FF, ROWS), bf16),
)
SHARED = (
    ("q", (F, ROWS), bf16), ("du", (FF, ROWS), bf16), ("t", (F, ROWS), f32), ("dz", (3 * F, ROWS), bf16),
)


def slot_kernel(names, *refs):
    r = Refs()
    for name, ref in zip(names, refs):
        setattr(r, name, ref)
    first = r.place[0] == 0
    source, target, label, live = unit_order(r.frames)
    fill_mask(r.mask, label)
    for j in range(UNITS):
        rows = pl.ds(pl.multiple_of(source[j] * UNIT, UNIT), UNIT)
        to = slice(j * UNIT, j * UNIT + UNIT)
        r.xin[to, :] = jnp.where(first, r.local[0, rows, :].astype(f32), r.arrived[rows, :].astype(f32))
        r.gin[to, :] = jnp.where(first, r.arrived[rows, :].astype(f32), r.local[1, rows, :].astype(f32))
    r.stream[...] = r.xin[...].T

    enc, pred = Refs(), Refs()
    enc.vec = columns(r.eg[...], r.eb[...], r.exb[...])
    pred.vec = columns(r.pg[...], r.pb[...], r.pxb[...])
    enc.project, enc.merge, enc.expand, enc.reduce = r.ew, r.em, r.ex, r.er
    pred.project, pred.merge, pred.expand, pred.reduce = r.pw, r.pm, r.px, r.pr
    es, ps = Refs(), Refs()
    for name, _, _ in KEPT:
        setattr(es, name, getattr(r, "e_" + name))
        setattr(ps, name, getattr(r, "p_" + name))
    for name, _, _ in SHARED:
        setattr(es, name, getattr(r, name))
        setattr(ps, name, getattr(r, name))
    es.e, es.over, ps.e, ps.over = r.e_e, r.e_over, r.p_e, r.p_over

    block_forward(r.stream, r.stream2, enc, es, HEADS, r.mask)
    r.sent[...] = r.stream2[...].astype(bf16)
    r.stream[...] = dot(r.embed[...], r.sent[...], 0, 0) + r.embed_bias[...].astype(f32).T
    block_forward(r.stream, r.stream2, pred, ps, PHEADS, r.mask)

    alive = lax.broadcasted_iota(jnp.int32, (F, ROWS), 1) < live * UNIT
    r.xin[...] = jnp.where(alive, r.stream2[...], 0.0).T
    r.stream[...] = jnp.where(alive, r.gin[...].T, 0.0)
    sums = block_backward(r.stream, pred, ps, PHEADS, r.grads.at[0], 384)
    r.q[...] = r.stream[...].astype(bf16)
    de = r.q[...]
    place(r.grads.at[0], 0, dot(r.sent[...], de, 1, 1))
    place_sums(r.grads.at[0], 4992, sums + [total(de)])
    r.grads[0, :, 5008:PART, :] = jnp.zeros((3, PART - 5008, 128), bf16)
    r.stream[...] = dot(r.embed[...], de, 1, 0).astype(bf16).astype(f32)
    sums = block_backward(r.stream, enc, es, HEADS, r.grads.at[1], 0)
    place_sums(r.grads.at[1], 4608, sums)
    r.grads[1, :, 4624:PART, :] = jnp.zeros((3, PART - 4624, 128), bf16)
    r.gin[...] = r.stream[...].T
    for j in range(UNITS):
        rows = pl.ds(pl.multiple_of(target[j] * UNIT, UNIT), UNIT)
        to = slice(j * UNIT, j * UNIT + UNIT)
        dx, out = r.gin[rows, :], r.xin[rows, :]
        r.kept[to, :] = jnp.where(first, dx, out)
        r.sends[to, :] = jnp.where(first, out, dx).astype(bf16)


def slot_call(side, frames, local, arrived, weights):
    args = [
        ("place", side), ("frames", frames), ("local", local), ("arrived", arrived),
    ] + list(zip(("eg", "eb", "ew", "em", "ex", "exb", "er", "embed", "embed_bias", "pg", "pb", "pw", "pm", "px", "pxb", "pr"), weights))
    outs = [
        ("grads", (2, 3, PART, 128), bf16), ("kept", (ROWS, F), f32), ("sends", (ROWS, F), bf16),
    ]
    scratch = [
        ("mask", (BLOCKS, BLOCK, BLOCK), f32), ("xin", (ROWS, F), f32), ("gin", (ROWS, F), f32),
        ("stream", (F, ROWS), f32), ("stream2", (F, ROWS), f32), ("sent", (F, ROWS), bf16),
        ("e_e", (HEADS, BLOCKS, BLOCK, BLOCK), bf16), ("p_e", (PHEADS, BLOCKS, BLOCK, BLOCK), bf16),
        ("e_over", (8, ROWS), f32), ("p_over", (16, ROWS), f32),
    ]
    scratch += [("e_" + n, sh, d) for n, sh, d in KEPT] + [("p_" + n, sh, d) for n, sh, d in KEPT]
    scratch += list(SHARED)
    names = [n for n, _ in args] + [n for n, _, _ in outs] + [n for n, _, _ in scratch]
    return pl.pallas_call(
        functools.partial(slot_kernel, names),
        out_shape=[jax.ShapeDtypeStruct(sh, d) for _, sh, d in outs],
        in_specs=[pl.BlockSpec(memory_space=pltpu.SMEM)] * 2
        + [pl.BlockSpec(memory_space=pltpu.VMEM)] * (len(args) - 2),
        out_specs=[pl.BlockSpec(memory_space=pltpu.VMEM)] * len(outs),
        scratch_shapes=[pltpu.VMEM(sh, d) for _, sh, d in scratch],
        compiler_params=pltpu.CompilerParams(vmem_limit_bytes=60 * 2**20),
    )(*[a for _, a in args])


LAYERS = (("pg", "pb", "pw", "pm", "px", "pxb", "pr"), ("eg", "eb", "ew", "em", "ex", "exb", "er"))
BIG = {"w": (F, 3 * F), "m": (F, F), "x": (F, FF), "r": (FF, F)}


def widen(g_ref, at, out_ref, rows, col):
    for c in range(3):
        out_ref[rows, col + c * 128 : col + c * 128 + 128] = g_ref[c, at : at + F, :].astype(f32)


def unpack_kernel(names, *refs):
    r = Refs()
    for name, ref in zip(names, refs):
        setattr(r, name, ref)
    copies = []

    def ship(name):
        copy = pltpu.make_async_copy(getattr(r, "s_" + name), getattr(r, name), r.sems.at[len(copies)])
        copy.start()
        copies.append(copy)

    for side, layer in enumerate(("p", "e")):
        g = r.grads.at[side]
        base, small = ((384, 4992), (0, 4608))[side]
        for part in range(4):
            rows = slice(part * F, part * F + F)
            widen(g, base + 3072 + part * F, getattr(r, "s_" + layer + "r"), rows, 0)
        ship(layer + "r")
        for part in range(4):
            widen(g, base + 1536 + part * F, getattr(r, "s_" + layer + "x"), slice(0, F), part * F)
        ship(layer + "x")
        for part in range(3):
            widen(g, base + part * F, getattr(r, "s_" + layer + "w"), slice(0, F), part * F)
        ship(layer + "w")
        widen(g, base + 1152, getattr(r, "s_" + layer + "m"), slice(0, F), 0)
        ship(layer + "m")
        if side == 0:
            widen(g, 0, r.s_embed, slice(0, F), 0)
            ship("embed")
        rows = jnp.concatenate([g[c, small : small + 16, :] for c in range(3)], axis=1).astype(f32)
        getattr(r, layer + "g")[...] = rows[0:2]
        getattr(r, layer + "b")[...] = rows[2:8]
        for part in range(4):
            getattr(r, layer + "xb")[:, part * F : part * F + F] = rows[8 + part : 9 + part]
        if side == 0:
            r.embed_bias[...] = rows[12:13]
    for copy in copies:
        copy.wait()


def unpack_call(grads):
    big = [("embed", (F, F))] + [(layer + n, BIG[n]) for layer in "pe" for n in BIG]
    small = [("embed_bias", (1, F))]
    for layer in "pe":
        small += [(layer + "g", (2, F)), (layer + "b", (6, F)), (layer + "xb", (1, FF))]
    names = ["grads"] + [n for n, _ in big + small] + ["s_" + n for n, _ in big] + ["sems"]
    outs = pl.pallas_call(
        functools.partial(unpack_kernel, names),
        out_shape=[jax.ShapeDtypeStruct(sh, f32) for _, sh in big + small],
        in_specs=[pl.BlockSpec(memory_space=pltpu.VMEM)],
        out_specs=[pl.BlockSpec(memory_space=pl.ANY)] * len(big)
        + [pl.BlockSpec(memory_space=pltpu.VMEM)] * len(small),
        scratch_shapes=[pltpu.VMEM(sh, f32) for _, sh in big] + [pltpu.SemaphoreType.DMA((len(big),))],
        compiler_params=pltpu.CompilerParams(vmem_limit_bytes=60 * 2**20),
    )(grads)
    return dict(zip([n for n, _ in big + small], outs))


def body(segment_data, clip_frames, *weights):
    position = lax.axis_index("pipe")
    first = position < 2
    side = (position // 2).reshape(1).astype(jnp.int32)
    local = segment_data[0, 0]
    frames = lax.dynamic_slice(clip_frames[0], (position // 2, position % 2, 0), (1, 1, CLIPS)).reshape(CLIPS)
    swap = [(0, 2), (1, 3), (2, 0), (3, 1)]
    arrived = lax.ppermute(jnp.where(first, local[1], local[0]), "pipe", swap)
    weights = [v.reshape(1, -1) if v.ndim == 1 else v for v in weights]
    grads, kept, sends = slot_call(side, frames, local, arrived, weights)
    back = lax.ppermute(sends, "pipe", swap).astype(f32)
    result = jnp.stack([jnp.where(first, kept, back), jnp.where(first, back, kept)])[None, None]
    grads = lax.psum(grads, ("pipe", "dp"))
    g = unpack_call(grads)
    order = ("eg", "eb", "ew", "em", "ex", "exb", "er", "embed", "embed_bias", "pg", "pb", "pw", "pm", "px", "pxb", "pr")
    flat = {"exb", "pxb", "embed_bias"}
    return (result,) + tuple(g[n].reshape(-1) if n in flat else g[n] for n in order)


def solution(mesh):
    return jax.shard_map(
        body,
        mesh=mesh,
        in_specs=(P("pipe", "dp", None, None, None), P("dp", None, None, None)) + (P(),) * 16,
        out_specs=(P("pipe", "dp", None, None, None),) + (P(),) * 16,
        check_vma=False,
    )
```

```python
import functools
import math

import jax
import jax.numpy as jnp
from jax import lax
from jax.experimental import pallas as pl
from jax.experimental.pallas import tpu as pltpu
from jax.sharding import PartitionSpec as P

HEADS = 6
PHEADS = 12
CLIPS = 8
F = 384
FF = 1536
ROWS = 512
UNIT = 64
UNITS = ROWS // UNIT
BLOCK = 256
BLOCKS = ROWS // BLOCK
TOTAL = 10240
EPS = 1e-06
MASKED = -1e30

f32 = jnp.float32
bf16 = jnp.bfloat16


def dot(a, b, ca, cb):
    return lax.dot_general(a, b, (((ca,), (cb,)), ((), ())), preferred_element_type=f32)


def unit_order(frames):
    rows = [frames[c] * (UNIT // 8) for c in range(CLIPS)]
    start, place = [], []
    total = jnp.int32(0)
    for c in range(CLIPS):
        start.append(total)
        total = total + rows[c]
    for c in range(CLIPS):
        before = jnp.int32(0)
        for d in range(CLIPS):
            if d < c:
                ahead = rows[d] >= rows[c]
            elif d > c:
                ahead = rows[d] > rows[c]
            else:
                continue
            before = before + jnp.where(ahead, rows[d], 0)
        place.append(before)
    source, label = [], []
    for j in range(UNITS):
        at = j * UNIT
        src, lab = jnp.int32(at), jnp.int32(CLIPS + j)
        for c in range(CLIPS):
            held = (at >= place[c]) & (at < place[c] + rows[c])
            src = jnp.where(held, start[c] + at - place[c], src)
            lab = jnp.where(held, c, lab)
        source.append(src)
        label.append(lab)
    return source, label, total


def fill_order(order_ref, source):
    lane = lax.broadcasted_iota(jnp.int32, (1, ROWS), 1)
    row = spread(source, (1, ROWS), 1) + lane % UNIT
    at = lax.broadcasted_iota(jnp.int32, (ROWS, ROWS), 0)
    order_ref[...] = jnp.where(at == row, 1.0, 0.0).astype(bf16)


def spread(values, shape, axis):
    at = lax.broadcasted_iota(jnp.int32, shape, axis) // UNIT
    out = jnp.full(shape, values[0], jnp.int32)
    for i in range(1, len(values)):
        out = jnp.where(at == i, values[i], out)
    return out


def fill_mask(mask_ref, label):
    for b in range(BLOCKS):
        own = label[b * 4 : b * 4 + 4]
        down = spread(own, (BLOCK, BLOCK), 0)
        across = spread(own, (BLOCK, BLOCK), 1)
        mask_ref[b] = jnp.where(down == across, 0.0, MASKED).astype(f32)


def norm(v, gain, shift):
    mean = jnp.mean(v, axis=0, keepdims=True)
    centred = v - mean
    inverse = lax.rsqrt(jnp.mean(centred * centred, axis=0, keepdims=True) + EPS)
    normed = centred * inverse
    return normed * gain + shift, normed, inverse


def norm_back(k, normed, inverse):
    return inverse * (
        k
        - jnp.mean(k, axis=0, keepdims=True)
        - normed * jnp.mean(k * normed, axis=0, keepdims=True)
    )


def block_forward(stream_ref, out_ref, w, s, heads, mask_ref):
    size = F // heads
    scale = math.log2(math.e) / math.sqrt(size)
    vec = w.vec
    for t in range(ROWS // 128):
        cols = slice(t * 128, t * 128 + 128)
        full, normed, inverse = norm(stream_ref[:, cols], vec[:, 0:1], vec[:, 2:3])
        s.n1[:, cols] = normed
        s.i1[:, cols] = inverse
        s.a1[:, cols] = full.astype(bf16)
    for part in range(3):
        rows = slice(part * F, part * F + F)
        z = dot(w.project[:, rows], s.a1[...], 0, 0)
        if part == 0:
            z = z + vec[:, 3:4]
        if part == 2:
            z = z + vec[:, 4:5]
        s.z[rows, :] = z.astype(bf16)
    for b in range(BLOCKS):
        cols = slice(b * BLOCK, b * BLOCK + BLOCK)
        for h in range(heads):
            own = slice(h * size, h * size + size)
            q = s.z[h * size : h * size + size, cols]
            k = s.z[F + h * size : F + h * size + size, cols]
            v = s.z[2 * F + h * size : 2 * F + h * size + size, cols]
            score = dot(k, q, 0, 0) * scale + mask_ref[b]
            e = jnp.exp2(score - jnp.max(score, axis=0, keepdims=True))
            over = 1.0 / jnp.sum(e, axis=0, keepdims=True)
            e = e.astype(bf16)
            s.e[h, b] = e
            s.over[h : h + 1, cols] = over
            s.o[own, cols] = (dot(v, e, 1, 0) * over).astype(bf16)
    middle = stream_ref[...] + (dot(w.merge[...], s.o[...], 0, 0) + vec[:, 5:6])
    s.m1[...] = middle
    for t in range(ROWS // 128):
        cols = slice(t * 128, t * 128 + 128)
        full, normed, inverse = norm(s.m1[:, cols], vec[:, 1:2], vec[:, 6:7])
        s.n2[:, cols] = normed
        s.i2[:, cols] = inverse
        s.a2[:, cols] = full.astype(bf16)
    for part in range(4):
        rows = slice(part * F, part * F + F)
        u = dot(w.expand[:, rows], s.a2[...], 0, 0) + vec[:, 8 + part : 9 + part]
        below = 0.5 * lax.erf(u * math.sqrt(0.5)) + 0.5
        density = jnp.exp2(u * u * (-0.5 * math.log2(math.e))) * (1.0 / math.sqrt(2.0 * math.pi))
        s.act[rows, :] = (u * below).astype(bf16)
        s.slope[rows, :] = (below + u * density).astype(bf16)
    out_ref[...] = s.m1[...] + (dot(w.reduce[...], s.act[...], 0, 0) + vec[:, 7:8])


def place(g_ref, at, value):
    for c in range(3):
        g_ref[c, at : at + value.shape[0], :] = value[:, c * 128 : c * 128 + 128].astype(bf16)


def total(x):
    return jnp.sum(x.astype(f32), axis=1, keepdims=True)


def block_backward(grad_ref, w, s, heads, g_ref, at, tick):
    size = F // heads
    vec = w.vec
    sums = [None] * 12
    s.q[...] = grad_ref[...].astype(bf16)
    q2 = s.q[...]
    sums[7] = total(q2)
    for part in range(4):
        rows = slice(part * F, part * F + F)
        place(g_ref, at["reduce"] + part * F, dot(s.act[rows, :], q2, 1, 1))
        du = (dot(w.reduce[rows, :], q2, 1, 0) * s.slope[rows, :].astype(f32)).astype(bf16)
        s.du[rows, :] = du
        sums[8 + part] = total(du)
        place(g_ref, at["expand"] + part * F, dot(s.a2[...], du, 1, 1))
    tick("hidden")
    da = dot(w.expand[...], s.du[...], 1, 0)
    s.t[...] = da
    sums[1] = total(da * s.n2[...])
    sums[6] = total(da)
    for t in range(ROWS // 128):
        cols = slice(t * 128, t * 128 + 128)
        grad_ref[:, cols] += norm_back(s.t[:, cols] * vec[:, 1:2], s.n2[:, cols], s.i2[:, cols])
    s.q[...] = grad_ref[...].astype(bf16)
    q1 = s.q[...]
    sums[5] = total(q1)
    place(g_ref, at["merge"], dot(s.o[...], q1, 1, 1))
    s.t[...] = dot(w.merge[...], q1, 1, 0)
    tick("merge")
    for b in range(BLOCKS):
        cols = slice(b * BLOCK, b * BLOCK + BLOCK)
        for h in range(heads):
            lo = h * size
            own = slice(lo, lo + size)
            q = s.z[lo : lo + size, cols]
            k = s.z[F + lo : F + lo + size, cols]
            v = s.z[2 * F + lo : 2 * F + lo + size, cols]
            do = (s.t[own, cols] * s.over[h : h + 1, cols]).astype(bf16)
            delta = jnp.sum(do.astype(f32) * s.o[own, cols].astype(f32), axis=0, keepdims=True)
            e = s.e[h, b]
            dp = dot(v, do, 0, 0) - delta
            ds = dp.astype(bf16) * e
            s.dz[2 * F + lo : 2 * F + lo + size, cols] = dot(do, e, 1, 1).astype(bf16)
            s.dz[lo : lo + size, cols] = (dot(k, ds, 1, 0) * (1.0 / math.sqrt(size))).astype(bf16)
            s.dz[F + lo : F + lo + size, cols] = (dot(q, ds, 1, 1) * (1.0 / math.sqrt(size))).astype(bf16)
        tick("block")
    sums[3] = total(s.dz[0:F, :])
    sums[4] = total(s.dz[2 * F : 3 * F, :])
    for part in range(3):
        rows = slice(part * F, part * F + F)
        place(g_ref, at["project"] + part * F, dot(s.a1[...], s.dz[rows, :], 1, 1))
    da = dot(w.project[...], s.dz[...], 1, 0)
    s.t[...] = da
    sums[0] = total(da * s.n1[...])
    sums[2] = total(da)
    tick("project")
    for t in range(ROWS // 128):
        cols = slice(t * 128, t * 128 + 128)
        grad_ref[:, cols] += norm_back(s.t[:, cols] * vec[:, 0:1], s.n1[:, cols], s.i1[:, cols])
    return sums


def columns(gains, biases, hidden):
    rows = [gains.astype(f32), biases.astype(f32)]
    for part in range(4):
        rows.append(hidden[:, part * F : part * F + F].astype(f32))
    rows.append(jnp.zeros((4, F), f32))
    return jnp.concatenate(rows, axis=0).T


def place_sums(g_ref, at, sums):
    lane = lax.broadcasted_iota(jnp.int32, (F, 128), 1)
    table = jnp.zeros((F, 128), f32)
    for i, column in enumerate(sums):
        table = jnp.where(lane == i, column, table)
    place(g_ref, at, table.T[0:16, :])


class Refs:
    pass


KEPT = (
    ("n1", (F, ROWS), f32), ("i1", (1, ROWS), f32), ("a1", (F, ROWS), bf16), ("z", (3 * F, ROWS), bf16),
    ("o", (F, ROWS), bf16), ("m1", (F, ROWS), f32), ("n2", (F, ROWS), f32), ("i2", (1, ROWS), f32),
    ("a2", (F, ROWS), bf16), ("act", (FF, ROWS), bf16), ("slope", (FF, ROWS), bf16),
)
SHARED = (
    ("q", (F, ROWS), bf16), ("du", (FF, ROWS), bf16), ("t", (F, ROWS), f32), ("dz", (3 * F, ROWS), bf16),
)


PHASES = ((0, 3072), (3072, 2048), (5120, 3584), (8704, 1536))
PRED_AT = {"reduce": 0, "expand": 1536, "merge": 3072, "project": 3456, "embed": 4608, "small": 4992, "end": 5008}
ENC_AT = {"reduce": 5120, "expand": 6656, "merge": 8192, "gap": 8576, "project": 8704, "small": 9856, "end": 9872}
ORDERS = ("xyz", "yzx", "zxy")
WEIGHTS = (
    ("ew", (F, 3 * F)), ("em", (F, F)), ("ex", (F, FF)), ("er", (FF, F)), ("embed", (F, F)),
    ("pw", (F, 3 * F)), ("pm", (F, F)), ("px", (F, FF)), ("pr", (FF, F)),
)


class Where:
    def __init__(self):
        p, d = lax.axis_index("pipe"), lax.axis_index("dp")
        self.core, low = p % 2, p // 2
        self.at = {"x": d // 8, "y": d % 4, "z": ((d // 4) % 2) * 2 + low}
        self.side = low

    def device(self, core, at):
        return {"pipe": (at["z"] % 2) * 2 + core, "dp": at["x"] * 8 + (at["z"] // 2) * 4 + at["y"]}

    def twin(self):
        return self.device(1 - self.core, self.at)

    def along(self, axis, d):
        to = (self.at[axis] + d) % 4
        return self.device(self.core, {**self.at, axis: to}), to

    def pair(self):
        z = self.at["z"]
        return self.device(self.core, {**self.at, "z": z + 1 - 2 * (z % 2)})

    def everyone(self):
        return [self.twin()] + [self.along(axis, d)[0] for axis in "xyz" for d in (1, 2, 3)]


def send(src, dst, sems, i, device):
    copy = pltpu.make_async_remote_copy(
        src_ref=src, dst_ref=dst, send_sem=sems.at[0, i], recv_sem=sems.at[1, i],
        device_id=device, device_id_type=pl.DeviceIdType.MESH,
    )
    copy.start()
    return copy


def reduce_phase(me, g, phase, recv, sems, free):
    base, size = phase
    half, quarter, small = size // 2, size // 8, size // 32
    mine, others = base + me.core * half, base + (1 - me.core) * half
    copy = send(g.at[:, pl.ds(others, half), :], recv.core, sems, 0, me.twin())
    yield
    copy.wait()

    def release(i, devices):
        for device in devices:
            pl.semaphore_signal(free.at[i], inc=1, device_id=device, device_id_type=pl.DeviceIdType.MESH)

    around = [me.along(axis, d)[0] for axis in "xyz" for d in (1, 2, 3)]
    release(0, [me.twin()])
    for c in range(3):
        rows = pl.ds(mine, half)
        g[c, rows, :] = (g[c, rows, :].astype(f32) + recv.core[c].astype(f32)).astype(bf16)

    def scatter(start, rows, buf, first_sem, step):
        copies = []
        for d in (1, 2, 3):
            for c in range(3):
                to, index = me.along(ORDERS[c][step], d)
                copies.append(
                    send(
                        g.at[c, pl.ds(start[c] + index * rows, rows), :], buf.at[c, d - 1], sems,
                        first_sem + len(copies), to,
                    )
                )
        return copies

    def gather(start, rows, first_sem, step):
        copies = []
        for d in (1, 2, 3):
            for c in range(3):
                to, _ = me.along(ORDERS[c][step], d)
                block = g.at[c, pl.ds(start[c], rows), :]
                copies.append(send(block, block, sems, first_sem + len(copies), to))
        return copies

    def add(start, rows, buf):
        for c in range(3):
            own = pl.ds(start[c], rows)
            terms = g[c, own, :].astype(f32)
            for d in range(3):
                terms = terms + buf[c, d].astype(f32)
            g[c, own, :] = terms.astype(bf16)

    zero = [mine] * 3
    copies = scatter(zero, quarter, recv.one, 1, 0)
    yield
    for copy in copies:
        copy.wait()
    release(1, around)
    one = [mine + me.at[ORDERS[c][0]] * quarter for c in range(3)]
    add(one, quarter, recv.one)
    copies = scatter(one, small, recv.two, 10, 1)
    yield
    for copy in copies:
        copy.wait()
    release(2, around)
    two = [one[c] + me.at[ORDERS[c][1]] * small for c in range(3)]
    add(two, small, recv.two)
    copies = []
    for c in range(3):
        slot = me.at[ORDERS[c][2]]
        recv.three[c, slot] = g[c, pl.ds(two[c], small), :]
    for d in (1, 2, 3):
        for c in range(3):
            slot = me.at[ORDERS[c][2]]
            to, _ = me.along(ORDERS[c][2], d)
            block = recv.three.at[c, slot]
            copies.append(send(block, block, sems, 19 + len(copies), to))
    yield
    for copy in copies:
        copy.wait()
    for c in range(3):
        terms = recv.three[c, 0].astype(f32)
        for j in range(1, 4):
            terms = terms + recv.three[c, j].astype(f32)
        g[c, pl.ds(two[c], small), :] = terms.astype(bf16)
    pl.semaphore_wait(free.at[2], len(around))
    copies = gather(two, small, 28, 1)
    yield
    for copy in copies:
        copy.wait()
    pl.semaphore_wait(free.at[1], len(around))
    copies = gather(one, quarter, 37, 0)
    yield
    for copy in copies:
        copy.wait()
    pl.semaphore_wait(free.at[0], 1)
    block = g.at[:, pl.ds(mine, half), :]
    copy = send(block, block, sems, 46, me.twin())
    yield
    copy.wait()


def slot_kernel(names, *refs):
    r = Refs()
    for name, ref in zip(names, refs):
        setattr(r, name, ref)
    me = Where()
    first = me.side == 0
    loads = {}
    for i, (name, _) in enumerate(WEIGHTS):
        loads[name] = pltpu.make_async_copy(getattr(r, "h_" + name), getattr(r, name), r.loads.at[i])
        loads[name].start()
    barrier = pltpu.get_barrier_semaphore()
    friends = me.everyone()
    for device in friends:
        pl.semaphore_signal(barrier, inc=1, device_id=device, device_id_type=pl.DeviceIdType.MESH)
    pl.semaphore_wait(barrier, len(friends))
    swap = send(r.local.at[1 - me.side], r.arrived, r.swaps, 0, me.pair())

    source, label, live = unit_order([r.frames[0, me.side, me.core, c] for c in range(CLIPS)])
    fill_mask(r.mask, label)
    fill_order(r.order, source)
    enc, pred = Refs(), Refs()
    enc.vec = columns(r.eg[...], r.eb[...], r.exb[...])
    pred.vec = columns(r.pg[...], r.pb[...], r.pxb[...])
    enc.project, enc.merge, enc.expand, enc.reduce = r.ew, r.em, r.ex, r.er
    pred.project, pred.merge, pred.expand, pred.reduce = r.pw, r.pm, r.px, r.pr
    es, ps = Refs(), Refs()
    for name, _, _ in KEPT:
        setattr(es, name, getattr(r, "e_" + name))
        setattr(ps, name, getattr(r, "p_" + name))
    for name, _, _ in SHARED:
        setattr(es, name, getattr(r, name))
        setattr(ps, name, getattr(r, name))
    es.e, es.over, ps.e, ps.over = r.e_e, r.e_over, r.p_e, r.p_over

    swap.wait()
    x = jnp.where(first, r.local[0], r.arrived[...])
    r.stream[...] = dot(x, r.order[...], 0, 0)
    for copy in loads.values():
        copy.wait()

    block_forward(r.stream, r.stream2, enc, es, HEADS, r.mask)
    r.sent[...] = r.stream2[...].astype(bf16)
    r.stream[...] = dot(r.embed[...], r.sent[...], 0, 0) + r.embed_bias[...].astype(f32).T
    block_forward(r.stream, r.stream2, pred, ps, PHEADS, r.mask)

    alive = lax.broadcasted_iota(jnp.int32, (F, ROWS), 1) < live
    r.out[...] = dot(r.order[...], jnp.where(alive, r.stream2[...], 0.0).astype(bf16), 1, 1).astype(bf16)
    cotangent = jnp.where(first, r.arrived[...], r.local[1])
    r.stream[...] = jnp.where(alive, dot(cotangent, r.order[...], 0, 0), 0.0)

    g = r.grads
    phases = []
    for i, phase in enumerate(PHASES):
        recv = Refs()
        for name in ("core", "one", "two", "three"):
            setattr(recv, name, getattr(r, f"{name}{i}"))
        phases.append(reduce_phase(me, g, phase, recv, r.sems.at[i], r.free.at[i]))

    def step(*which):
        for i in which:
            next(phases[i], None)

    plan = PLAN["pred"]
    sums = block_backward(r.stream, pred, ps, PHEADS, g, PRED_AT, lambda name: step(*plan.get(name, ())))
    r.q[...] = r.stream[...].astype(bf16)
    de = r.q[...]
    place(g, PRED_AT["embed"], dot(r.sent[...], de, 1, 1))
    place_sums(g, PRED_AT["small"], sums + [total(de)])
    g[:, PRED_AT["end"] : ENC_AT["reduce"], :] = jnp.zeros((3, ENC_AT["reduce"] - PRED_AT["end"], 128), bf16)
    g[:, ENC_AT["gap"] : ENC_AT["project"], :] = jnp.zeros((3, ENC_AT["project"] - ENC_AT["gap"], 128), bf16)
    g[:, ENC_AT["end"] : TOTAL, :] = jnp.zeros((3, TOTAL - ENC_AT["end"], 128), bf16)
    r.stream[...] = dot(r.embed[...], de, 1, 0).astype(bf16).astype(f32)
    step(*PLAN["embed"])
    later = PLAN["enc"]
    sums = block_backward(r.stream, enc, es, HEADS, g, ENC_AT, lambda name: step(*later.get(name, ())))
    place_sums(g, ENC_AT["small"], sums)
    step(*PLAN["ready"])
    dx, out = dot(r.order[...], r.stream[...].astype(bf16), 1, 1).astype(bf16), r.out[...]
    r.kept[...] = jnp.where(first, dx, out)
    r.sends[...] = jnp.where(first, out, dx)
    swap = send(r.sends, r.back, r.swaps, 1, me.pair())
    for which in PLAN["last"]:
        step(*which)
    swap.wait()


PLAN = {
    "pred": {"hidden": (0,), "merge": (0,), "block": (0,), "project": (0,)},
    "embed": (0, 1),
    "enc": {"hidden": (0, 1), "merge": (0, 1, 2), "block": (0, 1, 2), "project": (1, 2)},
    "ready": (1, 2, 3),
    "last": ((0, 1, 2, 3),) * 8,
}


def slot_call(frames, local, weights):
    args = [("frames", frames), ("local", local)]
    big = {name for name, _ in WEIGHTS}
    order = ("eg", "eb", "ew", "em", "ex", "exb", "er", "embed", "embed_bias", "pg", "pb", "pw", "pm", "px", "pxb", "pr")
    specs = [pl.BlockSpec(memory_space=pltpu.SMEM), pl.BlockSpec(memory_space=pltpu.VMEM)]
    for name, weight in zip(order, weights):
        args.append(("h_" + name if name in big else name, weight))
        specs.append(pl.BlockSpec(memory_space=pl.ANY if name in big else pltpu.VMEM))
    outs = [("grads", (3, TOTAL, 128), bf16), ("kept", (ROWS, F), bf16), ("back", (ROWS, F), bf16)]
    scratch = [
        ("mask", (BLOCKS, BLOCK, BLOCK), f32), ("order", (ROWS, ROWS), bf16), ("out", (ROWS, F), bf16),
        ("stream", (F, ROWS), f32), ("stream2", (F, ROWS), f32), ("sent", (F, ROWS), bf16),
        ("arrived", (ROWS, F), bf16), ("sends", (ROWS, F), bf16),
        ("e_e", (HEADS, BLOCKS, BLOCK, BLOCK), bf16), ("p_e", (PHEADS, BLOCKS, BLOCK, BLOCK), bf16),
        ("e_over", (8, ROWS), f32), ("p_over", (16, ROWS), f32),
    ]
    scratch += [(n, sh, bf16) for n, sh in WEIGHTS]
    scratch += [("e_" + n, sh, d) for n, sh, d in KEPT] + [("p_" + n, sh, d) for n, sh, d in KEPT]
    scratch += list(SHARED)
    for i, (_, size) in enumerate(PHASES):
        scratch += [
            (f"core{i}", (3, size // 2, 128), bf16), (f"one{i}", (3, 3, size // 8, 128), bf16),
            (f"two{i}", (3, 3, size // 32, 128), bf16), (f"three{i}", (3, 4, size // 32, 128), bf16),
        ]
    sems = [("loads", (len(WEIGHTS),)), ("swaps", (2, 2)), ("sems", (len(PHASES), 2, 47))]
    names = [n for n, _ in args] + [n for n, _, _ in outs] + [n for n, _, _ in scratch] + [n for n, _ in sems] + ["free"]
    return pl.pallas_call(
        functools.partial(slot_kernel, names),
        out_shape=[jax.ShapeDtypeStruct(sh, d) for _, sh, d in outs],
        in_specs=specs,
        out_specs=[pl.BlockSpec(memory_space=pltpu.VMEM)] * len(outs),
        scratch_shapes=[pltpu.VMEM(sh, d) for _, sh, d in scratch] + [pltpu.SemaphoreType.DMA(sh) for _, sh in sems]
        + [pltpu.SemaphoreType.REGULAR((len(PHASES), 3))],
        compiler_params=pltpu.CompilerParams(
            vmem_limit_bytes=62 * 2**20, collective_id=0, has_side_effects=True
        ),
    )(*[a for _, a in args])


LAYERS = (("pg", "pb", "pw", "pm", "px", "pxb", "pr"), ("eg", "eb", "ew", "em", "ex", "exb", "er"))
BIG = {"w": (F, 3 * F), "m": (F, F), "x": (F, FF), "r": (FF, F)}


def widen(g_ref, at, out_ref, rows, col):
    for c in range(3):
        out_ref[rows, col + c * 128 : col + c * 128 + 128] = g_ref[c, at : at + F, :].astype(f32)


def unpack_kernel(names, *refs):
    r = Refs()
    for name, ref in zip(names, refs):
        setattr(r, name, ref)
    copies = []

    def ship(src, dst):
        copy = pltpu.make_async_copy(src, dst, r.sems.at[len(copies)])
        copy.start()
        copies.append(copy)

    side = lax.axis_index("pipe") // 2
    r.wide[0] = r.kept[...].astype(f32)
    ship(r.wide.at[0], r.result.at[side])
    r.wide[1] = r.back[...].astype(f32)
    ship(r.wide.at[1], r.result.at[1 - side])
    g = r.grads
    for layer, at in (("p", PRED_AT), ("e", ENC_AT)):
        for part in range(4):
            rows = slice(part * F, part * F + F)
            widen(g, at["reduce"] + part * F, getattr(r, "s_" + layer + "r"), rows, 0)
        ship(getattr(r, "s_" + layer + "r"), getattr(r, layer + "r"))
        for part in range(4):
            widen(g, at["expand"] + part * F, getattr(r, "s_" + layer + "x"), slice(0, F), part * F)
        ship(getattr(r, "s_" + layer + "x"), getattr(r, layer + "x"))
        for part in range(3):
            widen(g, at["project"] + part * F, getattr(r, "s_" + layer + "w"), slice(0, F), part * F)
        ship(getattr(r, "s_" + layer + "w"), getattr(r, layer + "w"))
        widen(g, at["merge"], getattr(r, "s_" + layer + "m"), slice(0, F), 0)
        ship(getattr(r, "s_" + layer + "m"), getattr(r, layer + "m"))
        if layer == "p":
            widen(g, at["embed"], r.s_embed, slice(0, F), 0)
            ship(r.s_embed, r.embed)
        small = at["small"]
        rows = jnp.concatenate([g[c, small : small + 16, :] for c in range(3)], axis=1).astype(f32)
        getattr(r, layer + "g")[...] = rows[0:2]
        getattr(r, layer + "b")[...] = rows[2:8]
        for part in range(4):
            getattr(r, layer + "xb")[part * F : part * F + F] = rows[8 + part]
        if layer == "p":
            r.embed_bias[...] = rows[12]
    for copy in copies:
        copy.wait()


def unpack_call(grads, kept, back):
    big = [("embed", (F, F))] + [(layer + n, BIG[n]) for layer in "pe" for n in BIG]
    small = [("embed_bias", (F,))]
    for layer in "pe":
        small += [(layer + "g", (2, F)), (layer + "b", (6, F)), (layer + "xb", (FF,))]
    outs = [("result", (2, ROWS, F))] + big + small
    names = ["grads", "kept", "back"] + [n for n, _ in outs] + ["s_" + n for n, _ in big] + ["wide", "sems"]
    values = pl.pallas_call(
        functools.partial(unpack_kernel, names),
        out_shape=[jax.ShapeDtypeStruct(sh, f32) for _, sh in outs],
        in_specs=[pl.BlockSpec(memory_space=pltpu.VMEM)] * 3,
        out_specs=[pl.BlockSpec(memory_space=pl.ANY)] * (1 + len(big))
        + [pl.BlockSpec(memory_space=pltpu.VMEM)] * len(small),
        scratch_shapes=[pltpu.VMEM(sh, f32) for _, sh in big]
        + [pltpu.VMEM((2, ROWS, F), f32), pltpu.SemaphoreType.DMA((len(big) + 2,))],
        compiler_params=pltpu.CompilerParams(vmem_limit_bytes=60 * 2**20),
    )(grads, kept, back)
    return dict(zip([n for n, _ in outs], values))


def body(segment_data, clip_frames, *weights):
    weights = [v.reshape(1, -1) if v.ndim == 1 else v for v in weights]
    g = unpack_call(*slot_call(clip_frames, segment_data[0, 0], weights))
    order = ("eg", "eb", "ew", "em", "ex", "exb", "er", "embed", "embed_bias", "pg", "pb", "pw", "pm", "px", "pxb", "pr")
    return (g["result"][None, None],) + tuple(g[n] for n in order)


def solution(mesh):
    return jax.shard_map(
        body,
        mesh=mesh,
        in_specs=(P("pipe", "dp", None, None, None), P("dp", None, None, None)) + (P(),) * 16,
        out_specs=(P("pipe", "dp", None, None, None),) + (P(),) * 16,
        check_vma=False,
    )
```

```python
import functools
import math

import jax
import jax.numpy as jnp
from jax import lax
from jax.experimental import pallas as pl
from jax.experimental.pallas import tpu as pltpu
from jax.sharding import PartitionSpec as P

HEADS = 6
PHEADS = 12
CLIPS = 8
F = 384
FF = 1536
ROWS = 512
UNIT = 64
UNITS = ROWS // UNIT
BLOCK = 256
BLOCKS = ROWS // BLOCK
TOTAL = 10240
EPS = 1e-06
MASKED = -1e30

f32 = jnp.float32
bf16 = jnp.bfloat16


def dot(a, b, ca, cb):
    return lax.dot_general(a, b, (((ca,), (cb,)), ((), ())), preferred_element_type=f32)


def unit_order(frames):
    rows = [frames[c] * (UNIT // 8) for c in range(CLIPS)]
    start, place = [], []
    total = jnp.int32(0)
    for c in range(CLIPS):
        start.append(total)
        total = total + rows[c]
    for c in range(CLIPS):
        before = jnp.int32(0)
        for d in range(CLIPS):
            if d < c:
                ahead = rows[d] >= rows[c]
            elif d > c:
                ahead = rows[d] > rows[c]
            else:
                continue
            before = before + jnp.where(ahead, rows[d], 0)
        place.append(before)
    source, label = [], []
    for j in range(UNITS):
        at = j * UNIT
        src, lab = jnp.int32(at), jnp.int32(CLIPS + j)
        for c in range(CLIPS):
            held = (at >= place[c]) & (at < place[c] + rows[c])
            src = jnp.where(held, start[c] + at - place[c], src)
            lab = jnp.where(held, c, lab)
        source.append(src)
        label.append(lab)
    return source, label, total


def fill_order(order_ref, source):
    lane = lax.broadcasted_iota(jnp.int32, (1, ROWS), 1)
    row = spread(source, (1, ROWS), 1) + lane % UNIT
    at = lax.broadcasted_iota(jnp.int32, (ROWS, ROWS), 0)
    order_ref[...] = jnp.where(at == row, 1.0, 0.0).astype(bf16)


def spread(values, shape, axis):
    at = lax.broadcasted_iota(jnp.int32, shape, axis) // UNIT
    out = jnp.full(shape, values[0], jnp.int32)
    for i in range(1, len(values)):
        out = jnp.where(at == i, values[i], out)
    return out


def fill_mask(mask_ref, label):
    for b in range(BLOCKS):
        own = label[b * 4 : b * 4 + 4]
        down = spread(own, (BLOCK, BLOCK), 0)
        across = spread(own, (BLOCK, BLOCK), 1)
        mask_ref[b] = jnp.where(down == across, 0.0, MASKED).astype(f32)


def norm(v, gain, shift):
    mean = jnp.mean(v, axis=0, keepdims=True)
    centred = v - mean
    inverse = lax.rsqrt(jnp.mean(centred * centred, axis=0, keepdims=True) + EPS)
    normed = centred * inverse
    return normed * gain + shift, normed, inverse


def norm_back(k, normed, inverse):
    return inverse * (
        k
        - jnp.mean(k, axis=0, keepdims=True)
        - normed * jnp.mean(k * normed, axis=0, keepdims=True)
    )


def block_forward(stream_ref, out_ref, w, s, heads, mask_ref):
    size = F // heads
    scale = math.log2(math.e) / math.sqrt(size)
    vec = w.vec
    for t in range(ROWS // 128):
        cols = slice(t * 128, t * 128 + 128)
        full, normed, inverse = norm(stream_ref[:, cols], vec[:, 0:1], vec[:, 2:3])
        s.n1[:, cols] = normed
        s.i1[:, cols] = inverse
        s.a1[:, cols] = full.astype(bf16)
    for part in range(3):
        rows = slice(part * F, part * F + F)
        z = dot(w.project[:, rows], s.a1[...], 0, 0)
        if part == 0:
            z = z + vec[:, 3:4]
        if part == 2:
            z = z + vec[:, 4:5]
        s.z[rows, :] = z.astype(bf16)
    for b in range(BLOCKS):
        cols = slice(b * BLOCK, b * BLOCK + BLOCK)
        for h in range(heads):
            own = slice(h * size, h * size + size)
            q = s.z[h * size : h * size + size, cols]
            k = s.z[F + h * size : F + h * size + size, cols]
            v = s.z[2 * F + h * size : 2 * F + h * size + size, cols]
            score = dot(k, q, 0, 0) * scale + mask_ref[b]
            e = jnp.exp2(score - jnp.max(score, axis=0, keepdims=True))
            over = 1.0 / jnp.sum(e, axis=0, keepdims=True)
            e = e.astype(bf16)
            s.e[h, b] = e
            s.over[h : h + 1, cols] = over
            s.o[own, cols] = (dot(v, e, 1, 0) * over).astype(bf16)
    middle = stream_ref[...] + (dot(w.merge[...], s.o[...], 0, 0) + vec[:, 5:6])
    s.m1[...] = middle
    for t in range(ROWS // 128):
        cols = slice(t * 128, t * 128 + 128)
        full, normed, inverse = norm(s.m1[:, cols], vec[:, 1:2], vec[:, 6:7])
        s.n2[:, cols] = normed
        s.i2[:, cols] = inverse
        s.a2[:, cols] = full.astype(bf16)
    for part in range(4):
        rows = slice(part * F, part * F + F)
        u = dot(w.expand[:, rows], s.a2[...], 0, 0) + vec[:, 8 + part : 9 + part]
        below = 0.5 * lax.erf(u * math.sqrt(0.5)) + 0.5
        density = jnp.exp2(u * u * (-0.5 * math.log2(math.e))) * (1.0 / math.sqrt(2.0 * math.pi))
        s.act[rows, :] = (u * below).astype(bf16)
        s.slope[rows, :] = (below + u * density).astype(bf16)
    out_ref[...] = s.m1[...] + (dot(w.reduce[...], s.act[...], 0, 0) + vec[:, 7:8])


def place(g_ref, at, value):
    for c in range(3):
        g_ref[c, at : at + value.shape[0], :] = value[:, c * 128 : c * 128 + 128].astype(bf16)


def total(x):
    return jnp.sum(x.astype(f32), axis=1, keepdims=True)


def block_backward(grad_ref, w, s, heads, g_ref, at, tick):
    size = F // heads
    vec = w.vec
    sums = [None] * 12
    s.q[...] = grad_ref[...].astype(bf16)
    q2 = s.q[...]
    sums[7] = total(q2)
    for part in range(4):
        rows = slice(part * F, part * F + F)
        place(g_ref, at["reduce"] + part * F, dot(s.act[rows, :], q2, 1, 1))
    tick()
    for part in range(4):
        rows = slice(part * F, part * F + F)
        du = (dot(w.reduce[rows, :], q2, 1, 0) * s.slope[rows, :].astype(f32)).astype(bf16)
        s.du[rows, :] = du
        sums[8 + part] = total(du)
        place(g_ref, at["expand"] + part * F, dot(s.a2[...], du, 1, 1))
        tick()
    da = dot(w.expand[...], s.du[...], 1, 0)
    s.t[...] = da
    sums[1] = total(da * s.n2[...])
    sums[6] = total(da)
    for t in range(ROWS // 128):
        cols = slice(t * 128, t * 128 + 128)
        grad_ref[:, cols] += norm_back(s.t[:, cols] * vec[:, 1:2], s.n2[:, cols], s.i2[:, cols])
    s.q[...] = grad_ref[...].astype(bf16)
    q1 = s.q[...]
    sums[5] = total(q1)
    place(g_ref, at["merge"], dot(s.o[...], q1, 1, 1))
    s.t[...] = dot(w.merge[...], q1, 1, 0)
    tick()
    for b in range(BLOCKS):
        cols = slice(b * BLOCK, b * BLOCK + BLOCK)
        for h in range(heads):
            lo = h * size
            own = slice(lo, lo + size)
            q = s.z[lo : lo + size, cols]
            k = s.z[F + lo : F + lo + size, cols]
            v = s.z[2 * F + lo : 2 * F + lo + size, cols]
            do = (s.t[own, cols] * s.over[h : h + 1, cols]).astype(bf16)
            delta = jnp.sum(do.astype(f32) * s.o[own, cols].astype(f32), axis=0, keepdims=True)
            e = s.e[h, b]
            dp = dot(v, do, 0, 0) - delta
            ds = dp.astype(bf16) * e
            s.dz[2 * F + lo : 2 * F + lo + size, cols] = dot(do, e, 1, 1).astype(bf16)
            s.dz[lo : lo + size, cols] = (dot(k, ds, 1, 0) * (1.0 / math.sqrt(size))).astype(bf16)
            s.dz[F + lo : F + lo + size, cols] = (dot(q, ds, 1, 1) * (1.0 / math.sqrt(size))).astype(bf16)
            if h % 3 == 2:
                tick()
    sums[3] = total(s.dz[0:F, :])
    sums[4] = total(s.dz[2 * F : 3 * F, :])
    for part in range(3):
        rows = slice(part * F, part * F + F)
        place(g_ref, at["project"] + part * F, dot(s.a1[...], s.dz[rows, :], 1, 1))
    da = dot(w.project[...], s.dz[...], 1, 0)
    s.t[...] = da
    sums[0] = total(da * s.n1[...])
    sums[2] = total(da)
    tick()
    for t in range(ROWS // 128):
        cols = slice(t * 128, t * 128 + 128)
        grad_ref[:, cols] += norm_back(s.t[:, cols] * vec[:, 0:1], s.n1[:, cols], s.i1[:, cols])
    return sums


def columns(gains, biases, hidden):
    rows = [gains.astype(f32), biases.astype(f32)]
    for part in range(4):
        rows.append(hidden[part * F : part * F + F].astype(f32).reshape(1, F))
    rows.append(jnp.zeros((4, F), f32))
    return jnp.concatenate(rows, axis=0).T


def place_sums(g_ref, at, sums):
    lane = lax.broadcasted_iota(jnp.int32, (F, 128), 1)
    table = jnp.zeros((F, 128), f32)
    for i, column in enumerate(sums):
        table = jnp.where(lane == i, column, table)
    place(g_ref, at, table.T[0:16, :])


class Refs:
    pass


KEPT = (
    ("n1", (F, ROWS), f32), ("i1", (1, ROWS), f32), ("a1", (F, ROWS), bf16), ("z", (3 * F, ROWS), bf16),
    ("o", (F, ROWS), bf16), ("m1", (F, ROWS), f32), ("n2", (F, ROWS), f32), ("i2", (1, ROWS), f32),
    ("a2", (F, ROWS), bf16), ("act", (FF, ROWS), bf16), ("slope", (FF, ROWS), bf16),
)
SHARED = (
    ("q", (F, ROWS), bf16), ("du", (FF, ROWS), bf16), ("t", (F, ROWS), f32), ("dz", (3 * F, ROWS), bf16),
)


PHASES = ((0, 1536), (1536, 1536), (3072, 2048), (5120, 1536), (6656, 2048), (8704, 1536))
PRED_AT = {"reduce": 0, "expand": 1536, "merge": 3072, "project": 3456, "embed": 4608, "small": 4992, "end": 5008}
ENC_AT = {"reduce": 5120, "expand": 6656, "merge": 8192, "gap": 8576, "project": 8704, "small": 9856, "end": 9872}
ORDERS = ("xyz", "yzx", "zxy")
WEIGHTS = (
    ("ew", (F, 3 * F)), ("em", (F, F)), ("ex", (F, FF)), ("er", (FF, F)), ("embed", (F, F)),
    ("pw", (F, 3 * F)), ("pm", (F, F)), ("px", (F, FF)), ("pr", (FF, F)),
)


class Where:
    def __init__(self):
        p, d = lax.axis_index("pipe"), lax.axis_index("dp")
        self.core, low = p % 2, p // 2
        self.at = {"x": d // 8, "y": d % 4, "z": ((d // 4) % 2) * 2 + low}
        self.side = low

    def device(self, core, at):
        return {"pipe": (at["z"] % 2) * 2 + core, "dp": at["x"] * 8 + (at["z"] // 2) * 4 + at["y"]}

    def twin(self):
        return self.device(1 - self.core, self.at)

    def along(self, axis, d):
        to = (self.at[axis] + d) % 4
        return self.device(self.core, {**self.at, axis: to}), to

    def pair(self):
        z = self.at["z"]
        return self.device(self.core, {**self.at, "z": z + 1 - 2 * (z % 2)})

    def everyone(self):
        return [self.twin()] + [self.along(axis, d)[0] for axis in "xyz" for d in (1, 2, 3)]


def send(src, dst, sems, i, device):
    copy = pltpu.make_async_remote_copy(
        src_ref=src, dst_ref=dst, send_sem=sems.at[0, i], recv_sem=sems.at[1, i],
        device_id=device, device_id_type=pl.DeviceIdType.MESH,
    )
    copy.start()
    return copy


def reduce_phase(me, g, phase, recv, sems, free):
    base, size = phase
    half, quarter, small = size // 2, size // 8, size // 32
    mine, others = base + me.core * half, base + (1 - me.core) * half
    copy = send(g.at[:, pl.ds(others, half), :], recv.core, sems, 0, me.twin())
    yield
    copy.wait()

    def release(i, devices):
        for device in devices:
            pl.semaphore_signal(free.at[i], inc=1, device_id=device, device_id_type=pl.DeviceIdType.MESH)

    around = [me.along(axis, d)[0] for axis in "xyz" for d in (1, 2, 3)]
    release(0, [me.twin()])
    for c in range(3):
        rows = pl.ds(mine, half)
        g[c, rows, :] = (g[c, rows, :].astype(f32) + recv.core[c].astype(f32)).astype(bf16)

    def scatter(start, rows, buf, first_sem, step):
        copies = []
        for d in (1, 2, 3):
            for c in range(3):
                to, index = me.along(ORDERS[c][step], d)
                copies.append(
                    send(
                        g.at[c, pl.ds(start[c] + index * rows, rows), :], buf.at[c, d - 1], sems,
                        first_sem + len(copies), to,
                    )
                )
        return copies

    def gather(start, rows, first_sem, step):
        copies = []
        for d in (1, 2, 3):
            for c in range(3):
                to, _ = me.along(ORDERS[c][step], d)
                block = g.at[c, pl.ds(start[c], rows), :]
                copies.append(send(block, block, sems, first_sem + len(copies), to))
        return copies

    def add(start, rows, buf):
        for c in range(3):
            own = pl.ds(start[c], rows)
            terms = g[c, own, :].astype(f32)
            for d in range(3):
                terms = terms + buf[c, d].astype(f32)
            g[c, own, :] = terms.astype(bf16)

    zero = [mine] * 3
    copies = scatter(zero, quarter, recv.one, 1, 0)
    yield
    for copy in copies:
        copy.wait()
    release(1, around)
    one = [mine + me.at[ORDERS[c][0]] * quarter for c in range(3)]
    add(one, quarter, recv.one)
    copies = scatter(one, small, recv.two, 10, 1)
    yield
    for copy in copies:
        copy.wait()
    release(2, around)
    two = [one[c] + me.at[ORDERS[c][1]] * small for c in range(3)]
    add(two, small, recv.two)
    copies = []
    for c in range(3):
        slot = me.at[ORDERS[c][2]]
        recv.three[c, slot] = g[c, pl.ds(two[c], small), :]
    for d in (1, 2, 3):
        for c in range(3):
            slot = me.at[ORDERS[c][2]]
            to, _ = me.along(ORDERS[c][2], d)
            block = recv.three.at[c, slot]
            copies.append(send(block, block, sems, 19 + len(copies), to))
    yield
    for copy in copies:
        copy.wait()
    for c in range(3):
        terms = recv.three[c, 0].astype(f32)
        for j in range(1, 4):
            terms = terms + recv.three[c, j].astype(f32)
        g[c, pl.ds(two[c], small), :] = terms.astype(bf16)
    pl.semaphore_wait(free.at[2], len(around))
    copies = gather(two, small, 28, 1)
    yield
    for copy in copies:
        copy.wait()
    pl.semaphore_wait(free.at[1], len(around))
    copies = gather(one, quarter, 37, 0)
    yield
    for copy in copies:
        copy.wait()
    pl.semaphore_wait(free.at[0], 1)
    block = g.at[:, pl.ds(mine, half), :]
    copy = send(block, block, sems, 46, me.twin())
    yield
    copy.wait()


def slot_kernel(names, *refs):
    r = Refs()
    for name, ref in zip(names, refs):
        setattr(r, name, ref)
    me = Where()
    first = me.side == 0
    loads = {}
    for i, (name, _) in enumerate(WEIGHTS):
        loads[name] = pltpu.make_async_copy(getattr(r, "h_" + name), getattr(r, name), r.loads.at[i])
        loads[name].start()
    barrier = pltpu.get_barrier_semaphore()
    friends = me.everyone()
    for device in friends:
        pl.semaphore_signal(barrier, inc=1, device_id=device, device_id_type=pl.DeviceIdType.MESH)
    pl.semaphore_wait(barrier, len(friends))
    swap = send(r.local.at[1 - me.side], r.arrived, r.swaps, 0, me.pair())

    source, label, live = unit_order([r.frames[0, me.side, me.core, c] for c in range(CLIPS)])
    fill_mask(r.mask, label)
    fill_order(r.order, source)
    enc, pred = Refs(), Refs()
    enc.vec = columns(r.eg[...], r.eb[...], r.exb[...])
    pred.vec = columns(r.pg[...], r.pb[...], r.pxb[...])
    enc.project, enc.merge, enc.expand, enc.reduce = r.ew, r.em, r.ex, r.er
    pred.project, pred.merge, pred.expand, pred.reduce = r.pw, r.pm, r.px, r.pr
    es, ps = Refs(), Refs()
    for name, _, _ in KEPT:
        setattr(es, name, getattr(r, "e_" + name))
        setattr(ps, name, getattr(r, "p_" + name))
    for name, _, _ in SHARED:
        setattr(es, name, getattr(r, name))
        setattr(ps, name, getattr(r, name))
    es.e, es.over, ps.e, ps.over = r.e_e, r.e_over, r.p_e, r.p_over

    swap.wait()
    x = jnp.where(first, r.local[0], r.arrived[...])
    r.stream[...] = dot(x, r.order[...], 0, 0)
    for copy in loads.values():
        copy.wait()

    block_forward(r.stream, r.stream2, enc, es, HEADS, r.mask)
    r.sent[...] = r.stream2[...].astype(bf16)
    r.stream[...] = dot(r.embed[...], r.sent[...], 0, 0) + r.embed_bias[...].astype(f32).reshape(1, F).T
    block_forward(r.stream, r.stream2, pred, ps, PHEADS, r.mask)

    alive = lax.broadcasted_iota(jnp.int32, (F, ROWS), 1) < live
    r.out[...] = dot(r.order[...], jnp.where(alive, r.stream2[...], 0.0).astype(bf16), 1, 1).astype(bf16)
    copy_out = pltpu.make_async_remote_copy(
        src_ref=r.sends, dst_ref=r.back, send_sem=r.swaps.at[0, 1], recv_sem=r.swaps.at[1, 1],
        device_id=me.pair(), device_id_type=pl.DeviceIdType.MESH,
    )

    @pl.when(first)
    def _():
        r.sends[...] = r.out[...]
        copy_out.start()

    cotangent = jnp.where(first, r.arrived[...], r.local[1])
    r.stream[...] = jnp.where(alive, dot(cotangent, r.order[...], 0, 0), 0.0)

    g = r.grads
    phases = []
    for i, phase in enumerate(PHASES):
        recv = Refs()
        for name in ("core", "one", "two", "three"):
            setattr(recv, name, getattr(r, f"{name}{i}"))
        phases.append(reduce_phase(me, g, phase, recv, r.sems.at[i], r.free.at[i]))

    ticks = iter(PLAN)

    def tick():
        for i in next(ticks):
            next(phases[i], None)

    sums = block_backward(r.stream, pred, ps, PHEADS, g, PRED_AT, tick)
    r.q[...] = r.stream[...].astype(bf16)
    de = r.q[...]
    place(g, PRED_AT["embed"], dot(r.sent[...], de, 1, 1))
    place_sums(g, PRED_AT["small"], sums + [total(de)])
    g[:, PRED_AT["end"] : ENC_AT["reduce"], :] = jnp.zeros((3, ENC_AT["reduce"] - PRED_AT["end"], 128), bf16)
    g[:, ENC_AT["gap"] : ENC_AT["project"], :] = jnp.zeros((3, ENC_AT["project"] - ENC_AT["gap"], 128), bf16)
    g[:, ENC_AT["end"] : TOTAL, :] = jnp.zeros((3, TOTAL - ENC_AT["end"], 128), bf16)
    r.stream[...] = dot(r.embed[...], de, 1, 0).astype(bf16).astype(f32)
    tick()
    sums = block_backward(r.stream, enc, es, HEADS, g, ENC_AT, tick)
    place_sums(g, ENC_AT["small"], sums)
    tick()
    dx = dot(r.order[...], r.stream[...].astype(bf16), 1, 1).astype(bf16)

    @pl.when(first)
    def _():
        r.kept[...] = dx

    @pl.when(jnp.logical_not(first))
    def _():
        r.kept[...] = r.out[...]
        r.sends[...] = dx
        copy_out.start()

    for i in TAIL:
        next(phases[i], None)
    copy_out.wait()


PLAN = (
    (0,), (), (), (), (0, 1,), (), (), (1,), (), (), (), (), (0,), (), (), (1, 2,), (3,), (0,), (2,), (), (3, 1,), (4,), (), (0,), (), (4,), (), (2, 5,),
)
TAIL = (3, 5, 1, 0, 4, 2, 3, 5, 1, 0, 4, 2, 3, 0, 5, 1, 4, 2, 3, 1, 5, 4, 2, 3, 5, 2, 3, 4, 4, 5, 5)


def slot_call(frames, local, weights):
    args = [("frames", frames), ("local", local)]
    big = {name for name, _ in WEIGHTS}
    order = ("eg", "eb", "ew", "em", "ex", "exb", "er", "embed", "embed_bias", "pg", "pb", "pw", "pm", "px", "pxb", "pr")
    specs = [pl.BlockSpec(memory_space=pltpu.SMEM), pl.BlockSpec(memory_space=pltpu.VMEM)]
    for name, weight in zip(order, weights):
        args.append(("h_" + name if name in big else name, weight))
        specs.append(pl.BlockSpec(memory_space=pl.ANY if name in big else pltpu.VMEM))
    outs = [("grads", (3, TOTAL, 128), bf16), ("kept", (ROWS, F), bf16), ("back", (ROWS, F), bf16)]
    scratch = [
        ("mask", (BLOCKS, BLOCK, BLOCK), f32), ("order", (ROWS, ROWS), bf16), ("out", (ROWS, F), bf16),
        ("stream", (F, ROWS), f32), ("stream2", (F, ROWS), f32), ("sent", (F, ROWS), bf16),
        ("arrived", (ROWS, F), bf16), ("sends", (ROWS, F), bf16),
        ("e_e", (HEADS, BLOCKS, BLOCK, BLOCK), bf16), ("p_e", (PHEADS, BLOCKS, BLOCK, BLOCK), bf16),
        ("e_over", (8, ROWS), f32), ("p_over", (16, ROWS), f32),
    ]
    scratch += [(n, sh, bf16) for n, sh in WEIGHTS]
    scratch += [("e_" + n, sh, d) for n, sh, d in KEPT] + [("p_" + n, sh, d) for n, sh, d in KEPT]
    scratch += list(SHARED)
    for i, (_, size) in enumerate(PHASES):
        scratch += [
            (f"core{i}", (3, size // 2, 128), bf16), (f"one{i}", (3, 3, size // 8, 128), bf16),
            (f"two{i}", (3, 3, size // 32, 128), bf16), (f"three{i}", (3, 4, size // 32, 128), bf16),
        ]
    sems = [("loads", (len(WEIGHTS),)), ("swaps", (2, 2)), ("sems", (len(PHASES), 2, 47))]
    names = [n for n, _ in args] + [n for n, _, _ in outs] + [n for n, _, _ in scratch] + [n for n, _ in sems] + ["free"]
    return pl.pallas_call(
        functools.partial(slot_kernel, names),
        out_shape=[pltpu.VMEM(sh, d) for _, sh, d in outs],
        in_specs=specs,
        out_specs=[pl.BlockSpec(memory_space=pltpu.VMEM)] * len(outs),
        scratch_shapes=[pltpu.VMEM(sh, d) for _, sh, d in scratch] + [pltpu.SemaphoreType.DMA(sh) for _, sh in sems]
        + [pltpu.SemaphoreType.REGULAR((len(PHASES), 3))],
        compiler_params=pltpu.CompilerParams(
            vmem_limit_bytes=52 * 2**20, collective_id=0, has_side_effects=True
        ),
    )(*[a for _, a in args])


LAYERS = (("pg", "pb", "pw", "pm", "px", "pxb", "pr"), ("eg", "eb", "ew", "em", "ex", "exb", "er"))
BIG = {"w": (F, 3 * F), "m": (F, F), "x": (F, FF), "r": (FF, F)}


def widen(g_ref, at, out_ref, rows, col):
    for c in range(3):
        out_ref[rows, col + c * 128 : col + c * 128 + 128] = g_ref[c, at : at + F, :].astype(f32)


def unpack_kernel(names, *refs):
    r = Refs()
    for name, ref in zip(names, refs):
        setattr(r, name, ref)
    copies = []

    def ship(src, dst):
        copy = pltpu.make_async_copy(src, dst, r.sems.at[len(copies)])
        copy.start()
        copies.append(copy)

    side = lax.axis_index("pipe") // 2
    r.wide[0] = r.kept[...].astype(f32)
    ship(r.wide.at[0], r.result.at[side])
    r.wide[1] = r.back[...].astype(f32)
    ship(r.wide.at[1], r.result.at[1 - side])
    g = r.grads
    for layer, at in (("p", PRED_AT), ("e", ENC_AT)):
        for part in range(4):
            rows = slice(part * F, part * F + F)
            widen(g, at["reduce"] + part * F, getattr(r, "s_" + layer + "r"), rows, 0)
        ship(getattr(r, "s_" + layer + "r"), getattr(r, layer + "r"))
        for part in range(4):
            widen(g, at["expand"] + part * F, getattr(r, "s_" + layer + "x"), slice(0, F), part * F)
        ship(getattr(r, "s_" + layer + "x"), getattr(r, layer + "x"))
        for part in range(3):
            widen(g, at["project"] + part * F, getattr(r, "s_" + layer + "w"), slice(0, F), part * F)
        ship(getattr(r, "s_" + layer + "w"), getattr(r, layer + "w"))
        widen(g, at["merge"], getattr(r, "s_" + layer + "m"), slice(0, F), 0)
        ship(getattr(r, "s_" + layer + "m"), getattr(r, layer + "m"))
        if layer == "p":
            widen(g, at["embed"], r.s_embed, slice(0, F), 0)
            ship(r.s_embed, r.embed)
        small = at["small"]
        rows = jnp.concatenate([g[c, small : small + 16, :] for c in range(3)], axis=1).astype(f32)
        getattr(r, layer + "g")[...] = rows[0:2]
        getattr(r, layer + "b")[...] = rows[2:8]
        for part in range(4):
            getattr(r, layer + "xb")[part * F : part * F + F] = rows[8 + part]
        if layer == "p":
            r.embed_bias[...] = rows[12]
    for copy in copies:
        copy.wait()


def unpack_call(grads, kept, back):
    big = [("embed", (F, F))] + [(layer + n, BIG[n]) for layer in "pe" for n in BIG]
    small = [("embed_bias", (F,))]
    for layer in "pe":
        small += [(layer + "g", (2, F)), (layer + "b", (6, F)), (layer + "xb", (FF,))]
    outs = [("result", (2, ROWS, F))] + big + small
    names = ["grads", "kept", "back"] + [n for n, _ in outs] + ["s_" + n for n, _ in big] + ["wide", "sems"]
    values = pl.pallas_call(
        functools.partial(unpack_kernel, names),
        out_shape=[jax.ShapeDtypeStruct(sh, f32) for _, sh in outs],
        in_specs=[pl.BlockSpec(memory_space=pltpu.VMEM)] * 3,
        out_specs=[pl.BlockSpec(memory_space=pl.ANY)] * (1 + len(big))
        + [pl.BlockSpec(memory_space=pltpu.VMEM)] * len(small),
        scratch_shapes=[pltpu.VMEM(sh, f32) for _, sh in big]
        + [pltpu.VMEM((2, ROWS, F), f32), pltpu.SemaphoreType.DMA((len(big) + 2,))],
        compiler_params=pltpu.CompilerParams(vmem_limit_bytes=24 * 2**20),
    )(*[pltpu.with_memory_space_constraint(v, pltpu.VMEM) for v in (grads, kept, back)])
    return dict(zip([n for n, _ in outs], values))


def body(segment_data, clip_frames, *weights):
    g = unpack_call(*slot_call(clip_frames, segment_data[0, 0], weights))
    order = ("eg", "eb", "ew", "em", "ex", "exb", "er", "embed", "embed_bias", "pg", "pb", "pw", "pm", "px", "pxb", "pr")
    return (g["result"][None, None],) + tuple(g[n] for n in order)


def solution(mesh):
    return jax.shard_map(
        body,
        mesh=mesh,
        in_specs=(P("pipe", "dp", None, None, None), P("dp", None, None, None)) + (P(),) * 16,
        out_specs=(P("pipe", "dp", None, None, None),) + (P(),) * 16,
        check_vma=False,
    )
```

```python
import functools
import math

import jax
import jax.numpy as jnp
from jax import lax
from jax.experimental import pallas as pl
from jax.experimental.pallas import tpu as pltpu
from jax.sharding import PartitionSpec as P

HEADS = 6
PHEADS = 12
CLIPS = 8
F = 384
FF = 1536
ROWS = 512
UNIT = 64
UNITS = ROWS // UNIT
BLOCK = 256
BLOCKS = ROWS // BLOCK
TOTAL = 10240
EPS = 1e-06
MASKED = -1e30

f32 = jnp.float32
bf16 = jnp.bfloat16


def dot(a, b, ca, cb):
    return lax.dot_general(a, b, (((ca,), (cb,)), ((), ())), preferred_element_type=f32)


def unit_order(frames):
    rows = [frames[c] * (UNIT // 8) for c in range(CLIPS)]
    start, place = [], []
    total = jnp.int32(0)
    for c in range(CLIPS):
        start.append(total)
        total = total + rows[c]
    for c in range(CLIPS):
        before = jnp.int32(0)
        for d in range(CLIPS):
            if d < c:
                ahead = rows[d] >= rows[c]
            elif d > c:
                ahead = rows[d] > rows[c]
            else:
                continue
            before = before + jnp.where(ahead, rows[d], 0)
        place.append(before)
    source, label = [], []
    for j in range(UNITS):
        at = j * UNIT
        src, lab = jnp.int32(at), jnp.int32(CLIPS + j)
        for c in range(CLIPS):
            held = (at >= place[c]) & (at < place[c] + rows[c])
            src = jnp.where(held, start[c] + at - place[c], src)
            lab = jnp.where(held, c, lab)
        source.append(src)
        label.append(lab)
    return source, label, total


def fill_order(order_ref, source):
    lane = lax.broadcasted_iota(jnp.int32, (1, ROWS), 1)
    row = spread(source, (1, ROWS), 1) + lane % UNIT
    at = lax.broadcasted_iota(jnp.int32, (ROWS, ROWS), 0)
    order_ref[...] = jnp.where(at == row, 1.0, 0.0).astype(bf16)


def spread(values, shape, axis):
    at = lax.broadcasted_iota(jnp.int32, shape, axis) // UNIT
    out = jnp.full(shape, values[0], jnp.int32)
    for i in range(1, len(values)):
        out = jnp.where(at == i, values[i], out)
    return out


def fill_mask(mask_ref, label):
    for b in range(BLOCKS):
        own = label[b * 4 : b * 4 + 4]
        down = spread(own, (BLOCK, BLOCK), 0)
        across = spread(own, (BLOCK, BLOCK), 1)
        mask_ref[b] = jnp.where(down == across, 0.0, MASKED).astype(f32)


def norm(v, gain, shift):
    mean = jnp.mean(v, axis=0, keepdims=True)
    centred = v - mean
    inverse = lax.rsqrt(jnp.mean(centred * centred, axis=0, keepdims=True) + EPS)
    normed = centred * inverse
    return normed * gain + shift, normed, inverse


def norm_back(k, normed, inverse):
    return inverse * (
        k
        - jnp.mean(k, axis=0, keepdims=True)
        - normed * jnp.mean(k * normed, axis=0, keepdims=True)
    )


def block_forward(stream_ref, out_ref, w, s, heads, mask_ref):
    size = F // heads
    scale = math.log2(math.e) / math.sqrt(size)
    vec = w.vec
    for t in range(ROWS // 128):
        cols = slice(t * 128, t * 128 + 128)
        full, normed, inverse = norm(stream_ref[:, cols], vec[:, 0:1], vec[:, 2:3])
        s.n1[:, cols] = normed
        s.i1[:, cols] = inverse
        s.a1[:, cols] = full.astype(bf16)
    for part in range(3):
        rows = slice(part * F, part * F + F)
        z = dot(w.project[:, rows], s.a1[...], 0, 0)
        if part == 0:
            z = z + vec[:, 3:4]
        if part == 2:
            z = z + vec[:, 4:5]
        s.z[rows, :] = z.astype(bf16)
    turns = [(h, b) for h in range(heads) for b in range(BLOCKS)]

    def place_of(h, b):
        return slice(h * size, h * size + size), slice(b * BLOCK, b * BLOCK + BLOCK)

    def score_of(h, b):
        own, cols = place_of(h, b)
        return dot(s.z[F + h * size : F + h * size + size, cols], s.z[own, cols], 0, 0)

    ahead = [score_of(*turn) for turn in turns[:3]]
    for i, (h, b) in enumerate(turns):
        own, cols = place_of(h, b)
        score = ahead.pop(0) * scale + mask_ref[b]
        if i + 3 < len(turns):
            ahead.append(score_of(*turns[i + 3]))
        e = jnp.exp2(score - jnp.max(score, axis=0, keepdims=True))
        over = 1.0 / jnp.sum(e, axis=0, keepdims=True)
        e = e.astype(bf16)
        s.e[h, b] = e
        s.over[h : h + 1, cols] = over
        v = s.z[2 * F + h * size : 2 * F + h * size + size, cols]
        s.o[own, cols] = (dot(v, e, 1, 0) * over).astype(bf16)
    middle = stream_ref[...] + (dot(w.merge[...], s.o[...], 0, 0) + vec[:, 5:6])
    s.m1[...] = middle
    for t in range(ROWS // 128):
        cols = slice(t * 128, t * 128 + 128)
        full, normed, inverse = norm(s.m1[:, cols], vec[:, 1:2], vec[:, 6:7])
        s.n2[:, cols] = normed
        s.i2[:, cols] = inverse
        s.a2[:, cols] = full.astype(bf16)
    for part in range(4):
        rows = slice(part * F, part * F + F)
        u = dot(w.expand[:, rows], s.a2[...], 0, 0) + vec[:, 8 + part : 9 + part]
        below = 0.5 * lax.erf(u * math.sqrt(0.5)) + 0.5
        density = jnp.exp2(u * u * (-0.5 * math.log2(math.e))) * (1.0 / math.sqrt(2.0 * math.pi))
        s.act[rows, :] = (u * below).astype(bf16)
        s.slope[rows, :] = (below + u * density).astype(bf16)
    out_ref[...] = s.m1[...] + (dot(w.reduce[...], s.act[...], 0, 0) + vec[:, 7:8])


def place(g_ref, at, value):
    for c in range(3):
        g_ref[c, at : at + value.shape[0], :] = value[:, c * 128 : c * 128 + 128].astype(bf16)


def total(x):
    return jnp.sum(x.astype(f32), axis=1, keepdims=True)


def block_backward(grad_ref, w, s, heads, g_ref, at, tick):
    size = F // heads
    vec = w.vec
    sums = [None] * 12
    s.q[...] = grad_ref[...].astype(bf16)
    q2 = s.q[...]
    sums[7] = total(q2)
    ahead = dot(w.reduce[0:F, :], q2, 1, 0)
    for part in range(4):
        rows = slice(part * F, part * F + F)
        grad_act = ahead
        if part < 3:
            ahead = dot(w.reduce[part * F + F : part * F + 2 * F, :], q2, 1, 0)
        du = (grad_act * s.slope[rows, :].astype(f32)).astype(bf16)
        s.du[rows, :] = du
        sums[8 + part] = total(du)
        place(g_ref, at["reduce"] + part * F, dot(s.act[rows, :], q2, 1, 1))
        tick()
    da = dot(w.expand[...], s.du[...], 1, 0)
    s.t[...] = da
    for t in range(ROWS // 128):
        cols = slice(t * 128, t * 128 + 128)
        grad_ref[:, cols] += norm_back(s.t[:, cols] * vec[:, 1:2], s.n2[:, cols], s.i2[:, cols])
        place(g_ref, at["expand"] + t * F, dot(s.a2[...], s.du[t * F : t * F + F, :], 1, 1))
    tick()
    sums[1] = total(s.t[...] * s.n2[...])
    sums[6] = total(s.t[...])
    s.q[...] = grad_ref[...].astype(bf16)
    q1 = s.q[...]
    sums[5] = total(q1)
    place(g_ref, at["merge"], dot(s.o[...], q1, 1, 1))
    s.t[...] = dot(w.merge[...], q1, 1, 0)
    tick()
    turns = [(h, b) for h in range(heads) for b in range(BLOCKS)]

    def slope_of(h, b):
        own, cols = slice(h * size, h * size + size), slice(b * BLOCK, b * BLOCK + BLOCK)
        do = (s.t[own, cols] * s.over[h : h + 1, cols]).astype(bf16)
        delta = jnp.sum(do.astype(f32) * s.o[own, cols].astype(f32), axis=0, keepdims=True)
        v = s.z[2 * F + h * size : 2 * F + h * size + size, cols]
        return do, delta, dot(v, do, 0, 0)

    ahead = [slope_of(*turn) for turn in turns[:2]]
    for i, (h, b) in enumerate(turns):
        cols = slice(b * BLOCK, b * BLOCK + BLOCK)
        lo = h * size
        q = s.z[lo : lo + size, cols]
        k = s.z[F + lo : F + lo + size, cols]
        do, delta, dp = ahead.pop(0)
        if i + 2 < len(turns):
            ahead.append(slope_of(*turns[i + 2]))
        e = s.e[h, b]
        ds = (dp - delta).astype(bf16) * e
        s.dz[2 * F + lo : 2 * F + lo + size, cols] = dot(do, e, 1, 1).astype(bf16)
        s.dz[lo : lo + size, cols] = (dot(k, ds, 1, 0) * (1.0 / math.sqrt(size))).astype(bf16)
        s.dz[F + lo : F + lo + size, cols] = (dot(q, ds, 1, 1) * (1.0 / math.sqrt(size))).astype(bf16)
        if i % 4 == 3:
            tick()
    sums[3] = total(s.dz[0:F, :])
    sums[4] = total(s.dz[2 * F : 3 * F, :])
    da = dot(w.project[...], s.dz[...], 1, 0)
    s.t[...] = da
    for t in range(ROWS // 128):
        cols = slice(t * 128, t * 128 + 128)
        grad_ref[:, cols] += norm_back(s.t[:, cols] * vec[:, 0:1], s.n1[:, cols], s.i1[:, cols])
        if t < 3:
            place(g_ref, at["project"] + t * F, dot(s.a1[...], s.dz[t * F : t * F + F, :], 1, 1))
    sums[0] = total(s.t[...] * s.n1[...])
    sums[2] = total(s.t[...])
    tick()
    return sums


def columns(gains, biases, hidden):
    rows = [gains.astype(f32), biases.astype(f32)]
    for part in range(4):
        rows.append(hidden[part * F : part * F + F].astype(f32).reshape(1, F))
    rows.append(jnp.zeros((4, F), f32))
    return jnp.concatenate(rows, axis=0).T


def place_sums(g_ref, at, sums):
    lane = lax.broadcasted_iota(jnp.int32, (F, 128), 1)
    table = jnp.zeros((F, 128), f32)
    for i, column in enumerate(sums):
        table = jnp.where(lane == i, column, table)
    place(g_ref, at, table.T[0:16, :])


class Refs:
    pass


KEPT = (
    ("n1", (F, ROWS), f32), ("i1", (1, ROWS), f32), ("a1", (F, ROWS), bf16), ("z", (3 * F, ROWS), bf16),
    ("o", (F, ROWS), bf16), ("m1", (F, ROWS), f32), ("n2", (F, ROWS), f32), ("i2", (1, ROWS), f32),
    ("a2", (F, ROWS), bf16), ("act", (FF, ROWS), bf16), ("slope", (FF, ROWS), bf16),
)
SHARED = (
    ("q", (F, ROWS), bf16), ("du", (FF, ROWS), bf16), ("t", (F, ROWS), f32), ("dz", (3 * F, ROWS), bf16),
)


PHASES = ((0, 1536), (1536, 1536), (3072, 2048), (5120, 1536), (6656, 2048), (8704, 1536))
PRED_AT = {"reduce": 0, "expand": 1536, "merge": 3072, "project": 3456, "embed": 4608, "small": 4992, "end": 5008}
ENC_AT = {"reduce": 5120, "expand": 6656, "merge": 8192, "gap": 8576, "project": 8704, "small": 9856, "end": 9872}
ORDERS = ("xyz", "yzx", "zxy")
WEIGHTS = (
    ("ew", (F, 3 * F)), ("em", (F, F)), ("ex", (F, FF)), ("er", (FF, F)), ("embed", (F, F)),
    ("pw", (F, 3 * F)), ("pm", (F, F)), ("px", (F, FF)), ("pr", (FF, F)),
)


class Where:
    def __init__(self):
        p, d = lax.axis_index("pipe"), lax.axis_index("dp")
        self.core, low = p % 2, p // 2
        self.at = {"x": d // 8, "y": d % 4, "z": ((d // 4) % 2) * 2 + low}
        self.side = low

    def device(self, core, at):
        return {"pipe": (at["z"] % 2) * 2 + core, "dp": at["x"] * 8 + (at["z"] // 2) * 4 + at["y"]}

    def twin(self):
        return self.device(1 - self.core, self.at)

    def along(self, axis, d):
        to = (self.at[axis] + d) % 4
        return self.device(self.core, {**self.at, axis: to}), to

    def pair(self):
        z = self.at["z"]
        return self.device(self.core, {**self.at, "z": z + 1 - 2 * (z % 2)})

    def everyone(self):
        return [self.twin()] + [self.along(axis, d)[0] for axis in "xyz" for d in (1, 2, 3)]


def send(src, dst, sems, i, device):
    copy = pltpu.make_async_remote_copy(
        src_ref=src, dst_ref=dst, send_sem=sems.at[0, i], recv_sem=sems.at[1, i],
        device_id=device, device_id_type=pl.DeviceIdType.MESH,
    )
    copy.start()
    return copy


def reduce_phase(me, g, phase, recv, sems, free):
    base, size = phase
    half, quarter, small = size // 2, size // 8, size // 32
    mine, others = base + me.core * half, base + (1 - me.core) * half
    copy = send(g.at[:, pl.ds(others, half), :], recv.core, sems, 0, me.twin())
    yield
    copy.wait()

    def release(i, devices):
        for device in devices:
            pl.semaphore_signal(free.at[i], inc=1, device_id=device, device_id_type=pl.DeviceIdType.MESH)

    around = [me.along(axis, d)[0] for axis in "xyz" for d in (1, 2, 3)]
    release(0, [me.twin()])
    for c in range(3):
        rows = pl.ds(mine, half)
        g[c, rows, :] = (g[c, rows, :].astype(f32) + recv.core[c].astype(f32)).astype(bf16)

    def scatter(start, rows, buf, first_sem, step):
        copies = []
        for d in (1, 2, 3):
            for c in range(3):
                to, index = me.along(ORDERS[c][step], d)
                copies.append(
                    send(
                        g.at[c, pl.ds(start[c] + index * rows, rows), :], buf.at[c, d - 1], sems,
                        first_sem + len(copies), to,
                    )
                )
        return copies

    def gather(start, rows, first_sem, step):
        copies = []
        for d in (1, 2, 3):
            for c in range(3):
                to, _ = me.along(ORDERS[c][step], d)
                block = g.at[c, pl.ds(start[c], rows), :]
                copies.append(send(block, block, sems, first_sem + len(copies), to))
        return copies

    def add(start, rows, buf):
        for c in range(3):
            own = pl.ds(start[c], rows)
            terms = g[c, own, :].astype(f32)
            for d in range(3):
                terms = terms + buf[c, d].astype(f32)
            g[c, own, :] = terms.astype(bf16)

    zero = [mine] * 3
    copies = scatter(zero, quarter, recv.one, 1, 0)
    yield
    for copy in copies:
        copy.wait()
    release(1, around)
    one = [mine + me.at[ORDERS[c][0]] * quarter for c in range(3)]
    add(one, quarter, recv.one)
    copies = scatter(one, small, recv.two, 10, 1)
    yield
    for copy in copies:
        copy.wait()
    release(2, around)
    two = [one[c] + me.at[ORDERS[c][1]] * small for c in range(3)]
    add(two, small, recv.two)
    copies = []
    for c in range(3):
        slot = me.at[ORDERS[c][2]]
        recv.three[c, slot] = g[c, pl.ds(two[c], small), :]
    for d in (1, 2, 3):
        for c in range(3):
            slot = me.at[ORDERS[c][2]]
            to, _ = me.along(ORDERS[c][2], d)
            block = recv.three.at[c, slot]
            copies.append(send(block, block, sems, 19 + len(copies), to))
    yield
    for copy in copies:
        copy.wait()
    for c in range(3):
        terms = recv.three[c, 0].astype(f32)
        for j in range(1, 4):
            terms = terms + recv.three[c, j].astype(f32)
        g[c, pl.ds(two[c], small), :] = terms.astype(bf16)
    pl.semaphore_wait(free.at[2], len(around))
    copies = gather(two, small, 28, 1)
    yield
    for copy in copies:
        copy.wait()
    pl.semaphore_wait(free.at[1], len(around))
    copies = gather(one, quarter, 37, 0)
    yield
    for copy in copies:
        copy.wait()
    pl.semaphore_wait(free.at[0], 1)
    block = g.at[:, pl.ds(mine, half), :]
    copy = send(block, block, sems, 46, me.twin())
    yield
    copy.wait()


def slot_kernel(names, *refs):
    r = Refs()
    for name, ref in zip(names, refs):
        setattr(r, name, ref)
    me = Where()
    first = me.side == 0
    loads = {}
    for i, (name, _) in enumerate(WEIGHTS):
        loads[name] = pltpu.make_async_copy(getattr(r, "h_" + name), getattr(r, name), r.loads.at[i])
        loads[name].start()
    barrier = pltpu.get_barrier_semaphore()
    friends = me.everyone()
    for device in friends:
        pl.semaphore_signal(barrier, inc=1, device_id=device, device_id_type=pl.DeviceIdType.MESH)
    pl.semaphore_wait(barrier, len(friends))
    swap = send(r.local.at[1 - me.side], r.arrived, r.swaps, 0, me.pair())

    source, label, live = unit_order([r.frames[0, me.side, me.core, c] for c in range(CLIPS)])
    fill_mask(r.mask, label)
    fill_order(r.order, source)
    enc, pred = Refs(), Refs()
    enc.vec = columns(r.eg[...], r.eb[...], r.exb[...])
    pred.vec = columns(r.pg[...], r.pb[...], r.pxb[...])
    enc.project, enc.merge, enc.expand, enc.reduce = r.ew, r.em, r.ex, r.er
    pred.project, pred.merge, pred.expand, pred.reduce = r.pw, r.pm, r.px, r.pr
    es, ps = Refs(), Refs()
    for name, _, _ in KEPT:
        setattr(es, name, getattr(r, "e_" + name))
        setattr(ps, name, getattr(r, "p_" + name))
    for name, _, _ in SHARED:
        setattr(es, name, getattr(r, name))
        setattr(ps, name, getattr(r, name))
    es.e, es.over, ps.e, ps.over = r.e_e, r.e_over, r.p_e, r.p_over

    swap.wait()
    x = jnp.where(first, r.local[0], r.arrived[...])
    r.stream[...] = dot(x, r.order[...], 0, 0)
    for copy in loads.values():
        copy.wait()

    block_forward(r.stream, r.stream2, enc, es, HEADS, r.mask)
    r.sent[...] = r.stream2[...].astype(bf16)
    r.stream[...] = dot(r.embed[...], r.sent[...], 0, 0) + r.embed_bias[...].astype(f32).reshape(1, F).T
    block_forward(r.stream, r.stream2, pred, ps, PHEADS, r.mask)

    alive = lax.broadcasted_iota(jnp.int32, (F, ROWS), 1) < live
    r.out[...] = dot(r.order[...], jnp.where(alive, r.stream2[...], 0.0).astype(bf16), 1, 1).astype(bf16)
    copy_out = pltpu.make_async_remote_copy(
        src_ref=r.sends, dst_ref=r.back, send_sem=r.swaps.at[0, 1], recv_sem=r.swaps.at[1, 1],
        device_id=me.pair(), device_id_type=pl.DeviceIdType.MESH,
    )

    @pl.when(first)
    def _():
        r.sends[...] = r.out[...]
        copy_out.start()

    cotangent = jnp.where(first, r.arrived[...], r.local[1])
    r.stream[...] = jnp.where(alive, dot(cotangent, r.order[...], 0, 0), 0.0)

    g = r.grads
    phases = []
    for i, phase in enumerate(PHASES):
        recv = Refs()
        for name in ("core", "one", "two", "three"):
            setattr(recv, name, getattr(r, f"{name}{i}"))
        phases.append(reduce_phase(me, g, phase, recv, r.sems.at[i], r.free.at[i]))

    ticks = iter(PLAN)

    def tick():
        for i in next(ticks):
            next(phases[i], None)

    sums = block_backward(r.stream, pred, ps, PHEADS, g, PRED_AT, tick)
    r.q[...] = r.stream[...].astype(bf16)
    de = r.q[...]
    place(g, PRED_AT["embed"], dot(r.sent[...], de, 1, 1))
    place_sums(g, PRED_AT["small"], sums + [total(de)])
    g[:, PRED_AT["end"] : ENC_AT["reduce"], :] = jnp.zeros((3, ENC_AT["reduce"] - PRED_AT["end"], 128), bf16)
    g[:, ENC_AT["gap"] : ENC_AT["project"], :] = jnp.zeros((3, ENC_AT["project"] - ENC_AT["gap"], 128), bf16)
    g[:, ENC_AT["end"] : TOTAL, :] = jnp.zeros((3, TOTAL - ENC_AT["end"], 128), bf16)
    r.stream[...] = dot(r.embed[...], de, 1, 0).astype(bf16).astype(f32)
    tick()
    sums = block_backward(r.stream, enc, es, HEADS, g, ENC_AT, tick)
    place_sums(g, ENC_AT["small"], sums)
    tick()
    dx = dot(r.order[...], r.stream[...].astype(bf16), 1, 1).astype(bf16)

    @pl.when(first)
    def _():
        r.kept[...] = dx

    @pl.when(jnp.logical_not(first))
    def _():
        r.kept[...] = r.out[...]
        r.sends[...] = dx

    for i in TAIL:
        if i is None:

            @pl.when(jnp.logical_not(first))
            def _():
                copy_out.start()

        else:
            next(phases[i], None)
    copy_out.wait()


PLAN = (
    (), (), (), (0,), (1,), (), (0,), (), (), (), (1,), (), (), (2,), (), (0,), (), (3,), (2, 1,), (4,), (3,), (0,), (), (4,), (5,),
)
TAIL = (2, 5, 1, 3, 0, 4, 2, 5, None, 1, 3, 0, 4, 2, 5, 1, 3, 0, 4, 2, 5, 0, 1, 3, 4, 1, 2, 5, 3, 2, 3, 4, 5, 4, 5)


def slot_call(frames, local, weights):
    args = [("frames", frames), ("local", local)]
    big = {name for name, _ in WEIGHTS}
    order = ("eg", "eb", "ew", "em", "ex", "exb", "er", "embed", "embed_bias", "pg", "pb", "pw", "pm", "px", "pxb", "pr")
    specs = [pl.BlockSpec(memory_space=pltpu.SMEM), pl.BlockSpec(memory_space=pltpu.VMEM)]
    for name, weight in zip(order, weights):
        args.append(("h_" + name if name in big else name, weight))
        specs.append(pl.BlockSpec(memory_space=pl.ANY if name in big else pltpu.VMEM))
    outs = [("grads", (3, TOTAL, 128), bf16), ("kept", (ROWS, F), bf16), ("back", (ROWS, F), bf16)]
    scratch = [
        ("mask", (BLOCKS, BLOCK, BLOCK), f32), ("order", (ROWS, ROWS), bf16), ("out", (ROWS, F), bf16),
        ("stream", (F, ROWS), f32), ("stream2", (F, ROWS), f32), ("sent", (F, ROWS), bf16),
        ("arrived", (ROWS, F), bf16), ("sends", (ROWS, F), bf16),
        ("e_e", (HEADS, BLOCKS, BLOCK, BLOCK), bf16), ("p_e", (PHEADS, BLOCKS, BLOCK, BLOCK), bf16),
        ("e_over", (8, ROWS), f32), ("p_over", (16, ROWS), f32),
    ]
    scratch += [(n, sh, bf16) for n, sh in WEIGHTS]
    scratch += [("e_" + n, sh, d) for n, sh, d in KEPT] + [("p_" + n, sh, d) for n, sh, d in KEPT]
    scratch += list(SHARED)
    for i, (_, size) in enumerate(PHASES):
        scratch += [
            (f"core{i}", (3, size // 2, 128), bf16), (f"one{i}", (3, 3, size // 8, 128), bf16),
            (f"two{i}", (3, 3, size // 32, 128), bf16), (f"three{i}", (3, 4, size // 32, 128), bf16),
        ]
    sems = [("loads", (len(WEIGHTS),)), ("swaps", (2, 2)), ("sems", (len(PHASES), 2, 47))]
    names = [n for n, _ in args] + [n for n, _, _ in outs] + [n for n, _, _ in scratch] + [n for n, _ in sems] + ["free"]
    return pl.pallas_call(
        functools.partial(slot_kernel, names),
        out_shape=[pltpu.VMEM(sh, d) for _, sh, d in outs],
        in_specs=specs,
        out_specs=[pl.BlockSpec(memory_space=pltpu.VMEM)] * len(outs),
        scratch_shapes=[pltpu.VMEM(sh, d) for _, sh, d in scratch] + [pltpu.SemaphoreType.DMA(sh) for _, sh in sems]
        + [pltpu.SemaphoreType.REGULAR((len(PHASES), 3))],
        compiler_params=pltpu.CompilerParams(
            vmem_limit_bytes=52 * 2**20, collective_id=0, has_side_effects=True
        ),
    )(*[a for _, a in args])


LAYERS = (("pg", "pb", "pw", "pm", "px", "pxb", "pr"), ("eg", "eb", "ew", "em", "ex", "exb", "er"))
BIG = {"w": (F, 3 * F), "m": (F, F), "x": (F, FF), "r": (FF, F)}


def widen(g_ref, at, out_ref, rows, col):
    for c in range(3):
        out_ref[rows, col + c * 128 : col + c * 128 + 128] = g_ref[c, at : at + F, :].astype(f32)


def unpack_kernel(names, *refs):
    r = Refs()
    for name, ref in zip(names, refs):
        setattr(r, name, ref)
    copies = []

    def ship(src, dst):
        copy = pltpu.make_async_copy(src, dst, r.sems.at[len(copies)])
        copy.start()
        copies.append(copy)

    side = lax.axis_index("pipe") // 2
    r.wide[0] = r.kept[...].astype(f32)
    ship(r.wide.at[0], r.result.at[side])
    r.wide[1] = r.back[...].astype(f32)
    ship(r.wide.at[1], r.result.at[1 - side])
    g = r.grads
    for layer, at in (("p", PRED_AT), ("e", ENC_AT)):
        for part in range(4):
            rows = slice(part * F, part * F + F)
            widen(g, at["reduce"] + part * F, getattr(r, "s_" + layer + "r"), rows, 0)
        ship(getattr(r, "s_" + layer + "r"), getattr(r, layer + "r"))
        for part in range(4):
            widen(g, at["expand"] + part * F, getattr(r, "s_" + layer + "x"), slice(0, F), part * F)
        ship(getattr(r, "s_" + layer + "x"), getattr(r, layer + "x"))
        for part in range(3):
            widen(g, at["project"] + part * F, getattr(r, "s_" + layer + "w"), slice(0, F), part * F)
        ship(getattr(r, "s_" + layer + "w"), getattr(r, layer + "w"))
        widen(g, at["merge"], getattr(r, "s_" + layer + "m"), slice(0, F), 0)
        ship(getattr(r, "s_" + layer + "m"), getattr(r, layer + "m"))
        if layer == "p":
            widen(g, at["embed"], r.s_embed, slice(0, F), 0)
            ship(r.s_embed, r.embed)
        small = at["small"]
        rows = jnp.concatenate([g[c, small : small + 16, :] for c in range(3)], axis=1).astype(f32)
        getattr(r, layer + "g")[...] = rows[0:2]
        getattr(r, layer + "b")[...] = rows[2:8]
        for part in range(4):
            getattr(r, layer + "xb")[part * F : part * F + F] = rows[8 + part]
        if layer == "p":
            r.embed_bias[...] = rows[12]
    for copy in copies:
        copy.wait()


def unpack_call(grads, kept, back):
    big = [("embed", (F, F))] + [(layer + n, BIG[n]) for layer in "pe" for n in BIG]
    small = [("embed_bias", (F,))]
    for layer in "pe":
        small += [(layer + "g", (2, F)), (layer + "b", (6, F)), (layer + "xb", (FF,))]
    outs = [("result", (2, ROWS, F))] + big + small
    names = ["grads", "kept", "back"] + [n for n, _ in outs] + ["s_" + n for n, _ in big] + ["wide", "sems"]
    values = pl.pallas_call(
        functools.partial(unpack_kernel, names),
        out_shape=[jax.ShapeDtypeStruct(sh, f32) for _, sh in outs],
        in_specs=[pl.BlockSpec(memory_space=pltpu.VMEM)] * 3,
        out_specs=[pl.BlockSpec(memory_space=pl.ANY)] * (1 + len(big))
        + [pl.BlockSpec(memory_space=pltpu.VMEM)] * len(small),
        scratch_shapes=[pltpu.VMEM(sh, f32) for _, sh in big]
        + [pltpu.VMEM((2, ROWS, F), f32), pltpu.SemaphoreType.DMA((len(big) + 2,))],
        compiler_params=pltpu.CompilerParams(vmem_limit_bytes=24 * 2**20),
    )(*[pltpu.with_memory_space_constraint(v, pltpu.VMEM) for v in (grads, kept, back)])
    return dict(zip([n for n, _ in outs], values))


def body(segment_data, clip_frames, *weights):
    g = unpack_call(*slot_call(clip_frames, segment_data[0, 0], weights))
    order = ("eg", "eb", "ew", "em", "ex", "exb", "er", "embed", "embed_bias", "pg", "pb", "pw", "pm", "px", "pxb", "pr")
    return (g["result"][None, None],) + tuple(g[n] for n in order)


def solution(mesh):
    return jax.shard_map(
        body,
        mesh=mesh,
        in_specs=(P("pipe", "dp", None, None, None), P("dp", None, None, None)) + (P(),) * 16,
        out_specs=(P("pipe", "dp", None, None, None),) + (P(),) * 16,
        check_vma=False,
    )
```

```python
import functools
import math

import jax
import jax.numpy as jnp
from jax import lax
from jax.experimental import pallas as pl
from jax.experimental.pallas import tpu as pltpu
from jax.sharding import PartitionSpec as P

HEADS = 6
PHEADS = 12
CLIPS = 8
F = 384
FF = 1536
ROWS = 512
UNIT = 64
UNITS = ROWS // UNIT
BLOCK = 256
BLOCKS = ROWS // BLOCK
TOTAL = 10240
EPS = 1e-06
MASKED = -1e30

f32 = jnp.float32
bf16 = jnp.bfloat16


def dot(a, b, ca, cb):
    return lax.dot_general(a, b, (((ca,), (cb,)), ((), ())), preferred_element_type=f32)


def unit_order(frames):
    rows = [frames[c] * (UNIT // 8) for c in range(CLIPS)]
    start, place = [], []
    total = jnp.int32(0)
    for c in range(CLIPS):
        start.append(total)
        total = total + rows[c]
    for c in range(CLIPS):
        before = jnp.int32(0)
        for d in range(CLIPS):
            if d < c:
                ahead = rows[d] >= rows[c]
            elif d > c:
                ahead = rows[d] > rows[c]
            else:
                continue
            before = before + jnp.where(ahead, rows[d], 0)
        place.append(before)
    source, label = [], []
    for j in range(UNITS):
        at = j * UNIT
        src, lab = jnp.int32(at), jnp.int32(CLIPS + j)
        for c in range(CLIPS):
            held = (at >= place[c]) & (at < place[c] + rows[c])
            src = jnp.where(held, start[c] + at - place[c], src)
            lab = jnp.where(held, c, lab)
        source.append(src)
        label.append(lab)
    return source, label, total


def fill_order(order_ref, source):
    lane = lax.broadcasted_iota(jnp.int32, (1, ROWS), 1)
    row = spread(source, (1, ROWS), 1) + lane % UNIT
    at = lax.broadcasted_iota(jnp.int32, (ROWS, ROWS), 0)
    order_ref[...] = jnp.where(at == row, 1.0, 0.0).astype(bf16)


def spread(values, shape, axis):
    at = lax.broadcasted_iota(jnp.int32, shape, axis) // UNIT
    out = jnp.full(shape, values[0], jnp.int32)
    for i in range(1, len(values)):
        out = jnp.where(at == i, values[i], out)
    return out


def fill_mask(mask_ref, label):
    for b in range(BLOCKS):
        own = label[b * 4 : b * 4 + 4]
        down = spread(own, (BLOCK, BLOCK), 0)
        across = spread(own, (BLOCK, BLOCK), 1)
        mask_ref[b] = jnp.where(down == across, 0.0, MASKED).astype(f32)


def norm(v, gain, shift):
    mean = jnp.mean(v, axis=0, keepdims=True)
    centred = v - mean
    inverse = lax.rsqrt(jnp.mean(centred * centred, axis=0, keepdims=True) + EPS)
    normed = centred * inverse
    return normed * gain + shift, normed, inverse


def norm_back(k, normed, inverse):
    return inverse * (
        k
        - jnp.mean(k, axis=0, keepdims=True)
        - normed * jnp.mean(k * normed, axis=0, keepdims=True)
    )


def block_forward(stream_ref, out_ref, w, s, heads, mask_ref):
    size = F // heads
    scale = math.log2(math.e) / math.sqrt(size)
    vec = w.vec
    for t in range(ROWS // 128):
        cols = slice(t * 128, t * 128 + 128)
        full, normed, inverse = norm(stream_ref[:, cols], vec[:, 0:1], vec[:, 2:3])
        s.n1[:, cols] = normed
        s.i1[:, cols] = inverse
        s.a1[:, cols] = full.astype(bf16)
    for part in range(3):
        rows = slice(part * F, part * F + F)
        z = dot(w.project[:, rows], s.a1[...], 0, 0)
        if part == 0:
            z = z + vec[:, 3:4]
        if part == 2:
            z = z + vec[:, 4:5]
        s.z[rows, :] = z.astype(bf16)
    turns = [(h, b) for h in range(heads) for b in range(BLOCKS)]

    def place_of(h, b):
        return slice(h * size, h * size + size), slice(b * BLOCK, b * BLOCK + BLOCK)

    def score_of(h, b):
        own, cols = place_of(h, b)
        return dot(s.z[F + h * size : F + h * size + size, cols], s.z[own, cols], 0, 0)

    ahead = [score_of(*turn) for turn in turns[:3]]
    for i, (h, b) in enumerate(turns):
        own, cols = place_of(h, b)
        score = ahead.pop(0) * scale + mask_ref[b]
        if i + 3 < len(turns):
            ahead.append(score_of(*turns[i + 3]))
        e = jnp.exp2(score - jnp.max(score, axis=0, keepdims=True))
        over = 1.0 / jnp.sum(e, axis=0, keepdims=True)
        e = e.astype(bf16)
        s.e[h, b] = e
        s.over[h : h + 1, cols] = over
        v = s.z[2 * F + h * size : 2 * F + h * size + size, cols]
        s.o[own, cols] = (dot(v, e, 1, 0) * over).astype(bf16)
    middle = stream_ref[...] + (dot(w.merge[...], s.o[...], 0, 0) + vec[:, 5:6])
    s.m1[...] = middle
    for t in range(ROWS // 128):
        cols = slice(t * 128, t * 128 + 128)
        full, normed, inverse = norm(s.m1[:, cols], vec[:, 1:2], vec[:, 6:7])
        s.n2[:, cols] = normed
        s.i2[:, cols] = inverse
        s.a2[:, cols] = full.astype(bf16)
    for part in range(4):
        rows = slice(part * F, part * F + F)
        u = dot(w.expand[:, rows], s.a2[...], 0, 0) + vec[:, 8 + part : 9 + part]
        below = 0.5 * lax.erf(u * math.sqrt(0.5)) + 0.5
        density = jnp.exp2(u * u * (-0.5 * math.log2(math.e))) * (1.0 / math.sqrt(2.0 * math.pi))
        s.act[rows, :] = (u * below).astype(bf16)
        s.slope[rows, :] = (below + u * density).astype(bf16)
    out_ref[...] = s.m1[...] + (dot(w.reduce[...], s.act[...], 0, 0) + vec[:, 7:8])


def place(g_ref, at, value):
    for c in range(3):
        g_ref[c, at : at + value.shape[0], :] = value[:, c * 128 : c * 128 + 128].astype(bf16)


def total(x):
    return jnp.sum(x.astype(f32), axis=1, keepdims=True)


def block_backward(grad_ref, w, s, heads, g_ref, at, tick):
    size = F // heads
    vec = w.vec
    sums = [None] * 12
    s.q[...] = grad_ref[...].astype(bf16)
    q2 = s.q[...]
    sums[7] = total(q2)
    ahead = dot(w.reduce[0:F, :], q2, 1, 0)
    for part in range(4):
        rows = slice(part * F, part * F + F)
        grad_act = ahead
        if part < 3:
            ahead = dot(w.reduce[part * F + F : part * F + 2 * F, :], q2, 1, 0)
        du = (grad_act * s.slope[rows, :].astype(f32)).astype(bf16)
        s.du[rows, :] = du
        sums[8 + part] = total(du)
        place(g_ref, at["reduce"] + part * F, dot(s.act[rows, :], q2, 1, 1))
        tick()
    da = dot(w.expand[...], s.du[...], 1, 0)
    s.t[...] = da
    for t in range(ROWS // 128):
        cols = slice(t * 128, t * 128 + 128)
        grad_ref[:, cols] += norm_back(s.t[:, cols] * vec[:, 1:2], s.n2[:, cols], s.i2[:, cols])
        place(g_ref, at["expand"] + t * F, dot(s.a2[...], s.du[t * F : t * F + F, :], 1, 1))
    tick()
    sums[1] = total(s.t[...] * s.n2[...])
    sums[6] = total(s.t[...])
    s.q[...] = grad_ref[...].astype(bf16)
    q1 = s.q[...]
    sums[5] = total(q1)
    place(g_ref, at["merge"], dot(s.o[...], q1, 1, 1))
    s.t[...] = dot(w.merge[...], q1, 1, 0)
    tick()
    turns = [(h, b) for h in range(heads) for b in range(BLOCKS)]

    def slope_of(h, b):
        own, cols = slice(h * size, h * size + size), slice(b * BLOCK, b * BLOCK + BLOCK)
        do = (s.t[own, cols] * s.over[h : h + 1, cols]).astype(bf16)
        delta = jnp.sum(do.astype(f32) * s.o[own, cols].astype(f32), axis=0, keepdims=True)
        v = s.z[2 * F + h * size : 2 * F + h * size + size, cols]
        return do, delta, dot(v, do, 0, 0)

    ahead = [slope_of(*turn) for turn in turns[:2]]
    for i, (h, b) in enumerate(turns):
        cols = slice(b * BLOCK, b * BLOCK + BLOCK)
        lo = h * size
        q = s.z[lo : lo + size, cols]
        k = s.z[F + lo : F + lo + size, cols]
        do, delta, dp = ahead.pop(0)
        if i + 2 < len(turns):
            ahead.append(slope_of(*turns[i + 2]))
        e = s.e[h, b]
        ds = (dp - delta).astype(bf16) * e
        s.dz[2 * F + lo : 2 * F + lo + size, cols] = dot(do, e, 1, 1).astype(bf16)
        s.dz[lo : lo + size, cols] = (dot(k, ds, 1, 0) * (1.0 / math.sqrt(size))).astype(bf16)
        s.dz[F + lo : F + lo + size, cols] = (dot(q, ds, 1, 1) * (1.0 / math.sqrt(size))).astype(bf16)
        if i % 4 == 3:
            tick()
    sums[3] = total(s.dz[0:F, :])
    sums[4] = total(s.dz[2 * F : 3 * F, :])
    da = dot(w.project[...], s.dz[...], 1, 0)
    s.t[...] = da
    for t in range(ROWS // 128):
        cols = slice(t * 128, t * 128 + 128)
        grad_ref[:, cols] += norm_back(s.t[:, cols] * vec[:, 0:1], s.n1[:, cols], s.i1[:, cols])
        if t < 3:
            place(g_ref, at["project"] + t * F, dot(s.a1[...], s.dz[t * F : t * F + F, :], 1, 1))
    sums[0] = total(s.t[...] * s.n1[...])
    sums[2] = total(s.t[...])
    tick()
    return sums


def columns(gains, biases, hidden):
    rows = [gains.astype(f32), biases.astype(f32)]
    for part in range(4):
        rows.append(hidden[part * F : part * F + F].astype(f32).reshape(1, F))
    rows.append(jnp.zeros((4, F), f32))
    return jnp.concatenate(rows, axis=0).T


def place_sums(g_ref, at, sums):
    lane = lax.broadcasted_iota(jnp.int32, (F, 128), 1)
    table = jnp.zeros((F, 128), f32)
    for i, column in enumerate(sums):
        table = jnp.where(lane == i, column, table)
    place(g_ref, at, table.T[0:16, :])


class Refs:
    pass


KEPT = (
    ("n1", (F, ROWS), f32), ("i1", (1, ROWS), f32), ("a1", (F, ROWS), bf16), ("z", (3 * F, ROWS), bf16),
    ("o", (F, ROWS), bf16), ("m1", (F, ROWS), f32), ("n2", (F, ROWS), f32), ("i2", (1, ROWS), f32),
    ("a2", (F, ROWS), bf16), ("act", (FF, ROWS), bf16), ("slope", (FF, ROWS), bf16),
)
SHARED = (
    ("q", (F, ROWS), bf16), ("du", (FF, ROWS), bf16), ("t", (F, ROWS), f32), ("dz", (3 * F, ROWS), bf16),
)


PHASES = ((0, 3072, True, False), (3072, 2048, True, False), (5120, 1536, False, False), (6656, 2048, False, False), (8704, 1536, False, False))
PRED_AT = {"reduce": 0, "expand": 1536, "merge": 3072, "project": 3456, "embed": 4608, "small": 4992, "end": 5008}
ENC_AT = {"reduce": 5120, "expand": 6656, "merge": 8192, "gap": 8576, "project": 8704, "small": 9856, "end": 9872}
ORDERS = ("xyz", "yzx", "zxy")
WEIGHTS = (
    ("ew", (F, 3 * F)), ("em", (F, F)), ("ex", (F, FF)), ("er", (FF, F)), ("embed", (F, F)),
    ("pw", (F, 3 * F)), ("pm", (F, F)), ("px", (F, FF)), ("pr", (FF, F)),
)


class Where:
    def __init__(self):
        p, d = lax.axis_index("pipe"), lax.axis_index("dp")
        self.core, low = p % 2, p // 2
        self.at = {"x": d // 8, "y": d % 4, "z": ((d // 4) % 2) * 2 + low}
        self.side = low
        self.turn = {axis: [(self.at[axis] + k) % 4 for k in range(4)] for axis in "xyz"}
        self.near = {
            axis: [self.device(self.core, {**self.at, axis: self.turn[axis][k]}) for k in range(4)] for axis in "xyz"
        }
        self.twin = self.device(1 - self.core, self.at)
        z = self.at["z"]
        home = z + 1 - 2 * (z % 2)
        mate = home + self.core * (3 - z - home)
        self.out = self.device(self.core, {**self.at, "z": mate + self.side * (home - mate)})
        self.back = self.device(self.core, {**self.at, "z": home + self.side * (mate - home)})
        self.far = self.near["z"][2]

    def device(self, core, at):
        return {"pipe": (at["z"] % 2) * 2 + core, "dp": at["x"] * 8 + (at["z"] // 2) * 4 + at["y"]}

    def around(self, steps):
        return [self.near[axis][d] for axis in "xyz" for d in steps]


def send(src, dst, sems, i, device):
    copy = pltpu.make_async_remote_copy(
        src_ref=src, dst_ref=dst, send_sem=sems.at[0, i], recv_sem=sems.at[1, i],
        device_id=device, device_id_type=pl.DeviceIdType.MESH,
    )
    copy.start()
    return copy


def phase_buffers(size, relay, wide):
    quarter, small = size // 8, size // 32
    full = quarter if wide else small
    shapes = [("core", (3, size // 2, 128)), ("three", (3, 4, full, 128))]
    if relay:
        shapes += [("one", (3, 2, quarter // 2, 128)), ("two", (3, 2, quarter, 128))]
    else:
        shapes += [("one", (3, 3, quarter, 128))]
    shapes += [("wide", (3, 4, quarter, 128)) if wide else ("small", (3, 3, small, 128))]
    return shapes


def reduce_phase(me, g, phase, recv, sems, free):
    base, size, relay, wide = phase
    half, quarter, small = size // 2, size // 8, size // 32
    mine, others = base + me.core * half, base + (1 - me.core) * half
    step = [0]

    def go(src, dst, device):
        send(src, dst, sems, step[0], device)

    def wait(all_of_it):
        pltpu.make_async_remote_copy(
            src_ref=all_of_it, dst_ref=all_of_it, send_sem=sems.at[0, step[0]], recv_sem=sems.at[1, step[0]],
            device_id=me.twin, device_id_type=pl.DeviceIdType.MESH,
        ).wait()
        step[0] += 1

    def rows_of(c, start, count):
        return g.at[c, pl.ds(start, count), :]

    def release(i, devices):
        for device in devices:
            pl.semaphore_signal(free.at[i], inc=1, device_id=device, device_id_type=pl.DeviceIdType.MESH)

    def add(c, start, count, terms):
        own = pl.ds(start, count)
        value = g[c, own, :].astype(f32)
        for term in terms:
            value = value + term.astype(f32)
        g[c, own, :] = value.astype(bf16)

    def exchange(starts, rows, buf, turn):
        for c in range(3):
            buf[c, me.at[ORDERS[c][turn]]] = g[c, pl.ds(starts[c], rows), :]
        for d in (2, 1, 3):
            for c in range(3):
                block = buf.at[c, me.at[ORDERS[c][turn]]]
                go(block, block, me.near[ORDERS[c][turn]][d])

    def total_of(starts, rows, buf):
        for c in range(3):
            value = buf[c, 0].astype(f32)
            for j in range(1, 4):
                value = value + buf[c, j].astype(f32)
            g[c, pl.ds(starts[c], rows), :] = value.astype(bf16)

    go(g.at[:, pl.ds(others, half), :], recv.core, me.twin)
    yield
    wait(recv.core)
    release(0, [me.twin])
    for c in range(3):
        add(c, mine, half, [recv.core[c]])

    axes = [order[0] for order in ORDERS]
    chunk = [[mine + me.turn[axes[c]][k] * quarter for k in range(4)] for c in range(3)]
    one = [chunk[c][0] for c in range(3)]
    if relay:
        part = quarter // 2
        for c in range(3):
            go(rows_of(c, chunk[c][2], part), recv.one.at[c, 0], me.near[axes[c]][1])
            go(rows_of(c, chunk[c][2] + part, part), recv.one.at[c, 1], me.near[axes[c]][3])
        yield
        wait(recv.one)
        for c in range(3):
            add(c, chunk[c][1], part, [recv.one[c, 0]])
            add(c, chunk[c][3] + part, part, [recv.one[c, 1]])
            go(rows_of(c, chunk[c][1], quarter), recv.two.at[c, 0], me.near[axes[c]][1])
            go(rows_of(c, chunk[c][3], quarter), recv.two.at[c, 1], me.near[axes[c]][3])
        yield
        wait(recv.two)
        for c in range(3):
            add(c, one[c], quarter, [recv.two[c, 0], recv.two[c, 1]])
    else:
        for d in (2, 1, 3):
            for c in range(3):
                go(rows_of(c, chunk[c][d], quarter), recv.one.at[c, d - 1], me.near[axes[c]][d])
        yield
        wait(recv.one)
        for c in range(3):
            add(c, one[c], quarter, [recv.one[c, d] for d in range(3)])

    if wide:
        release(1, me.around((1, 2, 3)))
        exchange(one, quarter, recv.wide, 1)
        yield
        wait(recv.wide.at[:, 0:3])
        total_of(one, quarter, recv.wide)
        exchange(one, quarter, recv.three, 2)
        yield
        wait(recv.three.at[:, 0:3])
        total_of(one, quarter, recv.three)
    else:
        axes2 = [order[1] for order in ORDERS]
        two = [one[c] + me.at[axes2[c]] * small for c in range(3)]
        for d in (2, 1, 3):
            for c in range(3):
                block = rows_of(c, one[c] + me.turn[axes2[c]][d] * small, small)
                go(block, recv.small.at[c, d - 1], me.near[axes2[c]][d])
        yield
        wait(recv.small)
        release(1, me.around((1, 2, 3)))
        for c in range(3):
            add(c, two[c], small, [recv.small[c, d] for d in range(3)])
        exchange(two, small, recv.three, 2)
        yield
        wait(recv.three.at[:, 0:3])
        total_of(two, small, recv.three)
        pl.semaphore_wait(free.at[1], 9)
        for d in (2, 1, 3):
            for c in range(3):
                block = rows_of(c, two[c], small)
                go(block, block, me.near[axes2[c]][d])
        yield
        wait(recv.small)

    if wide:
        pl.semaphore_wait(free.at[1], 9)
    for d in (1, 3) if relay else (2, 1, 3):
        for c in range(3):
            block = rows_of(c, one[c], quarter)
            go(block, block, me.near[axes[c]][d])
    yield
    wait(recv.two if relay else recv.one)
    if relay:
        for c in range(3):
            block = rows_of(c, chunk[c][3], part)
            go(block, block, me.near[axes[c]][1])
            block = rows_of(c, chunk[c][1] + part, part)
            go(block, block, me.near[axes[c]][3])
        yield
        wait(recv.one)
    pl.semaphore_wait(free.at[0], 1)
    block = g.at[:, pl.ds(mine, half), :]
    go(block, block, me.twin)
    yield
    wait(recv.core)


def slot_kernel(names, *refs):
    r = Refs()
    for name, ref in zip(names, refs):
        setattr(r, name, ref)
    me = Where()
    first = me.side == 0
    loads = {}
    for i, (name, _) in enumerate(WEIGHTS):
        loads[name] = pltpu.make_async_copy(getattr(r, "h_" + name), getattr(r, name), r.loads.at[i])
        loads[name].start()
    barrier = pltpu.get_barrier_semaphore()
    friends = [me.twin] + me.around((1, 2, 3))
    for device in friends:
        pl.semaphore_signal(barrier, inc=1, device_id=device, device_id_type=pl.DeviceIdType.MESH)
    lane = lax.broadcasted_iota(jnp.int32, (8, 128), 1)
    counts = jnp.zeros((8, 128), jnp.int32)
    for c in range(CLIPS):
        counts = jnp.where(lane == c, r.frames[0, 1, me.core, c], counts)
    r.counts[...] = counts
    pl.semaphore_wait(barrier, len(friends))
    told = send(r.counts, r.far_counts, r.swaps, 4, me.far)
    swap = send(r.local.at[1 - me.side], r.arrived, r.swaps, 0, me.out)
    away = me.side * me.core == 1
    lookup = pltpu.make_async_copy(r.far_counts, r.scalars, r.loads.at[len(WEIGHTS)])

    @pl.when(away)
    def _():
        told.wait_recv()
        lookup.start()
        lookup.wait()

    @pl.when(jnp.logical_not(away))
    def _():
        for c in range(CLIPS):
            r.scalars[0, c] = r.frames[0, me.side, me.core, c]

    source, label, live = unit_order([r.scalars[0, c] for c in range(CLIPS)])
    fill_mask(r.mask, label)
    fill_order(r.order, source)
    enc, pred = Refs(), Refs()
    enc.vec = columns(r.eg[...], r.eb[...], r.exb[...])
    pred.vec = columns(r.pg[...], r.pb[...], r.pxb[...])
    enc.project, enc.merge, enc.expand, enc.reduce = r.ew, r.em, r.ex, r.er
    pred.project, pred.merge, pred.expand, pred.reduce = r.pw, r.pm, r.px, r.pr
    es, ps = Refs(), Refs()
    for name, _, _ in KEPT:
        setattr(es, name, getattr(r, "e_" + name))
        setattr(ps, name, getattr(r, "p_" + name))
    for name, _, _ in SHARED:
        setattr(es, name, getattr(r, name))
        setattr(ps, name, getattr(r, name))
    es.e, es.over, ps.e, ps.over = r.e_e, r.e_over, r.p_e, r.p_over


    @pl.when(jnp.logical_not(first))
    def _():
        swap.wait_recv()

    far_rows = pltpu.make_async_remote_copy(
        src_ref=r.local.at[1], dst_ref=r.cotangent, send_sem=r.swaps.at[0, 2], recv_sem=r.swaps.at[1, 2],
        device_id=me.far, device_id_type=pl.DeviceIdType.MESH,
    )

    @pl.when(away)
    def _():
        far_rows.start()

    @pl.when(first)
    def _():
        r.x[...] = r.local[0]

    @pl.when(jnp.logical_not(first))
    def _():
        r.x[...] = r.arrived[...]

    r.stream[...] = dot(r.x[...], r.order[...], 0, 0)
    for copy in loads.values():
        copy.wait()

    block_forward(r.stream, r.stream2, enc, es, HEADS, r.mask)
    r.sent[...] = r.stream2[...].astype(bf16)
    r.stream[...] = dot(r.embed[...], r.sent[...], 0, 0) + r.embed_bias[...].astype(f32).reshape(1, F).T
    block_forward(r.stream, r.stream2, pred, ps, PHEADS, r.mask)

    alive = lax.broadcasted_iota(jnp.int32, (F, ROWS), 1) < live
    r.out[...] = dot(r.order[...], jnp.where(alive, r.stream2[...], 0.0).astype(bf16), 1, 1).astype(bf16)
    copy_out = pltpu.make_async_remote_copy(
        src_ref=r.sends, dst_ref=r.back, send_sem=r.swaps.at[0, 1], recv_sem=r.swaps.at[1, 1],
        device_id=me.back, device_id_type=pl.DeviceIdType.MESH,
    )
    far_out = pltpu.make_async_remote_copy(
        src_ref=r.out, dst_ref=r.kept, send_sem=r.swaps.at[0, 3], recv_sem=r.swaps.at[1, 3],
        device_id=me.far, device_id_type=pl.DeviceIdType.MESH,
    )

    @pl.when(first)
    def _():
        r.sends[...] = r.out[...]
        copy_out.start()
        swap.wait_recv()
        r.cotangent[...] = r.arrived[...]

    @pl.when(away)
    def _():
        far_out.start()
        far_rows.wait()

    @pl.when(me.side * (1 - me.core) == 1)
    def _():
        r.cotangent[...] = r.local[1]
        r.kept[...] = r.out[...]

    swap.wait_send()
    told.wait_send()

    @pl.when(jnp.logical_not(away))
    def _():
        told.wait_recv()

    cotangent = r.cotangent[...]
    r.stream[...] = jnp.where(alive, dot(cotangent, r.order[...], 0, 0), 0.0)

    g = r.grads
    phases = []
    for i, phase in enumerate(PHASES):
        recv = Refs()
        for name, _ in phase_buffers(*phase[1:]):
            setattr(recv, name, getattr(r, f"{name}{i}"))
        phases.append(reduce_phase(me, g, phase, recv, r.sems.at[i], r.free.at[i]))

    ticks = iter(PLAN)

    def tick():
        for i in next(ticks):
            next(phases[i], None)

    sums = block_backward(r.stream, pred, ps, PHEADS, g, PRED_AT, tick)
    r.q[...] = r.stream[...].astype(bf16)
    de = r.q[...]
    place(g, PRED_AT["embed"], dot(r.sent[...], de, 1, 1))
    place_sums(g, PRED_AT["small"], sums + [total(de)])
    g[:, PRED_AT["end"] : ENC_AT["reduce"], :] = jnp.zeros((3, ENC_AT["reduce"] - PRED_AT["end"], 128), bf16)
    g[:, ENC_AT["gap"] : ENC_AT["project"], :] = jnp.zeros((3, ENC_AT["project"] - ENC_AT["gap"], 128), bf16)
    g[:, ENC_AT["end"] : TOTAL, :] = jnp.zeros((3, TOTAL - ENC_AT["end"], 128), bf16)
    r.stream[...] = dot(r.embed[...], de, 1, 0).astype(bf16).astype(f32)
    tick()
    sums = block_backward(r.stream, enc, es, HEADS, g, ENC_AT, tick)
    place_sums(g, ENC_AT["small"], sums)
    tick()
    dx = dot(r.order[...], r.stream[...].astype(bf16), 1, 1).astype(bf16)

    @pl.when(first)
    def _():
        r.kept[...] = dx

    @pl.when(jnp.logical_not(first))
    def _():
        r.sends[...] = dx

    for i in TAIL:
        if i is None:

            @pl.when(jnp.logical_not(first))
            def _():
                copy_out.start()

        else:
            next(phases[i], None)
    copy_out.wait()

    @pl.when(away)
    def _():
        far_out.wait()


PLAN = (
    (), (), (), (), (0,), (), (), (), (), (), (), (), (0,), (1,), (), (), (), (1, 0, 2,), (), (1, 2, 3,), (0,), (), (), (3, 1,), (4,),
)
TAIL = (2, 0, 4, 3, 1, 2, 0, 4, 3, 1, 2, 0, 4, 3, 1, 2, 0, 4, 3, 1, 2, 0, 4, None, 2, 3, 1, 0, 4, 3, 1, 4)


def slot_call(frames, local, weights):
    args = [("frames", frames), ("local", local)]
    big = {name for name, _ in WEIGHTS}
    order = ("eg", "eb", "ew", "em", "ex", "exb", "er", "embed", "embed_bias", "pg", "pb", "pw", "pm", "px", "pxb", "pr")
    specs = [pl.BlockSpec(memory_space=pltpu.SMEM), pl.BlockSpec(memory_space=pltpu.VMEM)]
    for name, weight in zip(order, weights):
        args.append(("h_" + name if name in big else name, weight))
        specs.append(pl.BlockSpec(memory_space=pl.ANY if name in big else pltpu.VMEM))
    outs = [("grads", (3, TOTAL, 128), bf16), ("kept", (ROWS, F), bf16), ("back", (ROWS, F), bf16)]
    scratch = [
        ("mask", (BLOCKS, BLOCK, BLOCK), f32), ("order", (ROWS, ROWS), bf16), ("out", (ROWS, F), bf16),
        ("stream", (F, ROWS), f32), ("stream2", (F, ROWS), f32), ("sent", (F, ROWS), bf16),
        ("arrived", (ROWS, F), bf16), ("cotangent", (ROWS, F), bf16), ("x", (ROWS, F), bf16),
        ("counts", (8, 128), jnp.int32), ("far_counts", (8, 128), jnp.int32), ("sends", (ROWS, F), bf16),
        ("e_e", (HEADS, BLOCKS, BLOCK, BLOCK), bf16), ("p_e", (PHEADS, BLOCKS, BLOCK, BLOCK), bf16),
        ("e_over", (8, ROWS), f32), ("p_over", (16, ROWS), f32),
    ]
    scratch += [(n, sh, bf16) for n, sh in WEIGHTS]
    scratch += [("e_" + n, sh, d) for n, sh, d in KEPT] + [("p_" + n, sh, d) for n, sh, d in KEPT]
    scratch += list(SHARED)
    for i, phase in enumerate(PHASES):
        scratch += [(f"{name}{i}", shape, bf16) for name, shape in phase_buffers(*phase[1:])]
    sems = [("loads", (len(WEIGHTS) + 1,)), ("swaps", (2, 5)), ("sems", (len(PHASES), 2, 9))]
    names = [n for n, _ in args] + [n for n, _, _ in outs] + [n for n, _, _ in scratch] + [n for n, _ in sems] + ["free", "scalars"]
    return pl.pallas_call(
        functools.partial(slot_kernel, names),
        out_shape=[pltpu.VMEM(sh, d) for _, sh, d in outs],
        in_specs=specs,
        out_specs=[pl.BlockSpec(memory_space=pltpu.VMEM)] * len(outs),
        scratch_shapes=[pltpu.VMEM(sh, d) for _, sh, d in scratch] + [pltpu.SemaphoreType.DMA(sh) for _, sh in sems]
        + [pltpu.SemaphoreType.REGULAR((len(PHASES), 2)), pltpu.SMEM((8, 128), jnp.int32)],
        compiler_params=pltpu.CompilerParams(
            vmem_limit_bytes=52 * 2**20, collective_id=0, has_side_effects=True
        ),
    )(*[a for _, a in args])


LAYERS = (("pg", "pb", "pw", "pm", "px", "pxb", "pr"), ("eg", "eb", "ew", "em", "ex", "exb", "er"))
BIG = {"w": (F, 3 * F), "m": (F, F), "x": (F, FF), "r": (FF, F)}


def widen(g_ref, at, out_ref, rows, col):
    for c in range(3):
        out_ref[rows, col + c * 128 : col + c * 128 + 128] = g_ref[c, at : at + F, :].astype(f32)


def unpack_kernel(names, *refs):
    r = Refs()
    for name, ref in zip(names, refs):
        setattr(r, name, ref)
    copies = []

    def ship(src, dst):
        copy = pltpu.make_async_copy(src, dst, r.sems.at[len(copies)])
        copy.start()
        copies.append(copy)

    side = lax.axis_index("pipe") // 2
    r.wide[0] = r.kept[...].astype(f32)
    ship(r.wide.at[0], r.result.at[side])
    r.wide[1] = r.back[...].astype(f32)
    ship(r.wide.at[1], r.result.at[1 - side])
    g = r.grads
    for layer, at in (("p", PRED_AT), ("e", ENC_AT)):
        for part in range(4):
            rows = slice(part * F, part * F + F)
            widen(g, at["reduce"] + part * F, getattr(r, "s_" + layer + "r"), rows, 0)
        ship(getattr(r, "s_" + layer + "r"), getattr(r, layer + "r"))
        for part in range(4):
            widen(g, at["expand"] + part * F, getattr(r, "s_" + layer + "x"), slice(0, F), part * F)
        ship(getattr(r, "s_" + layer + "x"), getattr(r, layer + "x"))
        for part in range(3):
            widen(g, at["project"] + part * F, getattr(r, "s_" + layer + "w"), slice(0, F), part * F)
        ship(getattr(r, "s_" + layer + "w"), getattr(r, layer + "w"))
        widen(g, at["merge"], getattr(r, "s_" + layer + "m"), slice(0, F), 0)
        ship(getattr(r, "s_" + layer + "m"), getattr(r, layer + "m"))
        if layer == "p":
            widen(g, at["embed"], r.s_embed, slice(0, F), 0)
            ship(r.s_embed, r.embed)
        small = at["small"]
        rows = jnp.concatenate([g[c, small : small + 16, :] for c in range(3)], axis=1).astype(f32)
        getattr(r, layer + "g")[...] = rows[0:2]
        getattr(r, layer + "b")[...] = rows[2:8]
        for part in range(4):
            getattr(r, layer + "xb")[part * F : part * F + F] = rows[8 + part]
        if layer == "p":
            r.embed_bias[...] = rows[12]
    for copy in copies:
        copy.wait()


def unpack_call(grads, kept, back):
    big = [("embed", (F, F))] + [(layer + n, BIG[n]) for layer in "pe" for n in BIG]
    small = [("embed_bias", (F,))]
    for layer in "pe":
        small += [(layer + "g", (2, F)), (layer + "b", (6, F)), (layer + "xb", (FF,))]
    outs = [("result", (2, ROWS, F))] + big + small
    names = ["grads", "kept", "back"] + [n for n, _ in outs] + ["s_" + n for n, _ in big] + ["wide", "sems"]
    values = pl.pallas_call(
        functools.partial(unpack_kernel, names),
        out_shape=[jax.ShapeDtypeStruct(sh, f32) for _, sh in outs],
        in_specs=[pl.BlockSpec(memory_space=pltpu.VMEM)] * 3,
        out_specs=[pl.BlockSpec(memory_space=pl.ANY)] * (1 + len(big))
        + [pl.BlockSpec(memory_space=pltpu.VMEM)] * len(small),
        scratch_shapes=[pltpu.VMEM(sh, f32) for _, sh in big]
        + [pltpu.VMEM((2, ROWS, F), f32), pltpu.SemaphoreType.DMA((len(big) + 2,))],
        compiler_params=pltpu.CompilerParams(vmem_limit_bytes=24 * 2**20),
    )(*[pltpu.with_memory_space_constraint(v, pltpu.VMEM) for v in (grads, kept, back)])
    return dict(zip([n for n, _ in outs], values))


def body(segment_data, clip_frames, *weights):
    g = unpack_call(*slot_call(clip_frames, segment_data[0, 0], weights))
    order = ("eg", "eb", "ew", "em", "ex", "exb", "er", "embed", "embed_bias", "pg", "pb", "pw", "pm", "px", "pxb", "pr")
    return (g["result"][None, None],) + tuple(g[n] for n in order)


def solution(mesh):
    return jax.shard_map(
        body,
        mesh=mesh,
        in_specs=(P("pipe", "dp", None, None, None), P("dp", None, None, None)) + (P(),) * 16,
        out_specs=(P("pipe", "dp", None, None, None),) + (P(),) * 16,
        check_vma=False,
    )
```

```python
import functools
import math

import jax
import jax.numpy as jnp
from jax import lax
from jax.experimental import pallas as pl
from jax.experimental.pallas import tpu as pltpu
from jax.sharding import PartitionSpec as P

HEADS = 6
PHEADS = 12
CLIPS = 8
F = 384
FF = 1536
ROWS = 512
UNIT = 64
UNITS = ROWS // UNIT
BLOCK = 256
BLOCKS = ROWS // BLOCK
TOTAL = 10240
EPS = 1e-06
MASKED = -1e30

f32 = jnp.float32
bf16 = jnp.bfloat16


def dot(a, b, ca, cb):
    return lax.dot_general(a, b, (((ca,), (cb,)), ((), ())), preferred_element_type=f32)


def unit_order(frames):
    rows = [frames[c] * (UNIT // 8) for c in range(CLIPS)]
    start, place = [], []
    total = jnp.int32(0)
    for c in range(CLIPS):
        start.append(total)
        total = total + rows[c]
    for c in range(CLIPS):
        before = jnp.int32(0)
        for d in range(CLIPS):
            if d < c:
                ahead = rows[d] >= rows[c]
            elif d > c:
                ahead = rows[d] > rows[c]
            else:
                continue
            before = before + jnp.where(ahead, rows[d], 0)
        place.append(before)
    source, label = [], []
    for j in range(UNITS):
        at = j * UNIT
        src, lab = jnp.int32(at), jnp.int32(CLIPS + j)
        for c in range(CLIPS):
            held = (at >= place[c]) & (at < place[c] + rows[c])
            src = jnp.where(held, start[c] + at - place[c], src)
            lab = jnp.where(held, c, lab)
        source.append(src)
        label.append(lab)
    return source, label, total


def fill_order(order_ref, source):
    lane = lax.broadcasted_iota(jnp.int32, (1, ROWS), 1)
    row = spread(source, (1, ROWS), 1) + lane % UNIT
    at = lax.broadcasted_iota(jnp.int32, (ROWS, ROWS), 0)
    order_ref[...] = jnp.where(at == row, 1.0, 0.0).astype(bf16)


def spread(values, shape, axis):
    at = lax.broadcasted_iota(jnp.int32, shape, axis) // UNIT
    out = jnp.full(shape, values[0], jnp.int32)
    for i in range(1, len(values)):
        out = jnp.where(at == i, values[i], out)
    return out


def fill_mask(mask_ref, label):
    for b in range(BLOCKS):
        own = label[b * 4 : b * 4 + 4]
        down = spread(own, (BLOCK, BLOCK), 0)
        across = spread(own, (BLOCK, BLOCK), 1)
        mask_ref[b] = jnp.where(down == across, 0.0, MASKED).astype(f32)


def norm(v, gain, shift):
    mean = jnp.mean(v, axis=0, keepdims=True)
    centred = v - mean
    inverse = lax.rsqrt(jnp.mean(centred * centred, axis=0, keepdims=True) + EPS)
    normed = centred * inverse
    return normed * gain + shift, normed, inverse


def norm_back(k, normed, inverse):
    return inverse * (
        k
        - jnp.mean(k, axis=0, keepdims=True)
        - normed * jnp.mean(k * normed, axis=0, keepdims=True)
    )


def block_forward(stream_ref, out_ref, w, s, heads, mask_ref):
    size = F // heads
    scale = math.log2(math.e) / math.sqrt(size)
    vec = w.vec
    for t in range(ROWS // 128):
        cols = slice(t * 128, t * 128 + 128)
        full, normed, inverse = norm(stream_ref[:, cols], vec[:, 0:1], vec[:, 2:3])
        s.n1[:, cols] = normed
        s.i1[:, cols] = inverse
        s.a1[:, cols] = full.astype(bf16)
    for part in range(3):
        rows = slice(part * F, part * F + F)
        z = dot(w.project[:, rows], s.a1[...], 0, 0)
        if part == 0:
            z = z + vec[:, 3:4]
        if part == 2:
            z = z + vec[:, 4:5]
        s.z[rows, :] = z.astype(bf16)
    turns = [(h, b) for h in range(heads) for b in range(BLOCKS)]

    def place_of(h, b):
        return slice(h * size, h * size + size), slice(b * BLOCK, b * BLOCK + BLOCK)

    def score_of(h, b):
        own, cols = place_of(h, b)
        return dot(s.z[F + h * size : F + h * size + size, cols], s.z[own, cols], 0, 0)

    ahead = [score_of(*turn) for turn in turns[:3]]
    for i, (h, b) in enumerate(turns):
        own, cols = place_of(h, b)
        score = ahead.pop(0) * scale + mask_ref[b]
        if i + 3 < len(turns):
            ahead.append(score_of(*turns[i + 3]))
        e = jnp.exp2(score - jnp.max(score, axis=0, keepdims=True))
        over = 1.0 / jnp.sum(e, axis=0, keepdims=True)
        e = e.astype(bf16)
        s.e[h, b] = e
        s.over[h : h + 1, cols] = over
        v = s.z[2 * F + h * size : 2 * F + h * size + size, cols]
        s.o[own, cols] = (dot(v, e, 1, 0) * over).astype(bf16)
    middle = stream_ref[...] + (dot(w.merge[...], s.o[...], 0, 0) + vec[:, 5:6])
    s.m1[...] = middle
    for t in range(ROWS // 128):
        cols = slice(t * 128, t * 128 + 128)
        full, normed, inverse = norm(s.m1[:, cols], vec[:, 1:2], vec[:, 6:7])
        s.n2[:, cols] = normed
        s.i2[:, cols] = inverse
        s.a2[:, cols] = full.astype(bf16)
    for part in range(4):
        rows = slice(part * F, part * F + F)
        u = dot(w.expand[:, rows], s.a2[...], 0, 0) + vec[:, 8 + part : 9 + part]
        below = 0.5 * lax.erf(u * math.sqrt(0.5)) + 0.5
        density = jnp.exp2(u * u * (-0.5 * math.log2(math.e))) * (1.0 / math.sqrt(2.0 * math.pi))
        s.act[rows, :] = (u * below).astype(bf16)
        s.slope[rows, :] = (below + u * density).astype(bf16)
    out_ref[...] = s.m1[...] + (dot(w.reduce[...], s.act[...], 0, 0) + vec[:, 7:8])


def place(g_ref, at, value):
    for c in range(3):
        g_ref[c, at : at + value.shape[0], :] = value[:, c * 128 : c * 128 + 128].astype(bf16)


def total(x):
    return jnp.sum(x.astype(f32), axis=1, keepdims=True)


def block_backward(grad_ref, w, s, heads, g_ref, at, tick, late):
    size = F // heads
    vec = w.vec
    sums = [None] * 12
    s.q[...] = grad_ref[...].astype(bf16)
    q2 = s.q[...]
    sums[7] = total(q2)
    ahead = dot(w.reduce[0:F, :], q2, 1, 0)
    for part in range(4):
        rows = slice(part * F, part * F + F)
        grad_act = ahead
        if part < 3:
            ahead = dot(w.reduce[part * F + F : part * F + 2 * F, :], q2, 1, 0)
        du = (grad_act * s.slope[rows, :].astype(f32)).astype(bf16)
        s.du[rows, :] = du
        sums[8 + part] = total(du)
        place(g_ref, at["reduce"] + part * F, dot(s.act[rows, :], q2, 1, 1))
        tick()
    da = dot(w.expand[...], s.du[...], 1, 0)
    s.t[...] = da
    for t in range(ROWS // 128):
        cols = slice(t * 128, t * 128 + 128)
        grad_ref[:, cols] += norm_back(s.t[:, cols] * vec[:, 1:2], s.n2[:, cols], s.i2[:, cols])
        place(g_ref, at["expand"] + t * F, dot(s.a2[...], s.du[t * F : t * F + F, :], 1, 1))
    tick()
    sums[1] = total(s.t[...] * s.n2[...])
    sums[6] = total(s.t[...])
    s.q[...] = grad_ref[...].astype(bf16)
    q1 = s.q[...]
    sums[5] = total(q1)
    place(g_ref, at["merge"], dot(s.o[...], q1, 1, 1))
    s.t[...] = dot(w.merge[...], q1, 1, 0)
    tick()
    turns = [(h, b) for h in range(heads) for b in range(BLOCKS)]

    def slope_of(h, b):
        own, cols = slice(h * size, h * size + size), slice(b * BLOCK, b * BLOCK + BLOCK)
        do = (s.t[own, cols] * s.over[h : h + 1, cols]).astype(bf16)
        delta = jnp.sum(do.astype(f32) * s.o[own, cols].astype(f32), axis=0, keepdims=True)
        v = s.z[2 * F + h * size : 2 * F + h * size + size, cols]
        return do, delta, dot(v, do, 0, 0)

    ahead = [slope_of(*turn) for turn in turns[:2]]
    for i, (h, b) in enumerate(turns):
        cols = slice(b * BLOCK, b * BLOCK + BLOCK)
        lo = h * size
        q = s.z[lo : lo + size, cols]
        k = s.z[F + lo : F + lo + size, cols]
        do, delta, dp = ahead.pop(0)
        if i + 2 < len(turns):
            ahead.append(slope_of(*turns[i + 2]))
        e = s.e[h, b]
        ds = (dp - delta).astype(bf16) * e
        s.dz[2 * F + lo : 2 * F + lo + size, cols] = dot(do, e, 1, 1).astype(bf16)
        s.dz[lo : lo + size, cols] = (dot(k, ds, 1, 0) * (1.0 / math.sqrt(size))).astype(bf16)
        s.dz[F + lo : F + lo + size, cols] = (dot(q, ds, 1, 1) * (1.0 / math.sqrt(size))).astype(bf16)
        if i % 4 == 3:
            tick()
    sums[3] = total(s.dz[0:F, :])
    sums[4] = total(s.dz[2 * F : 3 * F, :])
    da = dot(w.project[...], s.dz[...], 1, 0)
    s.t[...] = da

    def last(t):
        cols = slice(t * 128, t * 128 + 128)
        grad_ref[:, cols] += norm_back(s.t[:, cols] * vec[:, 0:1], s.n1[:, cols], s.i1[:, cols])

    for t in range(ROWS // 128):
        if not late:
            last(t)
        if t < 3:
            place(g_ref, at["project"] + t * F, dot(s.a1[...], s.dz[t * F : t * F + F, :], 1, 1))
    sums[0] = total(s.t[...] * s.n1[...])
    sums[2] = total(s.t[...])
    tick()
    return sums, last


def columns(gains, biases, hidden):
    rows = [gains.astype(f32), biases.astype(f32)]
    for part in range(4):
        rows.append(hidden[part * F : part * F + F].astype(f32).reshape(1, F))
    rows.append(jnp.zeros((4, F), f32))
    return jnp.concatenate(rows, axis=0).T


def place_sums(g_ref, at, sums):
    lane = lax.broadcasted_iota(jnp.int32, (F, 128), 1)
    table = jnp.zeros((F, 128), f32)
    for i, column in enumerate(sums):
        table = jnp.where(lane == i, column, table)
    place(g_ref, at, table.T[0:16, :])


class Refs:
    pass


KEPT = (
    ("n1", (F, ROWS), f32), ("i1", (1, ROWS), f32), ("a1", (F, ROWS), bf16), ("z", (3 * F, ROWS), bf16),
    ("o", (F, ROWS), bf16), ("m1", (F, ROWS), f32), ("n2", (F, ROWS), f32), ("i2", (1, ROWS), f32),
    ("a2", (F, ROWS), bf16), ("act", (FF, ROWS), bf16), ("slope", (FF, ROWS), bf16),
)
SHARED = (
    ("q", (F, ROWS), bf16), ("du", (FF, ROWS), bf16), ("t", (F, ROWS), f32), ("dz", (3 * F, ROWS), bf16),
)


PHASES = ((0, 3072, True, False), (3072, 2048, True, False), (5120, 1536, False, False), (6656, 2048, False, False), (8704, 1536, False, False))
PRED_AT = {"reduce": 0, "expand": 1536, "merge": 3072, "project": 3456, "embed": 4608, "small": 4992, "end": 5008}
ENC_AT = {"reduce": 5120, "expand": 6656, "merge": 8192, "gap": 8576, "project": 8704, "small": 9856, "end": 9872}
ORDERS = ("xyz", "yzx", "zxy")
WEIGHTS = (
    ("ew", (F, 3 * F)), ("em", (F, F)), ("ex", (F, FF)), ("er", (FF, F)), ("embed", (F, F)),
    ("pw", (F, 3 * F)), ("pm", (F, F)), ("px", (F, FF)), ("pr", (FF, F)),
)


class Where:
    def __init__(self):
        p, d = lax.axis_index("pipe"), lax.axis_index("dp")
        self.core, low = p % 2, p // 2
        self.at = {"x": d // 8, "y": d % 4, "z": ((d // 4) % 2) * 2 + low}
        self.side = low
        self.turn = {axis: [(self.at[axis] + k) % 4 for k in range(4)] for axis in "xyz"}
        self.near = {
            axis: [self.device(self.core, {**self.at, axis: self.turn[axis][k]}) for k in range(4)] for axis in "xyz"
        }
        self.twin = self.device(1 - self.core, self.at)
        z = self.at["z"]
        home = z + 1 - 2 * (z % 2)
        mate = home + self.core * (3 - z - home)
        self.out = self.device(self.core, {**self.at, "z": mate + self.side * (home - mate)})
        self.back = self.device(self.core, {**self.at, "z": home + self.side * (mate - home)})
        self.far = self.near["z"][2]

    def device(self, core, at):
        return {"pipe": (at["z"] % 2) * 2 + core, "dp": at["x"] * 8 + (at["z"] // 2) * 4 + at["y"]}

    def around(self, steps):
        return [self.near[axis][d] for axis in "xyz" for d in steps]


def send(src, dst, sems, i, device):
    copy = pltpu.make_async_remote_copy(
        src_ref=src, dst_ref=dst, send_sem=sems.at[0, i], recv_sem=sems.at[1, i],
        device_id=device, device_id_type=pl.DeviceIdType.MESH,
    )
    copy.start()
    return copy


def phase_buffers(size, relay, wide):
    quarter, small = size // 8, size // 32
    full = quarter if wide else small
    shapes = [("core", (3, size // 2, 128)), ("three", (3, 4, full, 128))]
    if relay:
        shapes += [("one", (3, 2, quarter // 2, 128)), ("two", (3, 2, quarter, 128))]
    else:
        shapes += [("one", (3, 3, quarter, 128))]
    shapes += [("wide", (3, 4, quarter, 128)) if wide else ("small", (3, 3, small, 128))]
    return shapes


def reduce_phase(me, g, phase, recv, sems, free):
    base, size, relay, wide = phase
    half, quarter, small = size // 2, size // 8, size // 32
    mine, others = base + me.core * half, base + (1 - me.core) * half
    step = [0]

    def go(src, dst, device):
        send(src, dst, sems, step[0], device)

    def wait(all_of_it):
        pltpu.make_async_remote_copy(
            src_ref=all_of_it, dst_ref=all_of_it, send_sem=sems.at[0, step[0]], recv_sem=sems.at[1, step[0]],
            device_id=me.twin, device_id_type=pl.DeviceIdType.MESH,
        ).wait()
        step[0] += 1

    def rows_of(c, start, count):
        return g.at[c, pl.ds(start, count), :]

    def release(i, devices):
        for device in devices:
            pl.semaphore_signal(free.at[i], inc=1, device_id=device, device_id_type=pl.DeviceIdType.MESH)

    def add(c, start, count, terms):
        own = pl.ds(start, count)
        value = g[c, own, :].astype(f32)
        for term in terms:
            value = value + term.astype(f32)
        g[c, own, :] = value.astype(bf16)

    def exchange(starts, rows, buf, turn):
        for c in range(3):
            buf[c, me.at[ORDERS[c][turn]]] = g[c, pl.ds(starts[c], rows), :]
        for d in (2, 1, 3):
            for c in range(3):
                block = buf.at[c, me.at[ORDERS[c][turn]]]
                go(block, block, me.near[ORDERS[c][turn]][d])

    def total_of(starts, rows, buf):
        for c in range(3):
            value = buf[c, 0].astype(f32)
            for j in range(1, 4):
                value = value + buf[c, j].astype(f32)
            g[c, pl.ds(starts[c], rows), :] = value.astype(bf16)

    go(g.at[:, pl.ds(others, half), :], recv.core, me.twin)
    yield
    wait(recv.core)
    release(0, [me.twin])
    for c in range(3):
        add(c, mine, half, [recv.core[c]])

    axes = [order[0] for order in ORDERS]
    chunk = [[mine + me.turn[axes[c]][k] * quarter for k in range(4)] for c in range(3)]
    one = [chunk[c][0] for c in range(3)]
    if relay:
        part = quarter // 2
        for c in range(3):
            go(rows_of(c, chunk[c][2], part), recv.one.at[c, 0], me.near[axes[c]][1])
            go(rows_of(c, chunk[c][2] + part, part), recv.one.at[c, 1], me.near[axes[c]][3])
        yield
        wait(recv.one)
        for c in range(3):
            add(c, chunk[c][1], part, [recv.one[c, 0]])
            add(c, chunk[c][3] + part, part, [recv.one[c, 1]])
            go(rows_of(c, chunk[c][1], quarter), recv.two.at[c, 0], me.near[axes[c]][1])
            go(rows_of(c, chunk[c][3], quarter), recv.two.at[c, 1], me.near[axes[c]][3])
        yield
        wait(recv.two)
        for c in range(3):
            add(c, one[c], quarter, [recv.two[c, 0], recv.two[c, 1]])
    else:
        for d in (2, 1, 3):
            for c in range(3):
                go(rows_of(c, chunk[c][d], quarter), recv.one.at[c, d - 1], me.near[axes[c]][d])
        yield
        wait(recv.one)
        for c in range(3):
            add(c, one[c], quarter, [recv.one[c, d] for d in range(3)])

    if wide:
        release(1, me.around((1, 2, 3)))
        exchange(one, quarter, recv.wide, 1)
        yield
        wait(recv.wide.at[:, 0:3])
        total_of(one, quarter, recv.wide)
        exchange(one, quarter, recv.three, 2)
        yield
        wait(recv.three.at[:, 0:3])
        total_of(one, quarter, recv.three)
    else:
        axes2 = [order[1] for order in ORDERS]
        two = [one[c] + me.at[axes2[c]] * small for c in range(3)]
        for d in (2, 1, 3):
            for c in range(3):
                block = rows_of(c, one[c] + me.turn[axes2[c]][d] * small, small)
                go(block, recv.small.at[c, d - 1], me.near[axes2[c]][d])
        yield
        wait(recv.small)
        release(1, me.around((1, 2, 3)))
        for c in range(3):
            add(c, two[c], small, [recv.small[c, d] for d in range(3)])
        exchange(two, small, recv.three, 2)
        yield
        wait(recv.three.at[:, 0:3])
        total_of(two, small, recv.three)
        pl.semaphore_wait(free.at[1], 9)
        for d in (2, 1, 3):
            for c in range(3):
                block = rows_of(c, two[c], small)
                go(block, block, me.near[axes2[c]][d])
        yield
        wait(recv.small)

    if wide:
        pl.semaphore_wait(free.at[1], 9)
    for d in (1, 3) if relay else (2, 1, 3):
        for c in range(3):
            block = rows_of(c, one[c], quarter)
            go(block, block, me.near[axes[c]][d])
    yield
    wait(recv.two if relay else recv.one)
    if relay:
        for c in range(3):
            block = rows_of(c, chunk[c][3], part)
            go(block, block, me.near[axes[c]][1])
            block = rows_of(c, chunk[c][1] + part, part)
            go(block, block, me.near[axes[c]][3])
        yield
        wait(recv.one)
    pl.semaphore_wait(free.at[0], 1)
    block = g.at[:, pl.ds(mine, half), :]
    go(block, block, me.twin)
    yield
    wait(recv.core)


def slot_kernel(names, *refs):
    r = Refs()
    for name, ref in zip(names, refs):
        setattr(r, name, ref)
    me = Where()
    first = me.side == 0
    loads = {}
    for i, (name, _) in enumerate(WEIGHTS):
        loads[name] = pltpu.make_async_copy(getattr(r, "h_" + name), getattr(r, name), r.loads.at[i])
        loads[name].start()
    barrier = pltpu.get_barrier_semaphore()
    friends = [me.twin] + me.around((1, 2, 3))
    for device in friends:
        pl.semaphore_signal(barrier, inc=1, device_id=device, device_id_type=pl.DeviceIdType.MESH)
    lane = lax.broadcasted_iota(jnp.int32, (8, 128), 1)
    counts = jnp.zeros((8, 128), jnp.int32)
    for c in range(CLIPS):
        counts = jnp.where(lane == c, r.frames[0, 1, me.core, c], counts)
    r.counts[...] = counts
    pl.semaphore_wait(barrier, len(friends))
    told = send(r.counts, r.far_counts, r.swaps, 4, me.far)
    swap = send(r.local.at[1 - me.side], r.arrived, r.swaps, 0, me.out)
    away = me.side * me.core == 1
    lookup = pltpu.make_async_copy(r.far_counts, r.scalars, r.loads.at[len(WEIGHTS)])

    @pl.when(away)
    def _():
        told.wait_recv()
        lookup.start()
        lookup.wait()

    @pl.when(jnp.logical_not(away))
    def _():
        for c in range(CLIPS):
            r.scalars[0, c] = r.frames[0, me.side, me.core, c]

    source, label, live = unit_order([r.scalars[0, c] for c in range(CLIPS)])
    fill_mask(r.mask, label)
    fill_order(r.order, source)
    enc, pred = Refs(), Refs()
    enc.vec = columns(r.eg[...], r.eb[...], r.exb[...])
    pred.vec = columns(r.pg[...], r.pb[...], r.pxb[...])
    enc.project, enc.merge, enc.expand, enc.reduce = r.ew, r.em, r.ex, r.er
    pred.project, pred.merge, pred.expand, pred.reduce = r.pw, r.pm, r.px, r.pr
    es, ps = Refs(), Refs()
    for name, _, _ in KEPT:
        setattr(es, name, getattr(r, "e_" + name))
        setattr(ps, name, getattr(r, "p_" + name))
    for name, _, _ in SHARED:
        setattr(es, name, getattr(r, name))
        setattr(ps, name, getattr(r, name))
    es.e, es.over, ps.e, ps.over = r.e_e, r.e_over, r.p_e, r.p_over


    @pl.when(jnp.logical_not(first))
    def _():
        swap.wait_recv()

    far_rows = pltpu.make_async_remote_copy(
        src_ref=r.local.at[1], dst_ref=r.cotangent, send_sem=r.swaps.at[0, 2], recv_sem=r.swaps.at[1, 2],
        device_id=me.far, device_id_type=pl.DeviceIdType.MESH,
    )

    @pl.when(away)
    def _():
        far_rows.start()

    @pl.when(first)
    def _():
        r.x[...] = r.local[0]

    @pl.when(jnp.logical_not(first))
    def _():
        r.x[...] = r.arrived[...]

    r.stream[...] = dot(r.x[...], r.order[...], 0, 0)
    for copy in loads.values():
        copy.wait()

    block_forward(r.stream, r.stream2, enc, es, HEADS, r.mask)
    r.sent[...] = r.stream2[...].astype(bf16)
    r.stream[...] = dot(r.embed[...], r.sent[...], 0, 0) + r.embed_bias[...].astype(f32).reshape(1, F).T
    block_forward(r.stream, r.stream2, pred, ps, PHEADS, r.mask)

    alive = lax.broadcasted_iota(jnp.int32, (F, ROWS), 1) < live
    r.out[...] = dot(r.order[...], jnp.where(alive, r.stream2[...], 0.0).astype(bf16), 1, 1).astype(bf16)
    copy_out = pltpu.make_async_remote_copy(
        src_ref=r.sends, dst_ref=r.back, send_sem=r.swaps.at[0, 1], recv_sem=r.swaps.at[1, 1],
        device_id=me.back, device_id_type=pl.DeviceIdType.MESH,
    )
    far_out = pltpu.make_async_remote_copy(
        src_ref=r.out, dst_ref=r.kept, send_sem=r.swaps.at[0, 3], recv_sem=r.swaps.at[1, 3],
        device_id=me.far, device_id_type=pl.DeviceIdType.MESH,
    )

    @pl.when(first)
    def _():
        r.sends[...] = r.out[...]
        copy_out.start()
        swap.wait_recv()
        r.cotangent[...] = r.arrived[...]

    @pl.when(away)
    def _():
        far_out.start()
        far_rows.wait()

    @pl.when(me.side * (1 - me.core) == 1)
    def _():
        r.cotangent[...] = r.local[1]
        r.kept[...] = r.out[...]

    swap.wait_send()
    told.wait_send()

    @pl.when(jnp.logical_not(away))
    def _():
        told.wait_recv()

    cotangent = r.cotangent[...]
    r.stream[...] = jnp.where(alive, dot(cotangent, r.order[...], 0, 0), 0.0)

    g = r.grads
    phases = []
    for i, phase in enumerate(PHASES):
        recv = Refs()
        for name, _ in phase_buffers(*phase[1:]):
            setattr(recv, name, getattr(r, f"{name}{i}"))
        phases.append(reduce_phase(me, g, phase, recv, r.sems.at[i], r.free.at[i]))

    ticks = iter(PLAN)

    def tick():
        for i in next(ticks):
            next(phases[i], None)

    sums, _ = block_backward(r.stream, pred, ps, PHEADS, g, PRED_AT, tick, False)
    r.q[...] = r.stream[...].astype(bf16)
    de = r.q[...]
    place(g, PRED_AT["embed"], dot(r.sent[...], de, 1, 1))
    place_sums(g, PRED_AT["small"], sums + [total(de)])
    g[:, PRED_AT["end"] : ENC_AT["reduce"], :] = jnp.zeros((3, ENC_AT["reduce"] - PRED_AT["end"], 128), bf16)
    g[:, ENC_AT["gap"] : ENC_AT["project"], :] = jnp.zeros((3, ENC_AT["project"] - ENC_AT["gap"], 128), bf16)
    g[:, ENC_AT["end"] : TOTAL, :] = jnp.zeros((3, TOTAL - ENC_AT["end"], 128), bf16)
    r.stream[...] = dot(r.embed[...], de, 1, 0).astype(bf16).astype(f32)
    tick()
    sums, last = block_backward(r.stream, enc, es, HEADS, g, ENC_AT, tick, True)
    place_sums(g, ENC_AT["small"], sums)
    tick()
    for n, i in enumerate(TAIL):
        if n == 3:
            for t in range(ROWS // 128):
                last(t)
            dx = dot(r.order[...], r.stream[...].astype(bf16), 1, 1).astype(bf16)

            @pl.when(first)
            def _():
                r.kept[...] = dx

            @pl.when(jnp.logical_not(first))
            def _():
                r.sends[...] = dx

        if i is None:

            @pl.when(jnp.logical_not(first))
            def _():
                copy_out.start()

        else:
            next(phases[i], None)
    copy_out.wait()

    @pl.when(away)
    def _():
        far_out.wait()


PLAN = (
    (), (), (), (), (0,), (), (), (), (), (), (), (), (0,), (1,), (), (), (), (1, 0, 2,), (), (1, 2, 3,), (0,), (), (), (3, 1,), (4,),
)
TAIL = (2, 0, 4, 3, 1, 2, 0, 4, 3, 1, 2, 0, 4, 3, 1, 2, 0, 4, 3, 1, 2, 0, 4, None, 2, 3, 1, 0, 4, 3, 1, 4)


def slot_call(frames, local, weights):
    args = [("frames", frames), ("local", local)]
    big = {name for name, _ in WEIGHTS}
    order = ("eg", "eb", "ew", "em", "ex", "exb", "er", "embed", "embed_bias", "pg", "pb", "pw", "pm", "px", "pxb", "pr")
    specs = [pl.BlockSpec(memory_space=pltpu.SMEM), pl.BlockSpec(memory_space=pltpu.VMEM)]
    for name, weight in zip(order, weights):
        args.append(("h_" + name if name in big else name, weight))
        specs.append(pl.BlockSpec(memory_space=pl.ANY if name in big else pltpu.VMEM))
    outs = [("grads", (3, TOTAL, 128), bf16), ("kept", (ROWS, F), bf16), ("back", (ROWS, F), bf16)]
    scratch = [
        ("mask", (BLOCKS, BLOCK, BLOCK), f32), ("order", (ROWS, ROWS), bf16), ("out", (ROWS, F), bf16),
        ("stream", (F, ROWS), f32), ("stream2", (F, ROWS), f32), ("sent", (F, ROWS), bf16),
        ("arrived", (ROWS, F), bf16), ("cotangent", (ROWS, F), bf16), ("x", (ROWS, F), bf16),
        ("counts", (8, 128), jnp.int32), ("far_counts", (8, 128), jnp.int32), ("sends", (ROWS, F), bf16),
        ("e_e", (HEADS, BLOCKS, BLOCK, BLOCK), bf16), ("p_e", (PHEADS, BLOCKS, BLOCK, BLOCK), bf16),
        ("e_over", (8, ROWS), f32), ("p_over", (16, ROWS), f32),
    ]
    scratch += [(n, sh, bf16) for n, sh in WEIGHTS]
    scratch += [("e_" + n, sh, d) for n, sh, d in KEPT] + [("p_" + n, sh, d) for n, sh, d in KEPT]
    scratch += list(SHARED)
    for i, phase in enumerate(PHASES):
        scratch += [(f"{name}{i}", shape, bf16) for name, shape in phase_buffers(*phase[1:])]
    sems = [("loads", (len(WEIGHTS) + 1,)), ("swaps", (2, 5)), ("sems", (len(PHASES), 2, 9))]
    names = [n for n, _ in args] + [n for n, _, _ in outs] + [n for n, _, _ in scratch] + [n for n, _ in sems] + ["free", "scalars"]
    return pl.pallas_call(
        functools.partial(slot_kernel, names),
        out_shape=[pltpu.VMEM(sh, d) for _, sh, d in outs],
        in_specs=specs,
        out_specs=[pl.BlockSpec(memory_space=pltpu.VMEM)] * len(outs),
        scratch_shapes=[pltpu.VMEM(sh, d) for _, sh, d in scratch] + [pltpu.SemaphoreType.DMA(sh) for _, sh in sems]
        + [pltpu.SemaphoreType.REGULAR((len(PHASES), 2)), pltpu.SMEM((8, 128), jnp.int32)],
        compiler_params=pltpu.CompilerParams(
            vmem_limit_bytes=52 * 2**20, collective_id=0, has_side_effects=True
        ),
    )(*[a for _, a in args])


LAYERS = (("pg", "pb", "pw", "pm", "px", "pxb", "pr"), ("eg", "eb", "ew", "em", "ex", "exb", "er"))
BIG = {"w": (F, 3 * F), "m": (F, F), "x": (F, FF), "r": (FF, F)}


def widen(g_ref, at, out_ref, rows, col):
    for c in range(3):
        out_ref[rows, col + c * 128 : col + c * 128 + 128] = g_ref[c, at : at + F, :].astype(f32)


def unpack_kernel(names, *refs):
    r = Refs()
    for name, ref in zip(names, refs):
        setattr(r, name, ref)
    copies = []

    def ship(src, dst):
        copy = pltpu.make_async_copy(src, dst, r.sems.at[len(copies)])
        copy.start()
        copies.append(copy)

    side = lax.axis_index("pipe") // 2
    r.wide[0] = r.kept[...].astype(f32)
    ship(r.wide.at[0], r.result.at[side])
    r.wide[1] = r.back[...].astype(f32)
    ship(r.wide.at[1], r.result.at[1 - side])
    g = r.grads
    for layer, at in (("p", PRED_AT), ("e", ENC_AT)):
        for part in range(4):
            rows = slice(part * F, part * F + F)
            widen(g, at["reduce"] + part * F, getattr(r, "s_" + layer + "r"), rows, 0)
        ship(getattr(r, "s_" + layer + "r"), getattr(r, layer + "r"))
        for part in range(4):
            widen(g, at["expand"] + part * F, getattr(r, "s_" + layer + "x"), slice(0, F), part * F)
        ship(getattr(r, "s_" + layer + "x"), getattr(r, layer + "x"))
        for part in range(3):
            widen(g, at["project"] + part * F, getattr(r, "s_" + layer + "w"), slice(0, F), part * F)
        ship(getattr(r, "s_" + layer + "w"), getattr(r, layer + "w"))
        widen(g, at["merge"], getattr(r, "s_" + layer + "m"), slice(0, F), 0)
        ship(getattr(r, "s_" + layer + "m"), getattr(r, layer + "m"))
        if layer == "p":
            widen(g, at["embed"], r.s_embed, slice(0, F), 0)
            ship(r.s_embed, r.embed)
        small = at["small"]
        rows = jnp.concatenate([g[c, small : small + 16, :] for c in range(3)], axis=1).astype(f32)
        getattr(r, layer + "g")[...] = rows[0:2]
        getattr(r, layer + "b")[...] = rows[2:8]
        for part in range(4):
            getattr(r, layer + "xb")[part * F : part * F + F] = rows[8 + part]
        if layer == "p":
            r.embed_bias[...] = rows[12]
    for copy in copies:
        copy.wait()


def unpack_call(grads, kept, back):
    big = [("embed", (F, F))] + [(layer + n, BIG[n]) for layer in "pe" for n in BIG]
    small = [("embed_bias", (F,))]
    for layer in "pe":
        small += [(layer + "g", (2, F)), (layer + "b", (6, F)), (layer + "xb", (FF,))]
    outs = [("result", (2, ROWS, F))] + big + small
    names = ["grads", "kept", "back"] + [n for n, _ in outs] + ["s_" + n for n, _ in big] + ["wide", "sems"]
    values = pl.pallas_call(
        functools.partial(unpack_kernel, names),
        out_shape=[jax.ShapeDtypeStruct(sh, f32) for _, sh in outs],
        in_specs=[pl.BlockSpec(memory_space=pltpu.VMEM)] * 3,
        out_specs=[pl.BlockSpec(memory_space=pl.ANY)] * (1 + len(big))
        + [pl.BlockSpec(memory_space=pltpu.VMEM)] * len(small),
        scratch_shapes=[pltpu.VMEM(sh, f32) for _, sh in big]
        + [pltpu.VMEM((2, ROWS, F), f32), pltpu.SemaphoreType.DMA((len(big) + 2,))],
        compiler_params=pltpu.CompilerParams(vmem_limit_bytes=24 * 2**20),
    )(*[pltpu.with_memory_space_constraint(v, pltpu.VMEM) for v in (grads, kept, back)])
    return dict(zip([n for n, _ in outs], values))


def body(segment_data, clip_frames, *weights):
    g = unpack_call(*slot_call(clip_frames, segment_data[0, 0], weights))
    order = ("eg", "eb", "ew", "em", "ex", "exb", "er", "embed", "embed_bias", "pg", "pb", "pw", "pm", "px", "pxb", "pr")
    return (g["result"][None, None],) + tuple(g[n] for n in order)


def solution(mesh):
    return jax.shard_map(
        body,
        mesh=mesh,
        in_specs=(P("pipe", "dp", None, None, None), P("dp", None, None, None)) + (P(),) * 16,
        out_specs=(P("pipe", "dp", None, None, None),) + (P(),) * 16,
        check_vma=False,
    )
```

```python
import functools
import math

import jax
import jax.numpy as jnp
from jax import lax
from jax.experimental import pallas as pl
from jax.experimental.pallas import tpu as pltpu
from jax.sharding import PartitionSpec as P

HEADS = 6
PHEADS = 12
CLIPS = 8
F = 384
FF = 1536
ROWS = 512
UNIT = 64
UNITS = ROWS // UNIT
BLOCK = 256
BLOCKS = ROWS // BLOCK
TOTAL = 10240
EPS = 1e-06
MASKED = -1e30

f32 = jnp.float32
bf16 = jnp.bfloat16


def dot(a, b, ca, cb):
    return lax.dot_general(a, b, (((ca,), (cb,)), ((), ())), preferred_element_type=f32)


def unit_order(frames):
    rows = [frames[c] * (UNIT // 8) for c in range(CLIPS)]
    start, place = [], []
    total = jnp.int32(0)
    for c in range(CLIPS):
        start.append(total)
        total = total + rows[c]
    for c in range(CLIPS):
        before = jnp.int32(0)
        for d in range(CLIPS):
            if d < c:
                ahead = rows[d] >= rows[c]
            elif d > c:
                ahead = rows[d] > rows[c]
            else:
                continue
            before = before + jnp.where(ahead, rows[d], 0)
        place.append(before)
    source, label = [], []
    for j in range(UNITS):
        at = j * UNIT
        src, lab = jnp.int32(at), jnp.int32(CLIPS + j)
        for c in range(CLIPS):
            held = (at >= place[c]) & (at < place[c] + rows[c])
            src = jnp.where(held, start[c] + at - place[c], src)
            lab = jnp.where(held, c, lab)
        source.append(src)
        label.append(lab)
    return source, label, total


def fill_order(order_ref, source):
    lane = lax.broadcasted_iota(jnp.int32, (1, ROWS), 1)
    row = spread(source, (1, ROWS), 1) + lane % UNIT
    at = lax.broadcasted_iota(jnp.int32, (ROWS, ROWS), 0)
    order_ref[...] = jnp.where(at == row, 1.0, 0.0).astype(bf16)


def spread(values, shape, axis):
    at = lax.broadcasted_iota(jnp.int32, shape, axis) // UNIT
    out = jnp.full(shape, values[0], jnp.int32)
    for i in range(1, len(values)):
        out = jnp.where(at == i, values[i], out)
    return out


def fill_mask(mask_ref, label):
    for b in range(BLOCKS):
        own = label[b * 4 : b * 4 + 4]
        down = spread(own, (BLOCK, BLOCK), 0)
        across = spread(own, (BLOCK, BLOCK), 1)
        mask_ref[b] = jnp.where(down == across, 0.0, MASKED).astype(f32)


def norm(v, gain, shift):
    mean = jnp.mean(v, axis=0, keepdims=True)
    centred = v - mean
    inverse = lax.rsqrt(jnp.mean(centred * centred, axis=0, keepdims=True) + EPS)
    normed = centred * inverse
    return normed * gain + shift, normed, inverse


def norm_back(k, normed, inverse):
    return inverse * (
        k
        - jnp.mean(k, axis=0, keepdims=True)
        - normed * jnp.mean(k * normed, axis=0, keepdims=True)
    )


def block_forward(stream_ref, out_ref, w, s, heads, mask_ref):
    size = F // heads
    scale = math.log2(math.e) / math.sqrt(size)
    vec = w.vec
    for t in range(ROWS // 128):
        cols = slice(t * 128, t * 128 + 128)
        full, normed, inverse = norm(stream_ref[:, cols], vec[:, 0:1], vec[:, 2:3])
        s.n1[:, cols] = normed
        s.i1[:, cols] = inverse
        s.a1[:, cols] = full.astype(bf16)
    for part in range(3):
        rows = slice(part * F, part * F + F)
        z = dot(w.project[:, rows], s.a1[...], 0, 0)
        if part == 0:
            z = z + vec[:, 3:4]
        if part == 2:
            z = z + vec[:, 4:5]
        s.z[rows, :] = z.astype(bf16)
    turns = [(h, b) for h in range(heads) for b in range(BLOCKS)]

    def place_of(h, b):
        return slice(h * size, h * size + size), slice(b * BLOCK, b * BLOCK + BLOCK)

    def score_of(h, b):
        own, cols = place_of(h, b)
        return dot(s.z[F + h * size : F + h * size + size, cols], s.z[own, cols], 0, 0)

    ahead = [score_of(*turn) for turn in turns[:3]]
    for i, (h, b) in enumerate(turns):
        own, cols = place_of(h, b)
        score = ahead.pop(0) * scale + mask_ref[b]
        if i + 3 < len(turns):
            ahead.append(score_of(*turns[i + 3]))
        e = jnp.exp2(score - jnp.max(score, axis=0, keepdims=True))
        over = 1.0 / jnp.sum(e, axis=0, keepdims=True)
        e = e.astype(bf16)
        s.e[h, b] = e
        s.over[h : h + 1, cols] = over
        v = s.z[2 * F + h * size : 2 * F + h * size + size, cols]
        s.o[own, cols] = (dot(v, e, 1, 0) * over).astype(bf16)
    middle = stream_ref[...] + (dot(w.merge[...], s.o[...], 0, 0) + vec[:, 5:6])
    s.m1[...] = middle
    for t in range(ROWS // 128):
        cols = slice(t * 128, t * 128 + 128)
        full, normed, inverse = norm(s.m1[:, cols], vec[:, 1:2], vec[:, 6:7])
        s.n2[:, cols] = normed
        s.i2[:, cols] = inverse
        s.a2[:, cols] = full.astype(bf16)
    for part in range(4):
        rows = slice(part * F, part * F + F)
        u = dot(w.expand[:, rows], s.a2[...], 0, 0) + vec[:, 8 + part : 9 + part]
        below = 0.5 * lax.erf(u * math.sqrt(0.5)) + 0.5
        density = jnp.exp2(u * u * (-0.5 * math.log2(math.e))) * (1.0 / math.sqrt(2.0 * math.pi))
        s.act[rows, :] = (u * below).astype(bf16)
        s.slope[rows, :] = (below + u * density).astype(bf16)
    out_ref[...] = s.m1[...] + (dot(w.reduce[...], s.act[...], 0, 0) + vec[:, 7:8])


def place(g_ref, at, value):
    for c in range(3):
        g_ref[c, at : at + value.shape[0], :] = value[:, c * 128 : c * 128 + 128].astype(bf16)


def total(x):
    return jnp.sum(x.astype(f32), axis=1, keepdims=True)


def block_backward(grad_ref, w, s, heads, g_ref, at, tick, late):
    size = F // heads
    vec = w.vec
    sums = [None] * 12
    s.q[...] = grad_ref[...].astype(bf16)
    q2 = s.q[...]
    sums[7] = total(q2)
    ahead = dot(w.reduce[0:F, :], q2, 1, 0)
    for part in range(4):
        rows = slice(part * F, part * F + F)
        grad_act = ahead
        if part < 3:
            ahead = dot(w.reduce[part * F + F : part * F + 2 * F, :], q2, 1, 0)
        du = (grad_act * s.slope[rows, :].astype(f32)).astype(bf16)
        s.du[rows, :] = du
        sums[8 + part] = total(du)
        place(g_ref, at["reduce"] + part * F, dot(s.act[rows, :], q2, 1, 1))
        tick()
    da = dot(w.expand[...], s.du[...], 1, 0)
    s.t[...] = da
    for t in range(ROWS // 128):
        cols = slice(t * 128, t * 128 + 128)
        grad_ref[:, cols] += norm_back(s.t[:, cols] * vec[:, 1:2], s.n2[:, cols], s.i2[:, cols])
        place(g_ref, at["expand"] + t * F, dot(s.a2[...], s.du[t * F : t * F + F, :], 1, 1))
    tick()
    sums[1] = total(s.t[...] * s.n2[...])
    sums[6] = total(s.t[...])
    s.q[...] = grad_ref[...].astype(bf16)
    q1 = s.q[...]
    sums[5] = total(q1)
    place(g_ref, at["merge"], dot(s.o[...], q1, 1, 1))
    s.t[...] = dot(w.merge[...], q1, 1, 0)
    tick()
    turns = [(h, b) for h in range(heads) for b in range(BLOCKS)]

    def slope_of(h, b):
        own, cols = slice(h * size, h * size + size), slice(b * BLOCK, b * BLOCK + BLOCK)
        do = (s.t[own, cols] * s.over[h : h + 1, cols]).astype(bf16)
        delta = jnp.sum(do.astype(f32) * s.o[own, cols].astype(f32), axis=0, keepdims=True)
        v = s.z[2 * F + h * size : 2 * F + h * size + size, cols]
        return do, delta, dot(v, do, 0, 0)

    ahead = [slope_of(*turn) for turn in turns[:2]]
    for i, (h, b) in enumerate(turns):
        cols = slice(b * BLOCK, b * BLOCK + BLOCK)
        lo = h * size
        q = s.z[lo : lo + size, cols]
        k = s.z[F + lo : F + lo + size, cols]
        do, delta, dp = ahead.pop(0)
        if i + 2 < len(turns):
            ahead.append(slope_of(*turns[i + 2]))
        e = s.e[h, b]
        ds = (dp - delta).astype(bf16) * e
        s.dz[2 * F + lo : 2 * F + lo + size, cols] = dot(do, e, 1, 1).astype(bf16)
        s.dz[lo : lo + size, cols] = (dot(k, ds, 1, 0) * (1.0 / math.sqrt(size))).astype(bf16)
        s.dz[F + lo : F + lo + size, cols] = (dot(q, ds, 1, 1) * (1.0 / math.sqrt(size))).astype(bf16)
        if i % 4 == 3:
            tick()
    sums[3] = total(s.dz[0:F, :])
    sums[4] = total(s.dz[2 * F : 3 * F, :])
    da = dot(w.project[...], s.dz[...], 1, 0)
    s.t[...] = da

    def last(t):
        cols = slice(t * 128, t * 128 + 128)
        grad_ref[:, cols] += norm_back(s.t[:, cols] * vec[:, 0:1], s.n1[:, cols], s.i1[:, cols])

    for t in range(ROWS // 128):
        if not late:
            last(t)
        if t < 3:
            place(g_ref, at["project"] + t * F, dot(s.a1[...], s.dz[t * F : t * F + F, :], 1, 1))
    sums[0] = total(s.t[...] * s.n1[...])
    sums[2] = total(s.t[...])
    tick()
    return sums, last


def columns(gains, biases, hidden):
    rows = [gains.astype(f32), biases.astype(f32)]
    for part in range(4):
        rows.append(hidden[part * F : part * F + F].astype(f32).reshape(1, F))
    rows.append(jnp.zeros((4, F), f32))
    return jnp.concatenate(rows, axis=0).T


def place_sums(g_ref, at, sums):
    lane = lax.broadcasted_iota(jnp.int32, (F, 128), 1)
    table = jnp.zeros((F, 128), f32)
    for i, column in enumerate(sums):
        table = jnp.where(lane == i, column, table)
    place(g_ref, at, table.T[0:16, :])


class Refs:
    pass


KEPT = (
    ("n1", (F, ROWS), f32), ("i1", (1, ROWS), f32), ("a1", (F, ROWS), bf16), ("z", (3 * F, ROWS), bf16),
    ("o", (F, ROWS), bf16), ("m1", (F, ROWS), f32), ("n2", (F, ROWS), f32), ("i2", (1, ROWS), f32),
    ("a2", (F, ROWS), bf16), ("act", (FF, ROWS), bf16), ("slope", (FF, ROWS), bf16),
)
SHARED = (
    ("q", (F, ROWS), bf16), ("du", (FF, ROWS), bf16), ("t", (F, ROWS), f32), ("dz", (3 * F, ROWS), bf16),
)


PHASES = ((0, 3072, True, False), (3072, 2048, True, False), (5120, 1536, False, False), (6656, 2048, False, False), (8704, 1536, False, False))
PRED_AT = {"reduce": 0, "expand": 1536, "merge": 3072, "project": 3456, "embed": 4608, "small": 4992, "end": 5008}
ENC_AT = {"reduce": 5120, "expand": 6656, "merge": 8192, "gap": 8576, "project": 8704, "small": 9856, "end": 9872}
ORDERS = ("xyz", "yzx", "zxy")
WEIGHTS = (
    ("ew", (F, 3 * F)), ("em", (F, F)), ("ex", (F, FF)), ("er", (FF, F)), ("embed", (F, F)),
    ("pw", (F, 3 * F)), ("pm", (F, F)), ("px", (F, FF)), ("pr", (FF, F)),
)


class Where:
    def __init__(self):
        p, d = lax.axis_index("pipe"), lax.axis_index("dp")
        self.core, low = p % 2, p // 2
        self.at = {"x": d // 8, "y": d % 4, "z": ((d // 4) % 2) * 2 + low}
        self.side = low
        self.turn = {axis: [(self.at[axis] + k) % 4 for k in range(4)] for axis in "xyz"}
        self.near = {
            axis: [self.device(self.core, {**self.at, axis: self.turn[axis][k]}) for k in range(4)] for axis in "xyz"
        }
        self.twin = self.device(1 - self.core, self.at)
        z = self.at["z"]
        home = z + 1 - 2 * (z % 2)
        mate = home + self.core * (3 - z - home)
        self.out = self.device(self.core, {**self.at, "z": mate + self.side * (home - mate)})
        self.back = self.device(self.core, {**self.at, "z": home + self.side * (mate - home)})
        self.far = self.near["z"][2]

    def device(self, core, at):
        return {"pipe": (at["z"] % 2) * 2 + core, "dp": at["x"] * 8 + (at["z"] // 2) * 4 + at["y"]}

    def around(self, steps):
        return [self.near[axis][d] for axis in "xyz" for d in steps]


def send(src, dst, sems, i, device):
    copy = pltpu.make_async_remote_copy(
        src_ref=src, dst_ref=dst, send_sem=sems.at[0, i], recv_sem=sems.at[1, i],
        device_id=device, device_id_type=pl.DeviceIdType.MESH,
    )
    copy.start()
    return copy


def phase_buffers(size, relay, wide):
    quarter, small = size // 8, size // 32
    full = quarter if wide else small
    shapes = [("core", (3, size // 2, 128)), ("three", (3, 4, full, 128))]
    if relay:
        shapes += [("one", (3, 2, quarter // 2, 128)), ("two", (3, 2, quarter, 128))]
    else:
        shapes += [("one", (3, 3, quarter, 128))]
    shapes += [("wide", (3, 4, quarter, 128)) if wide else ("small", (3, 3, small, 128))]
    return shapes


def reduce_phase(me, g, phase, recv, sems, free):
    base, size, relay, wide = phase
    half, quarter, small = size // 2, size // 8, size // 32
    mine, others = base + me.core * half, base + (1 - me.core) * half
    step = [0]

    def go(src, dst, device):
        send(src, dst, sems, step[0], device)

    def wait(all_of_it):
        pltpu.make_async_remote_copy(
            src_ref=all_of_it, dst_ref=all_of_it, send_sem=sems.at[0, step[0]], recv_sem=sems.at[1, step[0]],
            device_id=me.twin, device_id_type=pl.DeviceIdType.MESH,
        ).wait()
        step[0] += 1

    def rows_of(c, start, count):
        return g.at[c, pl.ds(start, count), :]

    def release(i, devices):
        for device in devices:
            pl.semaphore_signal(free.at[i], inc=1, device_id=device, device_id_type=pl.DeviceIdType.MESH)

    def add(c, start, count, terms):
        own = pl.ds(start, count)
        value = g[c, own, :].astype(f32)
        for term in terms:
            value = value + term.astype(f32)
        g[c, own, :] = value.astype(bf16)

    def exchange(starts, rows, buf, turn, came):
        for c in range(3):
            if came[c]:
                add(c, starts[c], rows, [term[...] for term in came[c]])
            buf[c, me.at[ORDERS[c][turn]]] = g[c, pl.ds(starts[c], rows), :]
            for d in (2, 1, 3):
                block = buf.at[c, me.at[ORDERS[c][turn]]]
                go(block, block, me.near[ORDERS[c][turn]][d])

    def total_of(starts, rows, buf):
        for c in range(3):
            value = buf[c, 0].astype(f32)
            for j in range(1, 4):
                value = value + buf[c, j].astype(f32)
            g[c, pl.ds(starts[c], rows), :] = value.astype(bf16)

    go(g.at[:, pl.ds(others, half), :], recv.core, me.twin)
    yield
    wait(recv.core)
    axes = [order[0] for order in ORDERS]
    chunk = [[mine + me.turn[axes[c]][k] * quarter for k in range(4)] for c in range(3)]
    one = [chunk[c][0] for c in range(3)]
    if relay:
        part = quarter // 2
        for c in range(3):
            add(c, mine, half, [recv.core[c]])
            go(rows_of(c, chunk[c][2], part), recv.one.at[c, 0], me.near[axes[c]][1])
            go(rows_of(c, chunk[c][2] + part, part), recv.one.at[c, 1], me.near[axes[c]][3])
        release(0, [me.twin])
        yield
        wait(recv.one)
        for c in range(3):
            add(c, chunk[c][1], part, [recv.one[c, 0]])
            add(c, chunk[c][3] + part, part, [recv.one[c, 1]])
            go(rows_of(c, chunk[c][1], quarter), recv.two.at[c, 0], me.near[axes[c]][1])
            go(rows_of(c, chunk[c][3], quarter), recv.two.at[c, 1], me.near[axes[c]][3])
        yield
        wait(recv.two)
        came = [[recv.two.at[c, k] for k in range(2)] for c in range(3)]
    else:
        for c in range(3):
            add(c, mine, half, [recv.core[c]])
            for d in (2, 1, 3):
                go(rows_of(c, chunk[c][d], quarter), recv.one.at[c, d - 1], me.near[axes[c]][d])
        release(0, [me.twin])
        yield
        wait(recv.one)
        came = [[recv.one.at[c, k] for k in range(3)] for c in range(3)]

    if wide:
        exchange(one, quarter, recv.wide, 1, came)
        release(1, me.around((1, 2, 3)))
        yield
        wait(recv.wide.at[:, 0:3])
        total_of(one, quarter, recv.wide)
        exchange(one, quarter, recv.three, 2, [[]] * 3)
        yield
        wait(recv.three.at[:, 0:3])
        total_of(one, quarter, recv.three)
    else:
        axes2 = [order[1] for order in ORDERS]
        two = [one[c] + me.at[axes2[c]] * small for c in range(3)]
        for c in range(3):
            add(c, one[c], quarter, [term[...] for term in came[c]])
            for d in (2, 1, 3):
                block = rows_of(c, one[c] + me.turn[axes2[c]][d] * small, small)
                go(block, recv.small.at[c, d - 1], me.near[axes2[c]][d])
        yield
        wait(recv.small)
        exchange(two, small, recv.three, 2, [[recv.small.at[c, d] for d in range(3)] for c in range(3)])
        release(1, me.around((1, 2, 3)))
        yield
        wait(recv.three.at[:, 0:3])
        total_of(two, small, recv.three)
        pl.semaphore_wait(free.at[1], 9)
        for d in (2, 1, 3):
            for c in range(3):
                block = rows_of(c, two[c], small)
                go(block, block, me.near[axes2[c]][d])
        yield
        wait(recv.small)

    if wide:
        pl.semaphore_wait(free.at[1], 9)
    for d in (1, 3) if relay else (2, 1, 3):
        for c in range(3):
            block = rows_of(c, one[c], quarter)
            go(block, block, me.near[axes[c]][d])
    yield
    wait(recv.two if relay else recv.one)
    if relay:
        for c in range(3):
            block = rows_of(c, chunk[c][3], part)
            go(block, block, me.near[axes[c]][1])
            block = rows_of(c, chunk[c][1] + part, part)
            go(block, block, me.near[axes[c]][3])
        yield
        wait(recv.one)
    pl.semaphore_wait(free.at[0], 1)
    block = g.at[:, pl.ds(mine, half), :]
    go(block, block, me.twin)
    yield
    wait(recv.core)


def slot_kernel(names, *refs):
    r = Refs()
    for name, ref in zip(names, refs):
        setattr(r, name, ref)
    me = Where()
    first = me.side == 0
    loads = {}
    for i, (name, _) in enumerate(WEIGHTS):
        loads[name] = pltpu.make_async_copy(getattr(r, "h_" + name), getattr(r, name), r.loads.at[i])
        loads[name].start()
    barrier = pltpu.get_barrier_semaphore()
    friends = [me.twin] + me.around((1, 2, 3))
    for device in friends:
        pl.semaphore_signal(barrier, inc=1, device_id=device, device_id_type=pl.DeviceIdType.MESH)
    lane = lax.broadcasted_iota(jnp.int32, (8, 128), 1)
    counts = jnp.zeros((8, 128), jnp.int32)
    for c in range(CLIPS):
        counts = jnp.where(lane == c, r.frames[0, 1, me.core, c], counts)
    r.counts[...] = counts
    pl.semaphore_wait(barrier, len(friends))
    told = send(r.counts, r.far_counts, r.swaps, 4, me.far)
    swap = send(r.local.at[1 - me.side], r.arrived, r.swaps, 0, me.out)
    away = me.side * me.core == 1
    lookup = pltpu.make_async_copy(r.far_counts, r.scalars, r.loads.at[len(WEIGHTS)])

    @pl.when(away)
    def _():
        told.wait_recv()
        lookup.start()
        lookup.wait()

    @pl.when(jnp.logical_not(away))
    def _():
        for c in range(CLIPS):
            r.scalars[0, c] = r.frames[0, me.side, me.core, c]

    source, label, live = unit_order([r.scalars[0, c] for c in range(CLIPS)])
    fill_mask(r.mask, label)
    fill_order(r.order, source)
    enc, pred = Refs(), Refs()
    enc.vec = columns(r.eg[...], r.eb[...], r.exb[...])
    pred.vec = columns(r.pg[...], r.pb[...], r.pxb[...])
    enc.project, enc.merge, enc.expand, enc.reduce = r.ew, r.em, r.ex, r.er
    pred.project, pred.merge, pred.expand, pred.reduce = r.pw, r.pm, r.px, r.pr
    es, ps = Refs(), Refs()
    for name, _, _ in KEPT:
        setattr(es, name, getattr(r, "e_" + name))
        setattr(ps, name, getattr(r, "p_" + name))
    for name, _, _ in SHARED:
        setattr(es, name, getattr(r, name))
        setattr(ps, name, getattr(r, name))
    es.e, es.over, ps.e, ps.over = r.e_e, r.e_over, r.p_e, r.p_over


    @pl.when(jnp.logical_not(first))
    def _():
        swap.wait_recv()

    far_rows = pltpu.make_async_remote_copy(
        src_ref=r.local.at[1], dst_ref=r.cotangent, send_sem=r.swaps.at[0, 2], recv_sem=r.swaps.at[1, 2],
        device_id=me.far, device_id_type=pl.DeviceIdType.MESH,
    )

    @pl.when(away)
    def _():
        far_rows.start()

    @pl.when(first)
    def _():
        r.x[...] = r.local[0]

    @pl.when(jnp.logical_not(first))
    def _():
        r.x[...] = r.arrived[...]

    r.stream[...] = dot(r.x[...], r.order[...], 0, 0)
    for copy in loads.values():
        copy.wait()

    block_forward(r.stream, r.stream2, enc, es, HEADS, r.mask)
    r.sent[...] = r.stream2[...].astype(bf16)
    r.stream[...] = dot(r.embed[...], r.sent[...], 0, 0) + r.embed_bias[...].astype(f32).reshape(1, F).T
    block_forward(r.stream, r.stream2, pred, ps, PHEADS, r.mask)

    alive = lax.broadcasted_iota(jnp.int32, (F, ROWS), 1) < live
    r.out[...] = dot(r.order[...], jnp.where(alive, r.stream2[...], 0.0).astype(bf16), 1, 1).astype(bf16)
    copy_out = pltpu.make_async_remote_copy(
        src_ref=r.sends, dst_ref=r.back, send_sem=r.swaps.at[0, 1], recv_sem=r.swaps.at[1, 1],
        device_id=me.back, device_id_type=pl.DeviceIdType.MESH,
    )
    far_out = pltpu.make_async_remote_copy(
        src_ref=r.out, dst_ref=r.kept, send_sem=r.swaps.at[0, 3], recv_sem=r.swaps.at[1, 3],
        device_id=me.far, device_id_type=pl.DeviceIdType.MESH,
    )

    @pl.when(first)
    def _():
        r.sends[...] = r.out[...]
        copy_out.start()
        swap.wait_recv()
        r.cotangent[...] = r.arrived[...]

    @pl.when(away)
    def _():
        far_out.start()
        far_rows.wait()

    @pl.when(me.side * (1 - me.core) == 1)
    def _():
        r.cotangent[...] = r.local[1]
        r.kept[...] = r.out[...]

    swap.wait_send()
    told.wait_send()

    @pl.when(jnp.logical_not(away))
    def _():
        told.wait_recv()

    cotangent = r.cotangent[...]
    r.stream[...] = jnp.where(alive, dot(cotangent, r.order[...], 0, 0), 0.0)

    g = r.grads
    phases = []
    for i, phase in enumerate(PHASES):
        recv = Refs()
        for name, _ in phase_buffers(*phase[1:]):
            setattr(recv, name, getattr(r, f"{name}{i}"))
        phases.append(reduce_phase(me, g, phase, recv, r.sems.at[i], r.free.at[i]))

    ticks = iter(PLAN)

    def tick():
        for i in next(ticks):
            next(phases[i], None)

    sums, _ = block_backward(r.stream, pred, ps, PHEADS, g, PRED_AT, tick, False)
    r.q[...] = r.stream[...].astype(bf16)
    de = r.q[...]
    place(g, PRED_AT["embed"], dot(r.sent[...], de, 1, 1))
    place_sums(g, PRED_AT["small"], sums + [total(de)])
    g[:, PRED_AT["end"] : ENC_AT["reduce"], :] = jnp.zeros((3, ENC_AT["reduce"] - PRED_AT["end"], 128), bf16)
    g[:, ENC_AT["gap"] : ENC_AT["project"], :] = jnp.zeros((3, ENC_AT["project"] - ENC_AT["gap"], 128), bf16)
    g[:, ENC_AT["end"] : TOTAL, :] = jnp.zeros((3, TOTAL - ENC_AT["end"], 128), bf16)
    r.stream[...] = dot(r.embed[...], de, 1, 0).astype(bf16).astype(f32)
    tick()
    sums, last = block_backward(r.stream, enc, es, HEADS, g, ENC_AT, tick, True)
    place_sums(g, ENC_AT["small"], sums)
    tick()
    for n, i in enumerate(TAIL):
        if n == 3:
            for t in range(ROWS // 128):
                last(t)
            dx = dot(r.order[...], r.stream[...].astype(bf16), 1, 1).astype(bf16)

            @pl.when(first)
            def _():
                r.kept[...] = dx

            @pl.when(jnp.logical_not(first))
            def _():
                r.sends[...] = dx

        if i is None:

            @pl.when(jnp.logical_not(first))
            def _():
                copy_out.start()

        else:
            next(phases[i], None)
    copy_out.wait()

    @pl.when(away)
    def _():
        far_out.wait()


PLAN = (
    (), (), (), (), (0,), (), (), (), (), (), (), (), (0,), (1,), (), (), (), (1, 0, 2,), (), (1, 2, 3,), (0,), (), (), (3, 1,), (4,),
)
TAIL = (2, 0, 4, 3, 1, 2, 0, 4, 3, 1, 2, 0, 4, 3, 1, 2, 0, 4, 3, 1, 2, 0, 4, None, 2, 3, 1, 0, 4, 3, 1, 4)


def slot_call(frames, local, weights):
    args = [("frames", frames), ("local", local)]
    big = {name for name, _ in WEIGHTS}
    order = ("eg", "eb", "ew", "em", "ex", "exb", "er", "embed", "embed_bias", "pg", "pb", "pw", "pm", "px", "pxb", "pr")
    specs = [pl.BlockSpec(memory_space=pltpu.SMEM), pl.BlockSpec(memory_space=pltpu.VMEM)]
    for name, weight in zip(order, weights):
        args.append(("h_" + name if name in big else name, weight))
        specs.append(pl.BlockSpec(memory_space=pl.ANY if name in big else pltpu.VMEM))
    outs = [("grads", (3, TOTAL, 128), bf16), ("kept", (ROWS, F), bf16), ("back", (ROWS, F), bf16)]
    scratch = [
        ("mask", (BLOCKS, BLOCK, BLOCK), f32), ("order", (ROWS, ROWS), bf16), ("out", (ROWS, F), bf16),
        ("stream", (F, ROWS), f32), ("stream2", (F, ROWS), f32), ("sent", (F, ROWS), bf16),
        ("arrived", (ROWS, F), bf16), ("cotangent", (ROWS, F), bf16), ("x", (ROWS, F), bf16),
        ("counts", (8, 128), jnp.int32), ("far_counts", (8, 128), jnp.int32), ("sends", (ROWS, F), bf16),
        ("e_e", (HEADS, BLOCKS, BLOCK, BLOCK), bf16), ("p_e", (PHEADS, BLOCKS, BLOCK, BLOCK), bf16),
        ("e_over", (8, ROWS), f32), ("p_over", (16, ROWS), f32),
    ]
    scratch += [(n, sh, bf16) for n, sh in WEIGHTS]
    scratch += [("e_" + n, sh, d) for n, sh, d in KEPT] + [("p_" + n, sh, d) for n, sh, d in KEPT]
    scratch += list(SHARED)
    for i, phase in enumerate(PHASES):
        scratch += [(f"{name}{i}", shape, bf16) for name, shape in phase_buffers(*phase[1:])]
    sems = [("loads", (len(WEIGHTS) + 1,)), ("swaps", (2, 5)), ("sems", (len(PHASES), 2, 9))]
    names = [n for n, _ in args] + [n for n, _, _ in outs] + [n for n, _, _ in scratch] + [n for n, _ in sems] + ["free", "scalars"]
    return pl.pallas_call(
        functools.partial(slot_kernel, names),
        out_shape=[pltpu.VMEM(sh, d) for _, sh, d in outs],
        in_specs=specs,
        out_specs=[pl.BlockSpec(memory_space=pltpu.VMEM)] * len(outs),
        scratch_shapes=[pltpu.VMEM(sh, d) for _, sh, d in scratch] + [pltpu.SemaphoreType.DMA(sh) for _, sh in sems]
        + [pltpu.SemaphoreType.REGULAR((len(PHASES), 2)), pltpu.SMEM((8, 128), jnp.int32)],
        compiler_params=pltpu.CompilerParams(
            vmem_limit_bytes=52 * 2**20, collective_id=0, has_side_effects=True
        ),
    )(*[a for _, a in args])


LAYERS = (("pg", "pb", "pw", "pm", "px", "pxb", "pr"), ("eg", "eb", "ew", "em", "ex", "exb", "er"))
BIG = {"w": (F, 3 * F), "m": (F, F), "x": (F, FF), "r": (FF, F)}


def widen(g_ref, at, out_ref, rows, col):
    for c in range(3):
        out_ref[rows, col + c * 128 : col + c * 128 + 128] = g_ref[c, at : at + F, :].astype(f32)


def unpack_kernel(names, *refs):
    r = Refs()
    for name, ref in zip(names, refs):
        setattr(r, name, ref)
    copies = []

    def ship(src, dst):
        copy = pltpu.make_async_copy(src, dst, r.sems.at[len(copies)])
        copy.start()
        copies.append(copy)

    side = lax.axis_index("pipe") // 2
    r.wide[0] = r.kept[...].astype(f32)
    ship(r.wide.at[0], r.result.at[side])
    r.wide[1] = r.back[...].astype(f32)
    ship(r.wide.at[1], r.result.at[1 - side])
    g = r.grads
    for layer, at in (("p", PRED_AT), ("e", ENC_AT)):
        for part in range(4):
            rows = slice(part * F, part * F + F)
            widen(g, at["reduce"] + part * F, getattr(r, "s_" + layer + "r"), rows, 0)
        ship(getattr(r, "s_" + layer + "r"), getattr(r, layer + "r"))
        for part in range(4):
            widen(g, at["expand"] + part * F, getattr(r, "s_" + layer + "x"), slice(0, F), part * F)
        ship(getattr(r, "s_" + layer + "x"), getattr(r, layer + "x"))
        for part in range(3):
            widen(g, at["project"] + part * F, getattr(r, "s_" + layer + "w"), slice(0, F), part * F)
        ship(getattr(r, "s_" + layer + "w"), getattr(r, layer + "w"))
        widen(g, at["merge"], getattr(r, "s_" + layer + "m"), slice(0, F), 0)
        ship(getattr(r, "s_" + layer + "m"), getattr(r, layer + "m"))
        if layer == "p":
            widen(g, at["embed"], r.s_embed, slice(0, F), 0)
            ship(r.s_embed, r.embed)
        small = at["small"]
        rows = jnp.concatenate([g[c, small : small + 16, :] for c in range(3)], axis=1).astype(f32)
        getattr(r, layer + "g")[...] = rows[0:2]
        getattr(r, layer + "b")[...] = rows[2:8]
        for part in range(4):
            getattr(r, layer + "xb")[part * F : part * F + F] = rows[8 + part]
        if layer == "p":
            r.embed_bias[...] = rows[12]
    for copy in copies:
        copy.wait()


def unpack_call(grads, kept, back):
    big = [("embed", (F, F))] + [(layer + n, BIG[n]) for layer in "pe" for n in BIG]
    small = [("embed_bias", (F,))]
    for layer in "pe":
        small += [(layer + "g", (2, F)), (layer + "b", (6, F)), (layer + "xb", (FF,))]
    outs = [("result", (2, ROWS, F))] + big + small
    names = ["grads", "kept", "back"] + [n for n, _ in outs] + ["s_" + n for n, _ in big] + ["wide", "sems"]
    values = pl.pallas_call(
        functools.partial(unpack_kernel, names),
        out_shape=[jax.ShapeDtypeStruct(sh, f32) for _, sh in outs],
        in_specs=[pl.BlockSpec(memory_space=pltpu.VMEM)] * 3,
        out_specs=[pl.BlockSpec(memory_space=pl.ANY)] * (1 + len(big))
        + [pl.BlockSpec(memory_space=pltpu.VMEM)] * len(small),
        scratch_shapes=[pltpu.VMEM(sh, f32) for _, sh in big]
        + [pltpu.VMEM((2, ROWS, F), f32), pltpu.SemaphoreType.DMA((len(big) + 2,))],
        compiler_params=pltpu.CompilerParams(vmem_limit_bytes=24 * 2**20),
    )(*[pltpu.with_memory_space_constraint(v, pltpu.VMEM) for v in (grads, kept, back)])
    return dict(zip([n for n, _ in outs], values))


def body(segment_data, clip_frames, *weights):
    g = unpack_call(*slot_call(clip_frames, segment_data[0, 0], weights))
    order = ("eg", "eb", "ew", "em", "ex", "exb", "er", "embed", "embed_bias", "pg", "pb", "pw", "pm", "px", "pxb", "pr")
    return (g["result"][None, None],) + tuple(g[n] for n in order)


def solution(mesh):
    return jax.shard_map(
        body,
        mesh=mesh,
        in_specs=(P("pipe", "dp", None, None, None), P("dp", None, None, None)) + (P(),) * 16,
        out_specs=(P("pipe", "dp", None, None, None),) + (P(),) * 16,
        check_vma=False,
    )
```
